256 devices in a mesh: flow: 4 (over y_lo, core), gy: 8 (over x, y_hi), gz: 8 (over z).
Axes of the slice: x: 4, y: 4 (y_hi: 2, y_lo: 2; y = y_hi * 2 + y_lo), z: 8, core: 2. Of those that a mesh axis runs over, the one named last changes fastest.
Arguments:
- momentum_sets: float32 [19, 16, 128, 1024], P(None, 'flow', 'gy', 'gz'), may hold values from 0 to 1, as said below
- labels: int32 [16, 128, 1024], P('flow', 'gy', 'gz'), may hold values 0 or 1
- solid_mask: int32 [16, 128, 1024], P('flow', 'gy', 'gz'), may hold values 0 or 1
Outputs:
- momentum_out: float32 [19, 16, 128, 1024], P(None, 'flow', 'gy', 'gz')
- red_out: float32 [7, 16, 128, 1024], P(None, 'flow', 'gy', 'gz')
- blue_out: float32 [7, 16, 128, 1024], P(None, 'flow', 'gy', 'gz')
The draws below stay inside these ranges and needn't reach their ends.
Inputs may be any that keep to these rules, and one draw needn't show every extreme that they name: `momentum_sets`: every entry is positive.
All inputs are finite; a program needn't handle non-finite values. No bound on the sum of `labels` or of `solid_mask` on one device may be relied on, other than what follows from the above.
Results may differ from the reference program's by a relative error of at most 0.0003.
Values sent between devices are 32-bit elements; how exact they have to be, the bound alone decides.
A program may use at most 64 MiB of HBM per device.

```python
import math
import jax
import jax.numpy as jnp

STEPS = 3
NX = 16
NY = 128
NZ = 1024


lattice_weights = (1.0 / 3.0,) + (1.0 / 18.0,) * 6 + (1.0 / 36.0,) * 12


def draw_momentum_sets(key, part):
    key = jax.random.fold_in(key, 11)
    first_key, second_key = jax.random.split(key)
    extent = (NX, NY, NZ)
    density = jnp.exp(jax.random.uniform(first_key, extent, jnp.float32, math.log(0.7), math.log(1.4)))
    noise = jax.random.uniform(second_key, (19,) + extent, jnp.float32, -0.1, 0.1)
    weights = jnp.array(lattice_weights, jnp.float32).reshape(19, 1, 1, 1)
    return weights * density[None] * (1.0 + noise)


def touch_ends(values, rng, low, high):
    longest = values.shape.index(max(values.shape))
    spots = []
    for shift in (0, 1):
        where = [jax.random.randint(jax.random.fold_in(rng, axis), (), 0, length) for axis, length in enumerate(values.shape)]
        where[longest] = (where[longest] + shift) % values.shape[longest]
        spots.append(tuple(where))
    return values.at[spots[0]].set(low).at[spots[1]].set(high)


def setup_inputs(seed: int = 0) -> dict:
    key_list = jax.random.split(jax.random.key(seed), 4)
    momentum_sets = draw_momentum_sets(jax.random.fold_in(key_list[3], 71), 0)
    labels = touch_ends((jax.random.randint(key_list[1], (NX, NY, NZ), 0, 2) < 1).astype(jnp.int32), jax.random.fold_in(key_list[1], 1), 0, 1)
    solid_mask = touch_ends((jax.random.randint(key_list[2], (NX, NY, NZ), 0, 4) < 1).astype(jnp.int32), jax.random.fold_in(key_list[2], 1), 0, 1)
    return {"momentum_sets": momentum_sets, "labels": labels, "solid_mask": solid_mask}


velocity_full = ((0, 0, 0), (1, 0, 0), (-1, 0, 0), (0, 1, 0), (0, -1, 0), (0, 0, 1), (0, 0, -1), (1, 1, 0), (-1, -1, 0), (1, -1, 0), (-1, 1, 0), (1, 0, 1), (-1, 0, -1), (1, 0, -1), (-1, 0, 1), (0, 1, 1), (0, -1, -1), (0, 1, -1), (0, -1, 1))
weight_full = (1.0 / 3.0,) + (1.0 / 18.0,) * 6 + (1.0 / 36.0,) * 12
opposite_full = (0, 2, 1, 4, 3, 6, 5, 8, 7, 10, 9, 12, 11, 14, 13, 16, 15, 18, 17)
weight_phase = (0.25,) + (0.125,) * 6
wetting = 0.3
surface_tension_coefficient = 0.05
recolouring_coefficient = 0.5
gradient_floor = 0.1
body_force = 0.001
relax_red = 1.0
relax_blue = 1.6

def project(offset, vector):
    total = 0.0
    for axis_number in range(3):
        if offset[axis_number] != 0:
            total = total + offset[axis_number] * vector[axis_number]
    return total

def gradient_of(phase_at):
    grads = [0.0, 0.0, 0.0]
    for direction in range(1, 19):
        offset = velocity_full[direction]
        nearby = phase_at(offset)
        for axis_number in range(3):
            if offset[axis_number] != 0:
                grads[axis_number] = grads[axis_number] + 3.0 * weight_full[direction] * offset[axis_number] * nearby
    return grads

def relax(moments, reds, blues, phase, gradient):
    density = sum(moments)
    flux = []
    for axis_number in range(3):
        total = 0.0
        for entry in range(19):
            if velocity_full[entry][axis_number] != 0:
                total = total + velocity_full[entry][axis_number] * moments[entry]
        flux.append(total)
    velocity = [flux[axis_number] / density for axis_number in range(3)]
    relax_time = 0.5 * (1.0 + phase) * relax_red + 0.5 * (1.0 - phase) * relax_blue
    shifted_values = [velocity[0] + relax_time * body_force / density, velocity[1], velocity[2]]
    square = shifted_values[0] * shifted_values[0] + shifted_values[1] * shifted_values[1] + shifted_values[2] * shifted_values[2]
    gradient_squared = gradient[0] * gradient[0] + gradient[1] * gradient[1] + gradient[2] * gradient[2]
    post_moments = []
    for direction in range(19):
        offset = velocity_full[direction]
        weight = weight_full[direction]
        along = project(offset, shifted_values)
        equil = weight * density * (1.0 + 3.0 * along + 4.5 * along * along - 1.5 * square)
        slope = project(offset, gradient)
        length_sq = abs(offset[0]) + abs(offset[1]) + abs(offset[2])
        surface = surface_tension_coefficient * weight * (slope * slope - length_sq * gradient_squared / 3.0)
        post_moments.append(moments[direction] - (moments[direction] - equil) / relax_time + surface)
    red_fluid_density = sum(reds)
    blue_fluid_density = sum(blues)
    colour_field = red_fluid_density + blue_fluid_density
    scale = jnp.maximum(jnp.sqrt(gradient_squared), gradient_floor)
    normal = [gradient[axis_number] / scale for axis_number in range(3)]
    mixing_fraction = recolouring_coefficient * red_fluid_density * blue_fluid_density / colour_field
    post_reds = []
    post_blues = []
    for direction in range(7):
        offset = velocity_full[direction]
        along = project(offset, velocity)
        across = project(offset, normal)
        post_reds.append(weight_phase[direction] * (red_fluid_density * (1.0 + 4.0 * along) + mixing_fraction * across))
        post_blues.append(weight_phase[direction] * (blue_fluid_density * (1.0 + 4.0 * along) - mixing_fraction * across))
    return (post_moments, post_reds, post_blues)

def take_from(field, offset):
    moved = jnp.roll(field, offset[0], axis=0)
    padded = jnp.pad(moved, ((0, 0), (1, 1), (1, 1)))
    return padded[:, 1 - offset[1]:1 - offset[1] + field.shape[1], 1 - offset[2]:1 - offset[2] + field.shape[2]]

def stream_set(posts, olds, opposite, fluid):
    result = []
    for direction in range(len(posts)):
        offset = velocity_full[direction]
        source = take_from(posts[direction], offset)
        opened = take_from(fluid, offset)
        arrived = jnp.where(opened > 0, source, posts[opposite[direction]])
        result.append(jnp.where(fluid > 0, arrived, olds[direction]))
    return result

def reference(momentum_sets, labels, solid_mask):
    fluid = (1 - solid_mask).astype(jnp.float32)
    moments = [momentum_sets[entry] for entry in range(19)]
    density = sum(moments)
    red_fluid_density = density * (0.05 + 0.9 * labels.astype(jnp.float32))
    blue_fluid_density = density - red_fluid_density
    reds = [weight_phase[entry] * red_fluid_density for entry in range(7)]
    blues = [weight_phase[entry] * blue_fluid_density for entry in range(7)]
    for iteration in range(STEPS):
        red_sum = sum(reds)
        blue_sum = sum(blues)
        phase = jnp.where(fluid > 0, (red_sum - blue_sum) / (red_sum + blue_sum), wetting)
        shifted_phase = phase - wetting
        gradient = gradient_of(lambda offset: take_from(shifted_phase, (-offset[0], -offset[1], -offset[2])) + wetting)
        post_moments, post_reds, post_blues = relax(moments, reds, blues, phase, gradient)
        moments = stream_set(post_moments, moments, opposite_full, fluid)
        reds = stream_set(post_reds, reds, opposite_full[:7], fluid)
        blues = stream_set(post_blues, blues, opposite_full[:7], fluid)
    momentum_out = jnp.where(fluid > 0, jnp.stack(moments), 0.0)
    red_out = jnp.where(fluid > 0, jnp.stack(reds), 0.0)
    blue_out = jnp.where(fluid > 0, jnp.stack(blues), 0.0)
    return (momentum_out, red_out, blue_out)
```

```python
import functools

import jax
import jax.numpy as jnp
from jax import lax
from jax.experimental import pallas as pl
from jax.experimental.pallas import tpu as pltpu
from jax.sharding import PartitionSpec as P

STEPS = 3
NX, NY, NZ = 4, 16, 128
LO, HI = 8, 8 + NY
ROWS = 32
WETTING = 0.3
TENSION = 0.05
MESH = pl.DeviceIdType.MESH
VMEM_LIMIT = 60 * 1024 * 1024

VELOCITY = (
    (0, 0, 0),
    (1, 0, 0),
    (-1, 0, 0),
    (0, 1, 0),
    (0, -1, 0),
    (0, 0, 1),
    (0, 0, -1),
    (1, 1, 0),
    (-1, -1, 0),
    (1, -1, 0),
    (-1, 1, 0),
    (1, 0, 1),
    (-1, 0, -1),
    (1, 0, -1),
    (-1, 0, 1),
    (0, 1, 1),
    (0, -1, -1),
    (0, 1, -1),
    (0, -1, 1),
)
OPPOSITE = (0, 2, 1, 4, 3, 6, 5, 8, 7, 10, 9, 12, 11, 14, 13, 16, 15, 18, 17)
PAIRS = ((1, 2), (3, 4), (5, 6), (7, 8), (9, 10), (11, 12), (13, 14), (15, 16), (17, 18))

X_UP = [("f", i) for i in (1, 7, 9, 11, 13)] + [("r", 1), ("b", 1)]
X_DOWN = [("f", i) for i in (2, 8, 10, 12, 14)] + [("r", 2), ("b", 2)]
EVERY = [("f", i) for i in range(19)] + [("r", i) for i in range(7)] + [("b", i) for i in range(7)]
ORDER = X_UP + X_DOWN + [name for name in EVERY if name not in X_UP + X_DOWN]
SLOT = {name: place for place, name in enumerate(ORDER)}
Y_FACE = {
    1: (("f", 3), ("r", 3), ("f", 7), ("f", 10), ("f", 15), ("f", 17), ("b", 3)),
    -1: (("f", 4), ("r", 4), ("f", 9), ("f", 8), ("f", 18), ("f", 16), ("b", 4)),
}
Z_FACE = {
    1: (("f", 5), ("f", 11), ("f", 14), ("f", 15), ("f", 18), ("r", 5), ("b", 5)),
    -1: (("f", 6), ("f", 13), ("f", 12), ("f", 17), ("f", 16), ("r", 6), ("b", 6)),
}
Z_MOVING = Z_FACE[1] + Z_FACE[-1]
UNROLLED = {name: place for place, name in enumerate(Z_MOVING)}
DIRECTIONS = VELOCITY[1:]
WAY = {offset: place for place, offset in enumerate(DIRECTIONS)}
SIDE = {1: 0, -1: 1}
YZ_WAY = {(1, 1): 0, (1, -1): 1, (-1, 1): 2, (-1, -1): 3}
OTHERS = sorted(DIRECTIONS[2:], key=lambda offset: (abs(offset[2]), abs(offset[0])))


def kernel(
    momentum_in,
    labels_in,
    solid_in,
    every_out,
    state,
    labels,
    solid,
    scalars,
    scalars_down,
    scalars_up,
    posts,
    unrolled,
    speed,
    colour,
    phase_y,
    phase_z,
    phase_yz,
    phase_y_got,
    phase_edge_got,
    phase_z_got,
    post_y,
    post_z,
    post_yz,
    post_y_got,
    post_edge_got,
    post_z_got,
    in_sem,
    out_sem,
    send_sem,
    recv_sem,
    *,
    sizes,
):
    here = tuple(lax.axis_index(axis) for axis in ("flow", "gy", "gz"))

    def neighbour(offset):
        return tuple(
            here[axis] if offset[axis] == 0 else lax.rem(here[axis] + offset[axis] + sizes[axis], sizes[axis])
            for axis in range(3)
        )

    closed = {
        (1, -1): here[1] == 0,
        (1, 1): here[1] == sizes[1] - 1,
        (2, -1): here[2] == 0,
        (2, 1): here[2] == sizes[2] - 1,
    }
    lane = lax.broadcasted_iota(jnp.int32, (8, NZ), 1)
    row_lane = lax.broadcasted_iota(jnp.int32, (1, NZ), 1)

    loads = [
        pltpu.make_async_copy(solid_in, solid, in_sem.at[0]),
        pltpu.make_async_copy(labels_in, labels, in_sem.at[1]),
        pltpu.make_async_copy(momentum_in, state.at[pl.ds(0, 19)], in_sem.at[2]),
    ]
    for load in loads:
        load.start()

    barrier = pltpu.get_barrier_semaphore()
    for offset in DIRECTIONS:
        pl.semaphore_signal(barrier, inc=1, device_id=neighbour(offset), device_id_type=MESH)

    def remote(source, target, turn, offset):
        way = WAY[offset]
        return pltpu.make_async_remote_copy(
            src_ref=source,
            dst_ref=target,
            send_sem=send_sem.at[turn, way],
            recv_sem=recv_sem.at[turn, way],
            device_id=neighbour(offset),
            device_id_type=MESH,
        )

    def phase_copies(step):
        first, count = (0, 2) if step == 0 else (step + 1, 1)
        copies = []
        for offset in DIRECTIONS:
            dx, dy, dz = offset
            way = WAY[offset]
            if dx != 0 and dy != 0:
                source = phase_y.at[step, SIDE[dy], pl.ds((NX - 1) * count if dx == 1 else 0, count)]
                target = phase_edge_got.at[step, way, pl.ds(0, count)]
            elif dy != 0 and dz != 0:
                source = phase_yz.at[step, YZ_WAY[(dy, dz)]]
                target = phase_edge_got.at[step, way, pl.ds(0, 1)]
            elif dy != 0:
                source = phase_y.at[step, SIDE[dy], pl.ds(0, NX * count)]
                target = phase_y_got.at[step, SIDE[dy], pl.ds(0, NX * count)]
            elif dz != 0:
                source = phase_z.at[step, SIDE[dz]]
                target = phase_z_got.at[step, way]
            else:
                near, far = (NX, 0) if offset[0] == 1 else (1, NX + 1)
                copies.append(
                    remote(
                        scalars.at[pl.ds(first, count), near, pl.ds(LO, NY)],
                        scalars.at[pl.ds(first, count), far, pl.ds(LO, NY)],
                        2 * step,
                        offset,
                    )
                )
                continue
            copies.append(remote(source, target, 2 * step, offset))
        return dict(zip(DIRECTIONS, copies))

    def post_x_copies(step):
        copies = {}
        for sign, first, near, far in ((1, 0, NX, 0), (-1, 7, 1, NX + 1)):
            copies[(sign, 0, 0)] = remote(
                posts.at[step, pl.ds(first, 7), near, pl.ds(LO, NY)],
                posts.at[step, pl.ds(first, 7), far, pl.ds(LO, NY)],
                2 * step + 1,
                (sign, 0, 0),
            )
        return copies

    def post_other_copies(step):
        copies = {}
        for offset in OTHERS:
            dx, dy, dz = offset
            way = WAY[offset]
            if dy != 0 and dx == 0 and dz == 0:
                source, target = post_y.at[step, SIDE[dy]], post_y_got.at[step, SIDE[dy]]
            elif dx != 0 and dy != 0:
                line = Y_FACE[dy].index(("f", VELOCITY.index(offset))) * 4 + (NX - 1 if dx == 1 else 0)
                source, target = post_y.at[step, SIDE[dy], line], post_edge_got.at[step, way]
            elif dy != 0:
                source, target = post_yz.at[step, YZ_WAY[(dy, dz)]], post_edge_got.at[step, way]
            else:
                source, target = post_z.at[step, SIDE[dz]], post_z_got.at[step, way]
            copies[offset] = remote(source, target, 2 * step + 1, offset)
        return copies

    def pack_z(tile, place, sign, packed):
        moved = pltpu.roll(tile, place + 1 if sign == 1 else place, axis=1)
        return jnp.where(lane == place, moved, packed)

    def unpack_z(packed, place, sign):
        return pltpu.roll(packed, (128 - place) % 128 if sign == 1 else 127 - place, axis=1)

    def edge_lane(sign):
        return 0 if sign == 1 else NZ - 1

    def set_phase(step, x, values, packed):
        first, count = (0, 2) if step == 0 else (step + 1, 1)
        up, down = packed
        for entry, value in enumerate(values):
            scalars[first + entry, x + 1, LO:HI, :] = value
            for dy, edge in ((1, HI - 1), (-1, LO)):
                phase_y[step, SIDE[dy], x * count + entry] = scalars[first + entry, x + 1, edge : edge + 1, :]
            for half in range(2):
                tile = value[8 * half : 8 * half + 8]
                place = entry * 8 + 2 * x + half
                up = pack_z(tile, place, 1, up)
                down = pack_z(tile, place, -1, down)
        return up, down

    def send_phase(step, packed):
        for dz in (1, -1):
            phase_z[step, SIDE[dz]] = packed[SIDE[dz]]
            for dy, edge in ((1, 7), (-1, 0)):
                phase_yz[step, YZ_WAY[(dy, dz)], 0] = phase_z[step, SIDE[dz], edge : edge + 1, :]
        copies = phase_copies(step)
        for copy in copies.values():
            copy.start()
        return copies

    def unpack_phase(step, copies):
        first, count = (0, 2) if step == 0 else (step + 1, 1)
        fills = (0.0, WETTING) if step == 0 else (WETTING,)
        shifted = {1: scalars_down, -1: scalars_up}

        def cover(offset, value, fill):
            for axis in (1, 2):
                if offset[axis] != 0:
                    value = jnp.where(closed[(axis, -offset[axis])], fill, value)
            return value

        def arrive(*offsets):
            for offset in offsets:
                copies[offset].wait_recv()

        def shift_plane(entry, plane, dz, face, column):
            for half in range(2):
                rows = slice(LO + 8 * half, LO + 8 * half + 8)
                value = scalars[first + entry, plane, rows, :]
                place = entry * 8 + 2 * column + half
                ghost = cover((0, 0, dz), unpack_z(face, place, dz), fills[entry])
                shifted[dz][min(first + entry, 1), plane, rows, :] = jnp.where(
                    lane == edge_lane(dz), ghost, pltpu.roll(value, 1 if dz == 1 else 127, axis=1)
                )

        for copy in copies.values():
            copy.wait_send()
        for dz in (1, -1):
            arrive((0, 0, dz))
            face = phase_z_got[step, WAY[(0, 0, dz)]]
            for entry in range(count):
                for x in range(NX):
                    shift_plane(entry, x + 1, dz, face, x)
        for dy, ghost in ((1, LO - 1), (-1, HI)):
            half = 1 if dy == 1 else 0
            arrive((0, dy, 0), (0, dy, 1), (0, dy, -1))
            for entry in range(count):
                for x in range(NX):
                    line = cover((0, dy, 0), phase_y_got[step, SIDE[dy], x * count + entry], fills[entry])
                    scalars[first + entry, x + 1, ghost : ghost + 1, :] = line
                    for dz in (1, -1):
                        corner = phase_edge_got[step, WAY[(0, dy, dz)], 0]
                        place = entry * 8 + 2 * x + half
                        corner = cover((0, dy, dz), unpack_z(corner, place, dz), fills[entry])
                        shifted[dz][min(first + entry, 1), x + 1, ghost : ghost + 1, :] = jnp.where(
                            row_lane == edge_lane(dz), corner, pltpu.roll(line, 1 if dz == 1 else 127, axis=1)
                        )
        for dx, plane, column in ((1, 0, NX - 1), (-1, NX + 1, 0)):
            for dy, ghost in ((1, LO - 1), (-1, HI)):
                arrive((dx, dy, 0))
                for entry in range(count):
                    line = phase_edge_got[step, WAY[(dx, dy, 0)], entry]
                    scalars[first + entry, plane, ghost : ghost + 1, :] = cover((0, dy, 0), line, fills[entry])
            arrive((dx, 0, 0))
            for dz in (1, -1):
                arrive((dx, 0, dz))
                for entry in range(count):
                    shift_plane(entry, plane, dz, phase_z_got[step, WAY[(dx, 0, dz)]], column)

    def relax_body(step, x):
        total = state[0, x]
        flux = [0.0, 0.0, 0.0]
        for up, down in PAIRS:
            first, second = state[up, x], state[down, x]
            total = total + (first + second)
            difference = first - second
            for axis in range(3):
                if VELOCITY[up][axis] == 1:
                    flux[axis] = flux[axis] + difference
                elif VELOCITY[up][axis] == -1:
                    flux[axis] = flux[axis] - difference
        inverse = 1.0 / total
        velocity = [part * inverse for part in flux]
        phase = scalars[step + 1, x + 1, LO:HI, :]
        tau = 1.3 - 0.3 * phase
        rate = 1.0 / tau
        keep = 1.0 - rate
        for axis in range(3):
            speed[axis, x] = velocity[axis]
        if step == 0:
            red = total * (0.05 + 0.9 * labels[x].astype(jnp.float32))
            blue = total - red
            colour[0, x] = red
            colour[1, x] = blue
        shifted = [velocity[0] + tau * inverse * 0.001, velocity[1], velocity[2]]
        square = shifted[0] * shifted[0] + shifted[1] * shifted[1] + shifted[2] * shifted[2]
        scale = rate * total
        base = scale * (1.0 - 1.5 * square)
        state[0, x] = keep * state[0, x] + base * (1.0 / 3.0)
        face, edge = base * (1.0 / 18.0), base * (1.0 / 36.0)
        for up, down in PAIRS:
            along = 0.0
            for axis in range(3):
                if VELOCITY[up][axis] == 1:
                    along = along + shifted[axis]
                elif VELOCITY[up][axis] == -1:
                    along = along - shifted[axis]
            push = scale * along
            if up < 7:
                even, odd = face + 0.25 * (push * along), push * (1.0 / 6.0)
            else:
                even, odd = edge + 0.125 * (push * along), push * (1.0 / 12.0)
            state[up, x] = keep * state[up, x] + (even + odd)
            state[down, x] = keep * state[down, x] + (even - odd)

    def gradient_at(step, x):
        def at(buffer, place, plane, dy):
            return buffer[place, plane, LO + dy : HI + dy, :]

        here_ = step + 1

        def spread(plane):
            return (
                2.0 * at(scalars, here_, plane, 0)
                + (at(scalars, here_, plane, 1) + at(scalars, here_, plane, -1))
                + (at(scalars_up, 1, plane, 0) + at(scalars_down, 1, plane, 0))
            )

        def slope_y(plane):
            return at(scalars, here_, plane, 1) - at(scalars, here_, plane, -1)

        def slope_z(plane):
            return at(scalars_up, 1, plane, 0) - at(scalars_down, 1, plane, 0)

        low, mid, high = x, x + 1, x + 2
        up_up, up_down = at(scalars_up, 1, mid, 1), at(scalars_up, 1, mid, -1)
        down_up, down_down = at(scalars_down, 1, mid, 1), at(scalars_down, 1, mid, -1)
        along_x = spread(high) - spread(low)
        along_y = 2.0 * slope_y(mid) + (slope_y(high) + slope_y(low)) + ((up_up - up_down) + (down_up - down_down))
        along_z = 2.0 * slope_z(mid) + (slope_z(high) + slope_z(low)) + ((up_up - down_up) + (up_down - down_down))
        return [part * (1.0 / 12.0) for part in (along_x, along_y, along_z)]

    def put_post(step, x, name, value, packed):
        kind, number = name
        offset = VELOCITY[number]
        if offset[1] != 0:
            sign = offset[1]
            edge = HI - 1 if sign == 1 else LO
        up, down = packed
        if offset[2] != 0:
            unrolled[UNROLLED[name], x] = value
            sign_z = offset[2]
            first = Z_FACE[sign_z].index(name) * 8
            for half in range(2):
                tile = value[8 * half : 8 * half + 8]
                place = first + 2 * x + half
                if sign_z == 1:
                    up = pack_z(tile, place, 1, up)
                else:
                    down = pack_z(tile, place, -1, down)
            value = pltpu.roll(value, 1 if sign_z == 1 else 127, axis=1)
        posts[step, SLOT[name], x + 1, LO:HI, :] = value
        if offset[1] != 0:
            line = Y_FACE[sign].index(name) * 4 + x
            post_y[step, SIDE[sign], line] = posts[step, SLOT[name], x + 1, edge : edge + 1, :]
        return up, down

    def collide_body(step, x, packed):
        gradient = gradient_at(step, x)
        squares = [part * part for part in gradient]
        total = squares[0] + squares[1] + squares[2]
        packed = put_post(step, x, ("f", 0), state[0, x], packed)
        third = total * (1.0 / 3.0)
        for up, down in PAIRS:
            if up < 7:
                surface = (TENSION / 18.0) * (squares[(up - 1) // 2] - third)
            else:
                slope = 0.0
                for axis in range(3):
                    if VELOCITY[up][axis] == 1:
                        slope = slope + gradient[axis]
                    elif VELOCITY[up][axis] == -1:
                        slope = slope - gradient[axis]
                surface = (TENSION / 36.0) * (slope * slope - 2.0 * third)
            packed = put_post(step, x, ("f", up), state[up, x] + surface, packed)
            packed = put_post(step, x, ("f", down), state[down, x] + surface, packed)
        red, blue = colour[0, x], colour[1, x]
        mixing = (0.5 * 0.125) * (red * blue / (red + blue)) * lax.rsqrt(jnp.maximum(total, 0.01))
        packed = put_post(step, x, ("r", 0), 0.25 * red, packed)
        packed = put_post(step, x, ("b", 0), 0.25 * blue, packed)
        for axis in range(3):
            drift = 0.5 * speed[axis, x]
            across = mixing * gradient[axis]
            for kind, amount, turn in (("r", red, 1.0), ("b", blue, -1.0)):
                mean = 0.125 * amount
                lean = amount * drift + turn * across
                packed = put_post(step, x, (kind, 2 * axis + 1), mean + lean, packed)
                packed = put_post(step, x, (kind, 2 * axis + 2), mean - lean, packed)
        return packed

    def unpack_posts(step, copies):
        def arrive(*offsets):
            for offset in offsets:
                copies[offset].wait_recv()

        def put_column(dz, entry, plane, face, column):
            slot = SLOT[Z_FACE[dz][entry]]
            for half in range(2):
                rows = slice(LO + 8 * half, LO + 8 * half + 8)
                place = entry * 8 + 2 * column + half
                posts[step, slot, plane, rows, :] = jnp.where(
                    lane == edge_lane(dz), unpack_z(face, place, dz), posts[step, slot, plane, rows, :]
                )

        for copy in copies.values():
            copy.wait_send()
        for dz in (1, -1):
            arrive((0, 0, dz))
            face = post_z_got[step, WAY[(0, 0, dz)]]
            for entry, name in enumerate(Z_FACE[dz]):
                for x in range(NX):
                    plane = x + 1 - VELOCITY[name[1]][0]
                    if 1 <= plane <= NX:
                        put_column(dz, entry, plane, face, plane - 1)
        for dy, ghost in ((1, LO - 1), (-1, HI)):
            half = 1 if dy == 1 else 0
            arrive((0, dy, 0), (0, dy, 1), (0, dy, -1))
            for entry, name in enumerate(Y_FACE[dy]):
                dx, _, dz = VELOCITY[name[1]]
                for x in range(NX):
                    plane = x + 1 - dx
                    if not 1 <= plane <= NX:
                        continue
                    line = post_y_got[step, SIDE[dy], entry * 4 + plane - 1]
                    if dz != 0:
                        corner = post_edge_got[step, WAY[(0, dy, dz)]]
                        place = Z_FACE[dz].index(name) * 8 + 2 * x + half
                        line = jnp.where(row_lane == edge_lane(dz), unpack_z(corner, place, dz), line)
                    posts[step, SLOT[name], plane, ghost : ghost + 1, :] = line
        for dx, plane, column in ((1, 0, NX - 1), (-1, NX + 1, 0)):
            for dy, ghost in ((1, LO - 1), (-1, HI)):
                offset = (dx, dy, 0)
                arrive(offset)
                slot = SLOT[("f", VELOCITY.index(offset))]
                posts[step, slot, plane, ghost : ghost + 1, :] = post_edge_got[step, WAY[offset]]
            arrive((dx, 0, 0))
            for dz in (1, -1):
                offset = (dx, 0, dz)
                arrive(offset)
                entry = Z_FACE[dz].index(("f", VELOCITY.index(offset)))
                put_column(dz, entry, plane, post_z_got[step, WAY[offset]], column)

    def stream_body(step, x, packed):
        last = step == STEPS - 1
        shifted = {0: scalars, 1: scalars_down, -1: scalars_up}
        fluid = scalars[0, x + 1, LO:HI, :] > 0.0
        opened = [fluid]
        for offset in DIRECTIONS:
            dx, dy, dz = offset
            opened.append(shifted[dz][0, x + 1 - dx, LO - dy : HI - dy, :] > 0.0)

        def pulled(kind, number):
            dx, dy, dz = VELOCITY[number]
            arriving = posts[step, SLOT[(kind, number)], x + 1 - dx, LO - dy : HI - dy, :]
            if number == 0:
                return arriving
            back = (kind, OPPOSITE[number])
            if dz != 0:
                bounced = unrolled[UNROLLED[back], x]
            else:
                bounced = posts[step, SLOT[back], x + 1, LO:HI, :]
            return jnp.where(opened[number], arriving, bounced)

        for number in range(19):
            value = pulled("f", number)
            state[number, x] = jnp.where(fluid, value, 0.0) if last else value
        sums = []
        for place, kind in enumerate(("r", "b")):
            total = 0.0
            for number in range(7):
                value = pulled(kind, number)
                if last:
                    state[19 + 7 * place + number, x] = jnp.where(fluid, value, 0.0)
                else:
                    total = total + value
            if not last:
                colour[place, x] = total
                sums.append(total)
        if last:
            return packed
        red, blue = sums
        phase = jnp.where(fluid, (red - blue) / (red + blue), WETTING)
        return set_phase(step + 1, x, [phase], packed)

    blank = jnp.zeros((8, NZ), jnp.float32)

    def first_phase(x, packed):
        fluid = 1.0 - solid[x].astype(jnp.float32)
        phase = jnp.where(fluid > 0.0, -0.9 + 1.8 * labels[x].astype(jnp.float32), WETTING)
        return set_phase(0, x, [fluid, phase], packed)

    loads[0].wait()
    loads[1].wait()
    packed = lax.fori_loop(0, NX, first_phase, (blank, blank), unroll=True)
    pl.semaphore_wait(barrier, len(DIRECTIONS))
    copies = send_phase(0, packed)
    loads[2].wait()
    for step in range(STEPS):
        lax.fori_loop(0, NX, lambda x, _: relax_body(step, x), None, unroll=True)
        unpack_phase(step, copies)
        packed = (blank, blank)
        packed = lax.fori_loop(0, 2, lambda turn, p: collide_body(step, 3 - 3 * turn, p), packed, unroll=True)
        copies = post_x_copies(step)
        for copy in copies.values():
            copy.start()
        packed = lax.fori_loop(1, 3, lambda x, p: collide_body(step, x, p), packed, unroll=True)
        for dz in (1, -1):
            post_z[step, SIDE[dz]] = packed[SIDE[dz]]
            for dy, edge in ((1, 7), (-1, 0)):
                post_yz[step, YZ_WAY[(dy, dz)]] = post_z[step, SIDE[dz], edge : edge + 1, :]
        others = post_other_copies(step)
        for copy in others.values():
            copy.start()
        unpack_posts(step, {**copies, **others})
        if step < STEPS - 1:
            packed = lax.fori_loop(0, NX, lambda x, p: stream_body(step, x, p), (blank, blank), unroll=True)
            copies = send_phase(step + 1, packed)
        else:
            lax.fori_loop(0, NX, lambda x, p: stream_body(step, x, p), (blank, blank), unroll=True)

    store = pltpu.make_async_copy(state, every_out, out_sem)
    store.start()
    store.wait()


def hand_out(every, momentum_out, red_out, blue_out, sem):
    copies = []
    first = 0
    for place, target in enumerate((momentum_out, red_out, blue_out)):
        count = target.shape[0]
        copies.append(pltpu.make_async_copy(every.at[pl.ds(first, count)], target, sem.at[place]))
        first += count
    for copy in copies:
        copy.start()
    for copy in copies:
        copy.wait()


def shards(sizes, momentum_sets, labels, solid_mask):
    block = (NX, NY, NZ)
    f32 = jnp.float32
    anywhere = pl.BlockSpec(memory_space=pl.ANY)
    vmem = lambda *shape, dtype=f32: pltpu.VMEM(shape, dtype)
    every = pl.pallas_call(
        functools.partial(kernel, sizes=sizes),
        out_shape=jax.ShapeDtypeStruct((33,) + block, f32),
        in_specs=[anywhere] * 3,
        out_specs=anywhere,
        scratch_shapes=[
            vmem(33, *block),
            vmem(*block, dtype=jnp.int32),
            vmem(*block, dtype=jnp.int32),
            vmem(1 + STEPS, NX + 2, ROWS, NZ),
            vmem(2, NX + 2, ROWS, NZ),
            vmem(2, NX + 2, ROWS, NZ),
            vmem(STEPS, 33, NX + 2, ROWS, NZ),
            vmem(14, *block),
            vmem(3, *block),
            vmem(2, *block),
            vmem(STEPS, 2, 8, 1, NZ),
            vmem(STEPS, 2, 8, NZ),
            vmem(STEPS, 4, 1, 1, NZ),
            vmem(STEPS, 2, 8, 1, NZ),
            vmem(STEPS, 18, 2, 1, NZ),
            vmem(STEPS, 18, 8, NZ),
            vmem(STEPS, 2, 28, 1, NZ),
            vmem(STEPS, 2, 8, NZ),
            vmem(STEPS, 4, 1, NZ),
            vmem(STEPS, 2, 28, 1, NZ),
            vmem(STEPS, 18, 1, NZ),
            vmem(STEPS, 18, 8, NZ),
            pltpu.SemaphoreType.DMA((3,)),
            pltpu.SemaphoreType.DMA,
            pltpu.SemaphoreType.DMA((2 * STEPS, 18)),
            pltpu.SemaphoreType.DMA((2 * STEPS, 18)),
        ],
        compiler_params=pltpu.CompilerParams(
            collective_id=0, has_side_effects=True, vmem_limit_bytes=VMEM_LIMIT
        ),
        cost_estimate=pl.CostEstimate(flops=15_000_000, bytes_accessed=1_800_000, transcendentals=0),
    )(momentum_sets, labels, solid_mask)
    return pl.pallas_call(
        hand_out,
        out_shape=[jax.ShapeDtypeStruct((count,) + block, f32) for count in (19, 7, 7)],
        in_specs=[anywhere],
        out_specs=[anywhere] * 3,
        scratch_shapes=[pltpu.SemaphoreType.DMA((3,))],
        compiler_params=pltpu.CompilerParams(vmem_limit_bytes=VMEM_LIMIT),
        cost_estimate=pl.CostEstimate(flops=0, bytes_accessed=2_200_000, transcendentals=0),
    )(every)


def solution(mesh):
    sizes = tuple(mesh.shape[axis] for axis in ("flow", "gy", "gz"))
    split = P("flow", "gy", "gz")
    split_sets = P(None, "flow", "gy", "gz")
    return jax.shard_map(
        functools.partial(shards, sizes),
        mesh=mesh,
        in_specs=(split_sets, split, split),
        out_specs=(split_sets, split_sets, split_sets),
        check_vma=False,
    )
```

```python
import functools

import jax
import jax.numpy as jnp
from jax import lax
from jax.experimental import pallas as pl
from jax.experimental.pallas import tpu as pltpu
from jax.sharding import PartitionSpec as P

STEPS = 3
NX, NY, NZ = 4, 16, 128
LO, HI = 8, 8 + NY
ROWS = 32
WETTING = 0.3
TENSION = 0.05
MESH = pl.DeviceIdType.MESH
VMEM_LIMIT = 40 * 1024 * 1024

VELOCITY = (
    (0, 0, 0),
    (1, 0, 0),
    (-1, 0, 0),
    (0, 1, 0),
    (0, -1, 0),
    (0, 0, 1),
    (0, 0, -1),
    (1, 1, 0),
    (-1, -1, 0),
    (1, -1, 0),
    (-1, 1, 0),
    (1, 0, 1),
    (-1, 0, -1),
    (1, 0, -1),
    (-1, 0, 1),
    (0, 1, 1),
    (0, -1, -1),
    (0, 1, -1),
    (0, -1, 1),
)
OPPOSITE = (0, 2, 1, 4, 3, 6, 5, 8, 7, 10, 9, 12, 11, 14, 13, 16, 15, 18, 17)
PAIRS = ((1, 2), (3, 4), (5, 6), (7, 8), (9, 10), (11, 12), (13, 14), (15, 16), (17, 18))

X_UP = [("f", i) for i in (1, 7, 9, 11, 13)] + [("r", 1), ("b", 1)]
X_DOWN = [("f", i) for i in (2, 8, 10, 12, 14)] + [("r", 2), ("b", 2)]
EVERY = [("f", i) for i in range(19)] + [("r", i) for i in range(7)] + [("b", i) for i in range(7)]
ORDER = X_UP + X_DOWN + [name for name in EVERY if name not in X_UP + X_DOWN]
SLOT = {name: place for place, name in enumerate(ORDER)}
Y_FACE = {
    1: (("f", 3), ("r", 3), ("f", 7), ("f", 10), ("f", 15), ("f", 17), ("b", 3)),
    -1: (("f", 4), ("r", 4), ("f", 9), ("f", 8), ("f", 18), ("f", 16), ("b", 4)),
}
Z_FACE = {
    1: (("f", 5), ("f", 11), ("f", 14), ("f", 15), ("f", 18), ("r", 5), ("b", 5)),
    -1: (("f", 6), ("f", 13), ("f", 12), ("f", 17), ("f", 16), ("r", 6), ("b", 6)),
}
Z_MOVING = Z_FACE[1] + Z_FACE[-1]
UNROLLED = {name: place for place, name in enumerate(Z_MOVING)}
DIRECTIONS = VELOCITY[1:]
WAY = {offset: place for place, offset in enumerate(DIRECTIONS)}
SIDE = {1: 0, -1: 1}
YZ_WAY = {(1, 1): 0, (1, -1): 1, (-1, 1): 2, (-1, -1): 3}
GROUPS = [
    [offset for offset in DIRECTIONS if offset[1:] == (dy, dz)]
    for dy, dz in ((0, 0), (1, 0), (-1, 0), (0, 1), (0, -1), (1, 1), (1, -1), (-1, 1), (-1, -1))
]
OTHERS = sorted(DIRECTIONS[2:], key=lambda offset: (abs(offset[2]), abs(offset[0])))


def kernel(
    momentum_in,
    labels_in,
    solid_in,
    state,
    labels,
    solid,
    scalars,
    scalars_down,
    scalars_up,
    posts,
    unrolled,
    speed,
    colour,
    phase_y,
    phase_z,
    phase_yz,
    phase_y_got,
    phase_edge_got,
    phase_z_got,
    post_y,
    post_z,
    post_yz,
    post_y_got,
    post_edge_got,
    post_z_got,
    in_sem,
    send_sem,
    recv_sem,
    *,
    sizes,
):
    here = tuple(lax.axis_index(axis) for axis in ("flow", "gy", "gz"))

    def neighbour(offset):
        return tuple(
            here[axis] if offset[axis] == 0 else lax.rem(here[axis] + offset[axis] + sizes[axis], sizes[axis])
            for axis in range(3)
        )

    closed = {
        (1, -1): here[1] == 0,
        (1, 1): here[1] == sizes[1] - 1,
        (2, -1): here[2] == 0,
        (2, 1): here[2] == sizes[2] - 1,
    }
    def has(offset):
        known = [jnp.logical_not(closed[(axis, offset[axis])]) for axis in (1, 2) if offset[axis] != 0]
        return functools.reduce(jnp.logical_and, known) if known else None

    def when(condition, action):
        if condition is None:
            action()
        else:
            pl.when(condition)(action)

    def each(copies, verb, backward=False):
        for group in GROUPS:
            mine = [copies[offset] for offset in group if offset in copies]
            dy, dz = group[0][1:]
            if mine:
                when(
                    has((0, -dy, -dz) if backward else (0, dy, dz)),
                    lambda mine=mine: [getattr(copy, verb)() for copy in mine] and None,
                )

    lane = lax.broadcasted_iota(jnp.int32, (8, NZ), 1)
    row_lane = lax.broadcasted_iota(jnp.int32, (1, NZ), 1)

    loads = [
        pltpu.make_async_copy(solid_in, solid, in_sem.at[0]),
        pltpu.make_async_copy(labels_in, labels, in_sem.at[1]),
        pltpu.make_async_copy(momentum_in, state.at[pl.ds(0, 19)], in_sem.at[2]),
    ]
    for load in loads:
        load.start()

    barrier = pltpu.get_barrier_semaphore()
    for group in GROUPS:

        def greet(group=group):
            for offset in group:
                pl.semaphore_signal(barrier, inc=1, device_id=neighbour(offset), device_id_type=MESH)

        when(has((0,) + group[0][1:]), greet)
    beside_y = 2 - closed[(1, 1)].astype(jnp.int32) - closed[(1, -1)].astype(jnp.int32)
    beside_z = 2 - closed[(2, 1)].astype(jnp.int32) - closed[(2, -1)].astype(jnp.int32)
    beside = 2 + 3 * (beside_y + beside_z) + beside_y * beside_z

    def remote(source, target, turn, offset):
        way = WAY[offset]
        return pltpu.make_async_remote_copy(
            src_ref=source,
            dst_ref=target,
            send_sem=send_sem.at[turn, way],
            recv_sem=recv_sem.at[turn, way],
            device_id=neighbour(offset),
            device_id_type=MESH,
        )

    def phase_copies(step, initial):
        first, count = (0, 2) if initial else (step + 1, 1)
        copies = []
        for offset in DIRECTIONS:
            dx, dy, dz = offset
            way = WAY[offset]
            if dx != 0 and dy != 0:
                source = phase_y.at[step, SIDE[dy], pl.ds((NX - 1) * count if dx == 1 else 0, count)]
                target = phase_edge_got.at[step, way, pl.ds(0, count)]
            elif dy != 0 and dz != 0:
                source = phase_yz.at[step, YZ_WAY[(dy, dz)]]
                target = phase_edge_got.at[step, way, pl.ds(0, 1)]
            elif dy != 0:
                source = phase_y.at[step, SIDE[dy], pl.ds(0, NX * count)]
                target = phase_y_got.at[step, SIDE[dy], pl.ds(0, NX * count)]
            elif dz != 0:
                source = phase_z.at[step, SIDE[dz]]
                target = phase_z_got.at[step, way]
            else:
                near, far = (NX, 0) if offset[0] == 1 else (1, NX + 1)
                copies.append(
                    remote(
                        scalars.at[pl.ds(first, count), near, pl.ds(LO, NY)],
                        scalars.at[pl.ds(first, count), far, pl.ds(LO, NY)],
                        2 * step,
                        offset,
                    )
                )
                continue
            copies.append(remote(source, target, 2 * step, offset))
        return dict(zip(DIRECTIONS, copies))

    def post_x_copies(step):
        copies = {}
        for sign, first, near, far in ((1, 0, NX, 0), (-1, 7, 1, NX + 1)):
            copies[(sign, 0, 0)] = remote(
                posts.at[step, pl.ds(first, 7), near, pl.ds(LO, NY)],
                posts.at[step, pl.ds(first, 7), far, pl.ds(LO, NY)],
                2 * step + 1,
                (sign, 0, 0),
            )
        return copies

    def post_other_copies(step):
        copies = {}
        for offset in OTHERS:
            dx, dy, dz = offset
            way = WAY[offset]
            if dy != 0 and dx == 0 and dz == 0:
                source, target = post_y.at[step, SIDE[dy]], post_y_got.at[step, SIDE[dy]]
            elif dx != 0 and dy != 0:
                line = Y_FACE[dy].index(("f", VELOCITY.index(offset))) * 4 + (NX - 1 if dx == 1 else 0)
                source, target = post_y.at[step, SIDE[dy], line], post_edge_got.at[step, way]
            elif dy != 0:
                source, target = post_yz.at[step, YZ_WAY[(dy, dz)]], post_edge_got.at[step, way]
            else:
                source, target = post_z.at[step, SIDE[dz]], post_z_got.at[step, way]
            copies[offset] = remote(source, target, 2 * step + 1, offset)
        return copies

    def pack_z(tile, place, sign, packed):
        moved = pltpu.roll(tile, place + 1 if sign == 1 else place, axis=1)
        return jnp.where(lane == place, moved, packed)

    def unpack_z(packed, place, sign):
        return pltpu.roll(packed, (128 - place) % 128 if sign == 1 else 127 - place, axis=1)

    def edge_lane(sign):
        return 0 if sign == 1 else NZ - 1

    def set_phase(step, x, values, packed):
        count = len(values)
        first = 0 if count == 2 else step + 1
        up, down = packed
        for entry, value in enumerate(values):
            scalars[first + entry, x + 1, LO:HI, :] = value
            for dy, edge in ((1, HI - 1), (-1, LO)):
                phase_y[step, SIDE[dy], x * count + entry] = scalars[first + entry, x + 1, edge : edge + 1, :]
            for half in range(2):
                tile = value[8 * half : 8 * half + 8]
                place = entry * 8 + 2 * x + half
                up = pack_z(tile, place, 1, up)
                down = pack_z(tile, place, -1, down)
        return up, down

    def send_phase(step, packed, initial):
        for dz in (1, -1):
            phase_z[step, SIDE[dz]] = packed[SIDE[dz]]
            for dy, edge in ((1, 7), (-1, 0)):
                phase_yz[step, YZ_WAY[(dy, dz)], 0] = phase_z[step, SIDE[dz], edge : edge + 1, :]
        copies = phase_copies(step, initial)
        each(copies, "start")
        return copies

    def unpack_phase(step, copies, initial):
        first, count = (0, 2) if initial else (step + 1, 1)
        fills = (0.0, WETTING) if initial else (WETTING,)
        shifted = {1: scalars_down, -1: scalars_up}

        def place_of(entry):
            return entry if initial else 1

        def cover(offset, value, fill):
            for axis in (1, 2):
                if offset[axis] != 0:
                    value = jnp.where(closed[(axis, -offset[axis])], fill, value)
            return value

        def arrive(*offsets):
            each({offset: copies[offset] for offset in offsets}, "wait_recv", backward=True)

        def shift_plane(entry, plane, dz, face, column):
            for half in range(2):
                rows = slice(LO + 8 * half, LO + 8 * half + 8)
                value = scalars[first + entry, plane, rows, :]
                place = entry * 8 + 2 * column + half
                ghost = cover((0, 0, dz), unpack_z(face, place, dz), fills[entry])
                shifted[dz][place_of(entry), plane, rows, :] = jnp.where(
                    lane == edge_lane(dz), ghost, pltpu.roll(value, 1 if dz == 1 else 127, axis=1)
                )

        each(copies, "wait_send")
        for dz in (1, -1):
            arrive((0, 0, dz))
            face = phase_z_got[step, WAY[(0, 0, dz)]]
            for entry in range(count):
                for x in range(NX):
                    shift_plane(entry, x + 1, dz, face, x)
        for dy, ghost in ((1, LO - 1), (-1, HI)):
            half = 1 if dy == 1 else 0
            arrive((0, dy, 0), (0, dy, 1), (0, dy, -1))
            for entry in range(count):
                for x in range(NX):
                    line = cover((0, dy, 0), phase_y_got[step, SIDE[dy], x * count + entry], fills[entry])
                    scalars[first + entry, x + 1, ghost : ghost + 1, :] = line
                    for dz in (1, -1):
                        corner = phase_edge_got[step, WAY[(0, dy, dz)], 0]
                        place = entry * 8 + 2 * x + half
                        corner = cover((0, dy, dz), unpack_z(corner, place, dz), fills[entry])
                        shifted[dz][place_of(entry), x + 1, ghost : ghost + 1, :] = jnp.where(
                            row_lane == edge_lane(dz), corner, pltpu.roll(line, 1 if dz == 1 else 127, axis=1)
                        )
        for dx, plane, column in ((1, 0, NX - 1), (-1, NX + 1, 0)):
            arrive((dx, 1, 0), (dx, -1, 0), (dx, 0, 0), (dx, 0, 1), (dx, 0, -1))
            for dy, ghost in ((1, LO - 1), (-1, HI)):
                for entry in range(count):
                    line = phase_edge_got[step, WAY[(dx, dy, 0)], entry]
                    scalars[first + entry, plane, ghost : ghost + 1, :] = cover((0, dy, 0), line, fills[entry])
            for dz in (1, -1):
                for entry in range(count):
                    shift_plane(entry, plane, dz, phase_z_got[step, WAY[(dx, 0, dz)]], column)

    def relax_body(step, x, initial):
        total = state[0, x]
        flux = [0.0, 0.0, 0.0]
        for up, down in PAIRS:
            first, second = state[up, x], state[down, x]
            total = total + (first + second)
            difference = first - second
            for axis in range(3):
                if VELOCITY[up][axis] == 1:
                    flux[axis] = flux[axis] + difference
                elif VELOCITY[up][axis] == -1:
                    flux[axis] = flux[axis] - difference
        inverse = 1.0 / total
        velocity = [part * inverse for part in flux]
        phase = scalars[step + 1, x + 1, LO:HI, :]
        tau = 1.3 - 0.3 * phase
        rate = 1.0 / tau
        keep = 1.0 - rate
        for axis in range(3):
            speed[axis, x] = velocity[axis]
        if initial:
            red = total * (0.05 + 0.9 * labels[x].astype(jnp.float32))
            blue = total - red
            colour[0, x] = red
            colour[1, x] = blue
        shifted = [velocity[0] + tau * inverse * 0.001, velocity[1], velocity[2]]
        square = shifted[0] * shifted[0] + shifted[1] * shifted[1] + shifted[2] * shifted[2]
        scale = rate * total
        base = scale * (1.0 - 1.5 * square)
        state[0, x] = keep * state[0, x] + base * (1.0 / 3.0)
        face, edge = base * (1.0 / 18.0), base * (1.0 / 36.0)
        for up, down in PAIRS:
            along = 0.0
            for axis in range(3):
                if VELOCITY[up][axis] == 1:
                    along = along + shifted[axis]
                elif VELOCITY[up][axis] == -1:
                    along = along - shifted[axis]
            push = scale * along
            if up < 7:
                even, odd = face + 0.25 * (push * along), push * (1.0 / 6.0)
            else:
                even, odd = edge + 0.125 * (push * along), push * (1.0 / 12.0)
            state[up, x] = keep * state[up, x] + (even + odd)
            state[down, x] = keep * state[down, x] + (even - odd)

    def gradient_at(step, x):
        def at(buffer, place, plane, dy):
            return buffer[place, plane, LO + dy : HI + dy, :]

        here_ = step + 1

        def spread(plane):
            return (
                2.0 * at(scalars, here_, plane, 0)
                + (at(scalars, here_, plane, 1) + at(scalars, here_, plane, -1))
                + (at(scalars_up, 1, plane, 0) + at(scalars_down, 1, plane, 0))
            )

        def slope_y(plane):
            return at(scalars, here_, plane, 1) - at(scalars, here_, plane, -1)

        def slope_z(plane):
            return at(scalars_up, 1, plane, 0) - at(scalars_down, 1, plane, 0)

        low, mid, high = x, x + 1, x + 2
        up_up, up_down = at(scalars_up, 1, mid, 1), at(scalars_up, 1, mid, -1)
        down_up, down_down = at(scalars_down, 1, mid, 1), at(scalars_down, 1, mid, -1)
        along_x = spread(high) - spread(low)
        along_y = 2.0 * slope_y(mid) + (slope_y(high) + slope_y(low)) + ((up_up - up_down) + (down_up - down_down))
        along_z = 2.0 * slope_z(mid) + (slope_z(high) + slope_z(low)) + ((up_up - down_up) + (up_down - down_down))
        return [part * (1.0 / 12.0) for part in (along_x, along_y, along_z)]

    def put_post(step, x, name, value, packed):
        kind, number = name
        offset = VELOCITY[number]
        if offset[1] != 0:
            sign = offset[1]
            edge = HI - 1 if sign == 1 else LO
        up, down = packed
        if offset[2] != 0:
            unrolled[UNROLLED[name], x] = value
            sign_z = offset[2]
            first = Z_FACE[sign_z].index(name) * 8
            for half in range(2):
                tile = value[8 * half : 8 * half + 8]
                place = first + 2 * x + half
                if sign_z == 1:
                    up = pack_z(tile, place, 1, up)
                else:
                    down = pack_z(tile, place, -1, down)
            value = pltpu.roll(value, 1 if sign_z == 1 else 127, axis=1)
        posts[step, SLOT[name], x + 1, LO:HI, :] = value
        if offset[1] != 0:
            line = Y_FACE[sign].index(name) * 4 + x
            post_y[step, SIDE[sign], line] = posts[step, SLOT[name], x + 1, edge : edge + 1, :]
        return up, down

    def collide_body(step, x, packed):
        gradient = gradient_at(step, x)
        squares = [part * part for part in gradient]
        total = squares[0] + squares[1] + squares[2]
        packed = put_post(step, x, ("f", 0), state[0, x], packed)
        third = total * (1.0 / 3.0)
        for up, down in PAIRS:
            if up < 7:
                surface = (TENSION / 18.0) * (squares[(up - 1) // 2] - third)
            else:
                slope = 0.0
                for axis in range(3):
                    if VELOCITY[up][axis] == 1:
                        slope = slope + gradient[axis]
                    elif VELOCITY[up][axis] == -1:
                        slope = slope - gradient[axis]
                surface = (TENSION / 36.0) * (slope * slope - 2.0 * third)
            packed = put_post(step, x, ("f", up), state[up, x] + surface, packed)
            packed = put_post(step, x, ("f", down), state[down, x] + surface, packed)
        red, blue = colour[0, x], colour[1, x]
        mixing = (0.5 * 0.125) * (red * blue / (red + blue)) * lax.rsqrt(jnp.maximum(total, 0.01))
        packed = put_post(step, x, ("r", 0), 0.25 * red, packed)
        packed = put_post(step, x, ("b", 0), 0.25 * blue, packed)
        for axis in range(3):
            drift = 0.5 * speed[axis, x]
            across = mixing * gradient[axis]
            for kind, amount, turn in (("r", red, 1.0), ("b", blue, -1.0)):
                mean = 0.125 * amount
                lean = amount * drift + turn * across
                packed = put_post(step, x, (kind, 2 * axis + 1), mean + lean, packed)
                packed = put_post(step, x, (kind, 2 * axis + 2), mean - lean, packed)
        return packed

    def unpack_posts(step, copies):
        def arrive(*offsets):
            each({offset: copies[offset] for offset in offsets}, "wait_recv", backward=True)

        def put_column(dz, entry, plane, face, column):
            slot = SLOT[Z_FACE[dz][entry]]
            for half in range(2):
                rows = slice(LO + 8 * half, LO + 8 * half + 8)
                place = entry * 8 + 2 * column + half
                posts[step, slot, plane, rows, :] = jnp.where(
                    lane == edge_lane(dz), unpack_z(face, place, dz), posts[step, slot, plane, rows, :]
                )

        each(copies, "wait_send")
        for dz in (1, -1):
            arrive((0, 0, dz))
            face = post_z_got[step, WAY[(0, 0, dz)]]
            for entry, name in enumerate(Z_FACE[dz]):
                for x in range(NX):
                    plane = x + 1 - VELOCITY[name[1]][0]
                    if 1 <= plane <= NX:
                        put_column(dz, entry, plane, face, plane - 1)
        for dy, ghost in ((1, LO - 1), (-1, HI)):
            half = 1 if dy == 1 else 0
            arrive((0, dy, 0), (0, dy, 1), (0, dy, -1))
            for entry, name in enumerate(Y_FACE[dy]):
                dx, _, dz = VELOCITY[name[1]]
                for x in range(NX):
                    plane = x + 1 - dx
                    if not 1 <= plane <= NX:
                        continue
                    line = post_y_got[step, SIDE[dy], entry * 4 + plane - 1]
                    if dz != 0:
                        corner = post_edge_got[step, WAY[(0, dy, dz)]]
                        place = Z_FACE[dz].index(name) * 8 + 2 * x + half
                        line = jnp.where(row_lane == edge_lane(dz), unpack_z(corner, place, dz), line)
                    posts[step, SLOT[name], plane, ghost : ghost + 1, :] = line
        for dx, plane, column in ((1, 0, NX - 1), (-1, NX + 1, 0)):
            arrive((dx, 1, 0), (dx, -1, 0), (dx, 0, 0), (dx, 0, 1), (dx, 0, -1))
            for dy, ghost in ((1, LO - 1), (-1, HI)):
                offset = (dx, dy, 0)
                slot = SLOT[("f", VELOCITY.index(offset))]
                posts[step, slot, plane, ghost : ghost + 1, :] = post_edge_got[step, WAY[offset]]
            for dz in (1, -1):
                offset = (dx, 0, dz)
                entry = Z_FACE[dz].index(("f", VELOCITY.index(offset)))
                put_column(dz, entry, plane, post_z_got[step, WAY[offset]], column)

    def stream_body(step, x, packed):
        shifted = {0: scalars, 1: scalars_down, -1: scalars_up}
        fluid = scalars[0, x + 1, LO:HI, :] > 0.0
        opened = [fluid]
        for offset in DIRECTIONS:
            dx, dy, dz = offset
            opened.append(shifted[dz][0, x + 1 - dx, LO - dy : HI - dy, :] > 0.0)

        def pulled(kind, number):
            dx, dy, dz = VELOCITY[number]
            arriving = posts[step, SLOT[(kind, number)], x + 1 - dx, LO - dy : HI - dy, :]
            if number == 0:
                return arriving
            back = (kind, OPPOSITE[number])
            if dz != 0:
                bounced = unrolled[UNROLLED[back], x]
            else:
                bounced = posts[step, SLOT[back], x + 1, LO:HI, :]
            return jnp.where(opened[number], arriving, bounced)

        for number in range(19):
            state[number, x] = jnp.where(fluid, pulled("f", number), 0.0)
        sums = []
        for place, kind in enumerate(("r", "b")):
            total = 0.0
            for number in range(7):
                value = pulled(kind, number)
                state[19 + 7 * place + number, x] = jnp.where(fluid, value, 0.0)
                total = total + value
            colour[place, x] = total
            sums.append(total)
        red, blue = sums
        phase = jnp.where(fluid, (red - blue) / (red + blue), WETTING)
        return set_phase(step + 1, x, [phase], packed)

    blank = jnp.zeros((8, NZ), jnp.float32)

    def first_phase(x, packed):
        fluid = 1.0 - solid[x].astype(jnp.float32)
        phase = jnp.where(fluid > 0.0, -0.9 + 1.8 * labels[x].astype(jnp.float32), WETTING)
        return set_phase(0, x, [fluid, phase], packed)

    loads[0].wait()
    loads[1].wait()
    packed = lax.fori_loop(0, NX, first_phase, (blank, blank), unroll=True)
    pl.semaphore_wait(barrier, beside)
    copies = send_phase(0, packed, True)
    loads[2].wait()
    lax.fori_loop(0, NX, lambda x, _: relax_body(0, x, True), None, unroll=True)
    unpack_phase(0, copies, True)

    def step_body(step, _):
        packed = (blank, blank)
        packed = lax.fori_loop(0, 2, lambda turn, p: collide_body(step, 3 - 3 * turn, p), packed, unroll=True)
        copies = post_x_copies(step)
        each(copies, "start")
        packed = lax.fori_loop(1, 3, lambda x, p: collide_body(step, x, p), packed, unroll=True)
        for dz in (1, -1):
            post_z[step, SIDE[dz]] = packed[SIDE[dz]]
            for dy, edge in ((1, 7), (-1, 0)):
                post_yz[step, YZ_WAY[(dy, dz)]] = post_z[step, SIDE[dz], edge : edge + 1, :]
        others = post_other_copies(step)
        each(others, "start")
        unpack_posts(step, {**copies, **others})
        packed = lax.fori_loop(0, NX, lambda x, p: stream_body(step, x, p), (blank, blank), unroll=True)

        @pl.when(step < STEPS - 1)
        def _():
            copies = send_phase(step + 1, packed, False)
            lax.fori_loop(0, NX, lambda x, _: relax_body(step + 1, x, False), None, unroll=True)
            unpack_phase(step + 1, copies, False)

    lax.fori_loop(0, STEPS, step_body, None)


def hand_out(every, momentum_out, red_out, blue_out, sem):
    copies = []
    first = 0
    for place, target in enumerate((momentum_out, red_out, blue_out)):
        count = target.shape[0]
        copies.append(pltpu.make_async_copy(every.at[pl.ds(first, count)], target, sem.at[place]))
        first += count
    for copy in copies:
        copy.start()
    for copy in copies:
        copy.wait()


def shards(sizes, momentum_sets, labels, solid_mask):
    block = (NX, NY, NZ)
    f32 = jnp.float32
    vmem = lambda *shape, dtype=f32: pltpu.VMEM(shape, dtype)
    every = pl.pallas_call(
        functools.partial(kernel, sizes=sizes),
        out_shape=vmem(33, *block),
        in_specs=[pl.BlockSpec(memory_space=pltpu.HBM)] * 3,
        out_specs=pl.BlockSpec(memory_space=pltpu.VMEM),
        scratch_shapes=[
            vmem(*block, dtype=jnp.int32),
            vmem(*block, dtype=jnp.int32),
            vmem(2 + STEPS, NX + 2, ROWS, NZ),
            vmem(2, NX + 2, ROWS, NZ),
            vmem(2, NX + 2, ROWS, NZ),
            vmem(STEPS, 33, NX + 2, ROWS, NZ),
            vmem(14, *block),
            vmem(3, *block),
            vmem(2, *block),
            vmem(STEPS + 1, 2, 8, 1, NZ),
            vmem(STEPS, 2, 8, NZ),
            vmem(STEPS, 4, 1, 1, NZ),
            vmem(STEPS, 2, 8, 1, NZ),
            vmem(STEPS, 18, 2, 1, NZ),
            vmem(STEPS, 18, 8, NZ),
            vmem(STEPS, 2, 28, 1, NZ),
            vmem(STEPS, 2, 8, NZ),
            vmem(STEPS, 4, 1, NZ),
            vmem(STEPS, 2, 28, 1, NZ),
            vmem(STEPS, 18, 1, NZ),
            vmem(STEPS, 18, 8, NZ),
            pltpu.SemaphoreType.DMA((3,)),
            pltpu.SemaphoreType.DMA((2 * STEPS, 18)),
            pltpu.SemaphoreType.DMA((2 * STEPS, 18)),
        ],
        compiler_params=pltpu.CompilerParams(
            collective_id=0, has_side_effects=True, vmem_limit_bytes=VMEM_LIMIT
        ),
        cost_estimate=pl.CostEstimate(flops=15_000_000, bytes_accessed=1_800_000, transcendentals=0),
    )(*(pltpu.with_memory_space_constraint(array, pltpu.HBM) for array in (momentum_sets, labels, solid_mask)))
    return pl.pallas_call(
        hand_out,
        out_shape=[jax.ShapeDtypeStruct((count,) + block, f32) for count in (19, 7, 7)],
        in_specs=[pl.BlockSpec(memory_space=pltpu.VMEM)],
        out_specs=[pl.BlockSpec(memory_space=pltpu.HBM)] * 3,
        scratch_shapes=[pltpu.SemaphoreType.DMA((3,))],
        cost_estimate=pl.CostEstimate(flops=0, bytes_accessed=2_200_000, transcendentals=0),
    )(every)


def solution(mesh):
    sizes = tuple(mesh.shape[axis] for axis in ("flow", "gy", "gz"))
    split = P("flow", "gy", "gz")
    split_sets = P(None, "flow", "gy", "gz")
    return jax.shard_map(
        functools.partial(shards, sizes),
        mesh=mesh,
        in_specs=(split_sets, split, split),
        out_specs=(split_sets, split_sets, split_sets),
        check_vma=False,
    )
```

```python
import functools

import jax
import jax.numpy as jnp
from jax import lax
from jax.experimental import pallas as pl
from jax.experimental.pallas import tpu as pltpu
from jax.sharding import PartitionSpec as P

STEPS = 3
NX, NY, NZ = 4, 16, 128
LO, HI = 8, 8 + NY
ROWS = 32
WETTING = 0.3
TENSION = 0.05
MESH = pl.DeviceIdType.MESH
VMEM_LIMIT = 40 * 1024 * 1024

VELOCITY = (
    (0, 0, 0),
    (1, 0, 0),
    (-1, 0, 0),
    (0, 1, 0),
    (0, -1, 0),
    (0, 0, 1),
    (0, 0, -1),
    (1, 1, 0),
    (-1, -1, 0),
    (1, -1, 0),
    (-1, 1, 0),
    (1, 0, 1),
    (-1, 0, -1),
    (1, 0, -1),
    (-1, 0, 1),
    (0, 1, 1),
    (0, -1, -1),
    (0, 1, -1),
    (0, -1, 1),
)
OPPOSITE = (0, 2, 1, 4, 3, 6, 5, 8, 7, 10, 9, 12, 11, 14, 13, 16, 15, 18, 17)
PAIRS = ((1, 2), (3, 4), (5, 6), (7, 8), (9, 10), (11, 12), (13, 14), (15, 16), (17, 18))

X_UP = [("f", i) for i in (1, 7, 9, 11, 13)] + [("r", 1), ("b", 1)]
X_DOWN = [("f", i) for i in (2, 8, 10, 12, 14)] + [("r", 2), ("b", 2)]
EVERY = [("f", i) for i in range(19)] + [("r", i) for i in range(7)] + [("b", i) for i in range(7)]
ORDER = X_UP + X_DOWN + [name for name in EVERY if name not in X_UP + X_DOWN]
SLOT = {name: place for place, name in enumerate(ORDER)}
Y_FACE = {
    1: (("f", 3), ("r", 3), ("f", 7), ("f", 10), ("f", 15), ("f", 17), ("b", 3)),
    -1: (("f", 4), ("r", 4), ("f", 9), ("f", 8), ("f", 18), ("f", 16), ("b", 4)),
}
Z_FACE = {
    1: (("f", 5), ("f", 11), ("f", 14), ("f", 15), ("f", 18), ("r", 5), ("b", 5)),
    -1: (("f", 6), ("f", 13), ("f", 12), ("f", 17), ("f", 16), ("r", 6), ("b", 6)),
}
Z_MOVING = Z_FACE[1] + Z_FACE[-1]
UNROLLED = {name: place for place, name in enumerate(Z_MOVING)}
DIRECTIONS = VELOCITY[1:]
CORNERS = tuple((a, b, c) for a in (1, -1) for b in (1, -1) for c in (1, -1))
NEIGHBOURS = DIRECTIONS + CORNERS
SIDE = {1: 0, -1: 1}
TURN = {0: 0, 1: 1, -1: 2}
FACE = {(1, 1): 3, (1, -1): 4, (0, 1): 1, (0, -1): 2, (2, 1): 5, (2, -1): 6}
IN_Z, SUM_Z, X_Z, Y_Z = 40, 56, 72, 88
SUM_Y, X_Y, Z_Y, ROWS_Y = 28, 36, 40, 42
Y_XY, SUM_XY, X_XY, ROWS_XY = 1, 3, 5, 7
ROWS_Y_ALL = ROWS_Y + 2 * ROWS_XY
Y_PART, Z_PART, ROWS_PART = 32, 40, 56
CLASSES = ((1, 0), (-1, 0), (1, 1), (1, -1), (-1, 1), (-1, -1), (0, 1), (0, -1))
CLASS = {way: place for place, way in enumerate(CLASSES)}
X_CLASS = {1: 8, -1: 9}
PART_CLASS = {1: 10, -1: 11}
ACROSS_YZ = tuple(("f", number) for number in (15, 16, 17, 18))


def kernel(
    momentum_in,
    labels_in,
    solid_in,
    state,
    labels,
    solid,
    scalars,
    scalars_down,
    scalars_up,
    posts,
    unrolled,
    speed,
    colour,
    phase_y,
    phase_z,
    phase_yz,
    phase_y_got,
    phase_z_got,
    phase_yz_got,
    post_y,
    post_z,
    post_row,
    post_xy,
    post_part,
    post_y_got,
    post_z_got,
    post_row_got,
    post_part_got,
    partial,
    in_sem,
    send_sem,
    recv_sem,
    *,
    sizes,
):
    here = tuple(lax.axis_index(axis) for axis in ("flow", "gy", "gz"))

    flow = {
        0: here[0],
        1: jnp.where(here[0] == sizes[0] - 1, 0, here[0] + 1),
        -1: jnp.where(here[0] == 0, sizes[0] - 1, here[0] - 1),
    }
    lateral = [{0: here[axis], 1: here[axis] + 1, -1: here[axis] - 1} for axis in (1, 2)]

    def neighbour(offset):
        return (flow[offset[0]], lateral[0][offset[1]], lateral[1][offset[2]])

    closed = {
        (1, -1): here[1] == 0,
        (1, 1): here[1] == sizes[1] - 1,
        (2, -1): here[2] == 0,
        (2, 1): here[2] == sizes[2] - 1,
    }
    def has(offset):
        known = [jnp.logical_not(closed[(axis, offset[axis])]) for axis in (1, 2) if offset[axis] != 0]
        return functools.reduce(jnp.logical_and, known) if known else None

    def when(condition, action):
        if condition is None:
            action()
        else:
            pl.when(condition)(action)

    def by_class(action, backward=False):
        for dy, dz in CLASSES:
            when(has((0, -dy, -dz) if backward else (0, dy, dz)), functools.partial(action, dy, dz))

    lane = lax.broadcasted_iota(jnp.int32, (8, NZ), 1)
    wide_lane = lax.broadcasted_iota(jnp.int32, (NY, NZ), 1)
    wide_row = lax.broadcasted_iota(jnp.int32, (NY, NZ), 0)
    row = lax.broadcasted_iota(jnp.int32, (8, NZ), 0)
    row_lane = lax.broadcasted_iota(jnp.int32, (1, NZ), 1)

    loads = [
        pltpu.make_async_copy(solid_in, solid, in_sem.at[0]),
        pltpu.make_async_copy(labels_in, labels, in_sem.at[1]),
        pltpu.make_async_copy(momentum_in, state.at[pl.ds(0, 19)], in_sem.at[2]),
    ]
    for load in loads:
        load.start()

    def send(source, target, turn, place, offset):
        pltpu.make_async_remote_copy(
            src_ref=source,
            dst_ref=target,
            send_sem=send_sem.at[turn, place],
            recv_sem=recv_sem.at[turn, place],
            device_id=neighbour(offset),
            device_id_type=MESH,
        ).start()

    def await_bytes(sems, turn, place, like):
        pltpu.make_async_copy(like, like, sems.at[turn, place]).wait()

    def send_phase_class(dy, dz):
        place = CLASS[(dy, dz)]
        if dz == 0:
            side = SIDE[dy]
            send(phase_y.at[side], phase_y_got.at[side, pl.ds(0, 8)], 0, place, (0, dy, 0))
            for dx, line, target in ((1, 6, 8), (-1, 0, 10)):
                source = phase_y.at[side, pl.ds(line, 2)]
                send(source, phase_y_got.at[side, pl.ds(target, 2)], 0, place, (dx, dy, 0))
        elif dy == 0:
            side = SIDE[dz]
            for dx in (0, 1, -1):
                send(phase_z.at[side], phase_z_got.at[side, TURN[dx]], 0, place, (dx, 0, dz))
        else:
            sides = SIDE[dy], SIDE[dz]
            send(phase_yz.at[sides], phase_yz_got.at[sides], 0, place, (0, dy, dz))

    def phase_like(dy, dz):
        if dz == 0:
            return phase_y_got.at[SIDE[dy]]
        if dy == 0:
            return phase_z_got.at[SIDE[dz]]
        return phase_yz_got.at[SIDE[dy], SIDE[dz]]

    def phase_plane(plane):
        return scalars.at[pl.ds(0, 2), plane, pl.ds(LO, NY)]

    def post_plane(step, dx, plane):
        return posts.at[step, pl.ds(0 if dx == 1 else 7, 7), plane, pl.ds(LO, NY)]

    def send_post_class(step, fused, dy, dz):
        turn, place = step + 1, CLASS[(dy, dz)]
        if dz == 0:
            side = SIDE[dy]
            send(post_y.at[step, side], post_y_got.at[step, side, pl.ds(0, ROWS_Y)], turn, place, (0, dy, 0))
            for dx in (1, -1):
                target = post_y_got.at[step, side, pl.ds(ROWS_Y + ROWS_XY * SIDE[dx], ROWS_XY)]
                send(post_xy.at[step, SIDE[dx], side], target, turn, place, (dx, dy, 0))
        elif dy == 0:
            side = SIDE[dz]
            for dx in (0, 1, -1):
                send(post_z.at[step, side], post_z_got.at[step, side, TURN[dx]], turn, place, (dx, 0, dz))
        else:
            sides = SIDE[dy], SIDE[dz]
            for dx in (0, 1, -1) if fused else (0,):
                target = post_row_got.at[step, sides[0], sides[1], TURN[dx]]
                send(post_row.at[step, sides[0], sides[1]], target, turn, place, (dx, dy, dz))

    def post_like(step, fused, dy, dz):
        if dz == 0:
            return post_y_got.at[step, SIDE[dy]]
        if dy == 0:
            return post_z_got.at[step, SIDE[dz]]
        return post_row_got.at[step, SIDE[dy], SIDE[dz], pl.ds(0, 3 if fused else 1)]

    def pack_z(tile, place, sign, packed):
        moved = pltpu.roll(tile, place + 1 if sign == 1 else place, axis=1)
        return jnp.where(lane == place, moved, packed)

    def unpack_z(packed, place, sign):
        return pltpu.roll(packed, (128 - place) % 128 if sign == 1 else 127 - place, axis=1)

    def edge_lane(sign):
        return 0 if sign == 1 else NZ - 1

    def set_phase(x, values, packed):
        up, down = packed
        for entry, value in enumerate(values):
            scalars[entry, x + 1, LO:HI, :] = value
            for dy, edge in ((1, HI - 1), (-1, LO)):
                phase_y[SIDE[dy], x * 2 + entry] = scalars[entry, x + 1, edge : edge + 1, :]
            for half in range(2):
                tile = value[8 * half : 8 * half + 8]
                place = entry * 8 + 2 * x + half
                up = pack_z(tile, place, 1, up)
                down = pack_z(tile, place, -1, down)
        return up, down

    def send_phase(packed):
        for dz in (1, -1):
            phase_z[SIDE[dz]] = packed[SIDE[dz]]
            for dy, edge in ((1, 7), (-1, 0)):
                phase_yz[SIDE[dy], SIDE[dz]] = phase_z[SIDE[dz], edge : edge + 1, :]
        by_class(send_phase_class)
        for dx, near, far in ((1, NX, 0), (-1, 1, NX + 1)):
            send(phase_plane(near), phase_plane(far), 0, X_CLASS[dx], (dx, 0, 0))

    def unpack_phase():
        first, count = 0, 2
        fills = (0.0, WETTING)
        shifted = {1: scalars_down, -1: scalars_up}

        def place_of(entry):
            return entry

        def cover(offset, value, fill):
            for axis in (1, 2):
                if offset[axis] != 0:
                    value = jnp.where(closed[(axis, -offset[axis])], fill, value)
            return value

        def arrive(sems, backward):
            by_class(lambda dy, dz: await_bytes(sems, 0, CLASS[(dy, dz)], phase_like(dy, dz)), backward)
            for dx in (1, -1):
                await_bytes(sems, 0, X_CLASS[dx], phase_plane(0))

        def shift_plane(entry, plane, dz, face, column):
            for half in range(2):
                rows = slice(LO + 8 * half, LO + 8 * half + 8)
                value = scalars[first + entry, plane, rows, :]
                place = entry * 8 + 2 * column + half
                ghost = cover((0, 0, dz), unpack_z(face, place, dz), fills[entry])
                shifted[dz][place_of(entry), plane, rows, :] = jnp.where(
                    lane == edge_lane(dz), ghost, pltpu.roll(value, 1 if dz == 1 else 127, axis=1)
                )

        arrive(send_sem, False)
        arrive(recv_sem, True)
        for dz in (1, -1):
            face = phase_z_got[SIDE[dz], 0]
            for entry in range(count):
                for x in range(NX):
                    shift_plane(entry, x + 1, dz, face, x)
        for dy, ghost in ((1, LO - 1), (-1, HI)):
            half = 1 if dy == 1 else 0
            for entry in range(count):
                for x in range(NX):
                    line = cover((0, dy, 0), phase_y_got[SIDE[dy], x * count + entry], fills[entry])
                    scalars[first + entry, x + 1, ghost : ghost + 1, :] = line
                    for dz in (1, -1):
                        corner = phase_yz_got[SIDE[dy], SIDE[dz]]
                        place = entry * 8 + 2 * x + half
                        corner = cover((0, dy, dz), unpack_z(corner, place, dz), fills[entry])
                        shifted[dz][place_of(entry), x + 1, ghost : ghost + 1, :] = jnp.where(
                            row_lane == edge_lane(dz), corner, pltpu.roll(line, 1 if dz == 1 else 127, axis=1)
                        )
        for dx, plane, column in ((1, 0, NX - 1), (-1, NX + 1, 0)):
            for dy, ghost in ((1, LO - 1), (-1, HI)):
                for entry in range(count):
                    line = phase_y_got[SIDE[dy], 8 + 2 * SIDE[dx] + entry]
                    scalars[first + entry, plane, ghost : ghost + 1, :] = cover((0, dy, 0), line, fills[entry])
            for dz in (1, -1):
                for entry in range(count):
                    shift_plane(entry, plane, dz, phase_z_got[SIDE[dz], TURN[dx]], column)

    def relax_body(step, x, initial):
        total = state[0, x]
        flux = [0.0, 0.0, 0.0]
        for up, down in PAIRS:
            first, second = state[up, x], state[down, x]
            total = total + (first + second)
            difference = first - second
            for axis in range(3):
                if VELOCITY[up][axis] == 1:
                    flux[axis] = flux[axis] + difference
                elif VELOCITY[up][axis] == -1:
                    flux[axis] = flux[axis] - difference
        inverse = 1.0 / total
        velocity = [part * inverse for part in flux]
        phase = scalars[step + 1, x + 1, LO:HI, :]
        tau = 1.3 - 0.3 * phase
        rate = 1.0 / tau
        keep = 1.0 - rate
        for axis in range(3):
            speed[axis, x] = velocity[axis]
        if initial:
            red = total * (0.05 + 0.9 * labels[x].astype(jnp.float32))
            blue = total - red
            colour[0, x] = red
            colour[1, x] = blue
        shifted = [velocity[0] + tau * inverse * 0.001, velocity[1], velocity[2]]
        square = shifted[0] * shifted[0] + shifted[1] * shifted[1] + shifted[2] * shifted[2]
        scale = rate * total
        base = scale * (1.0 - 1.5 * square)
        state[0, x] = keep * state[0, x] + base * (1.0 / 3.0)
        face, edge = base * (1.0 / 18.0), base * (1.0 / 36.0)
        for up, down in PAIRS:
            along = 0.0
            for axis in range(3):
                if VELOCITY[up][axis] == 1:
                    along = along + shifted[axis]
                elif VELOCITY[up][axis] == -1:
                    along = along - shifted[axis]
            push = scale * along
            if up < 7:
                even, odd = face + 0.25 * (push * along), push * (1.0 / 6.0)
            else:
                even, odd = edge + 0.125 * (push * along), push * (1.0 / 12.0)
            state[up, x] = keep * state[up, x] + (even + odd)
            state[down, x] = keep * state[down, x] + (even - odd)

    def gradient_at(step, x):
        def at(buffer, place, plane, dy):
            return buffer[place, plane, LO + dy : HI + dy, :]

        here_ = step + 1

        def spread(plane):
            return (
                2.0 * at(scalars, here_, plane, 0)
                + (at(scalars, here_, plane, 1) + at(scalars, here_, plane, -1))
                + (at(scalars_up, 1, plane, 0) + at(scalars_down, 1, plane, 0))
            )

        def slope_y(plane):
            return at(scalars, here_, plane, 1) - at(scalars, here_, plane, -1)

        def slope_z(plane):
            return at(scalars_up, 1, plane, 0) - at(scalars_down, 1, plane, 0)

        low, mid, high = x, x + 1, x + 2
        up_up, up_down = at(scalars_up, 1, mid, 1), at(scalars_up, 1, mid, -1)
        down_up, down_down = at(scalars_down, 1, mid, 1), at(scalars_down, 1, mid, -1)
        along_x = spread(high) - spread(low)
        along_y = 2.0 * slope_y(mid) + (slope_y(high) + slope_y(low)) + ((up_up - up_down) + (down_up - down_down))
        along_z = 2.0 * slope_z(mid) + (slope_z(high) + slope_z(low)) + ((up_up - down_up) + (up_down - down_down))
        return [part * (1.0 / 12.0) for part in (along_x, along_y, along_z)]

    def put_post(step, x, name, value, packed, fluid=None):
        kind, number = name
        offset = VELOCITY[number]
        value = jnp.where(fluid, value, 0.0)
        if offset[1] != 0:
            sign = offset[1]
            edge = HI - 1 if sign == 1 else LO
        up, down = packed
        if offset[2] != 0:
            unrolled[UNROLLED[name], x] = value
            sign_z = offset[2]
            first = Z_FACE[sign_z].index(name) * 8
            for half in range(2):
                tile = value[8 * half : 8 * half + 8]
                place = first + 2 * x + half
                if sign_z == 1:
                    up = pack_z(tile, place, 1, up)
                else:
                    down = pack_z(tile, place, -1, down)
            value = pltpu.roll(value, 1 if sign_z == 1 else 127, axis=1)
            if name not in ACROSS_YZ:
                value = jnp.where(wide_lane == edge_lane(sign_z), 0.0, value)
        posts[step, SLOT[name], x + 1, LO:HI, :] = value
        if offset[1] != 0:
            line = Y_FACE[sign].index(name) * 4 + x
            post_y[step, SIDE[sign], line] = posts[step, SLOT[name], x + 1, edge : edge + 1, :]
        return up, down

    def collide_body(step, x, packed):
        gradient = gradient_at(step, x)
        squares = [part * part for part in gradient]
        total = squares[0] + squares[1] + squares[2]
        fluid = scalars[0, x + 1, LO:HI, :] > 0.0
        packed = put_post(step, x, ("f", 0), state[0, x], packed, fluid)
        third = total * (1.0 / 3.0)
        for up, down in PAIRS:
            if up < 7:
                surface = (TENSION / 18.0) * (squares[(up - 1) // 2] - third)
            else:
                slope = 0.0
                for axis in range(3):
                    if VELOCITY[up][axis] == 1:
                        slope = slope + gradient[axis]
                    elif VELOCITY[up][axis] == -1:
                        slope = slope - gradient[axis]
                surface = (TENSION / 36.0) * (slope * slope - 2.0 * third)
            packed = put_post(step, x, ("f", up), state[up, x] + surface, packed, fluid)
            packed = put_post(step, x, ("f", down), state[down, x] + surface, packed, fluid)
        red, blue = colour[0, x], colour[1, x]
        mixing = (0.5 * 0.125) * (red * blue / (red + blue)) * lax.rsqrt(jnp.maximum(total, 0.01))
        packed = put_post(step, x, ("r", 0), 0.25 * red, packed, fluid)
        packed = put_post(step, x, ("b", 0), 0.25 * blue, packed, fluid)
        for axis in range(3):
            drift = 0.5 * speed[axis, x]
            across = mixing * gradient[axis]
            for kind, amount, turn in (("r", red, 1.0), ("b", blue, -1.0)):
                mean = 0.125 * amount
                lean = amount * drift + turn * across
                packed = put_post(step, x, (kind, 2 * axis + 1), mean + lean, packed, fluid)
                packed = put_post(step, x, (kind, 2 * axis + 2), mean - lean, packed, fluid)
        return packed

    def state_at(name):
        return {"f": 0, "r": 19, "b": 26}[name[0]] + name[1]

    def opened_at(x, offset):
        dx, dy, dz = offset
        return shifted_scalars[dz][0, x + 1 - dx, LO - dy : HI - dy, :] > 0.0

    def bounced_at(step, x, name):
        back = (name[0], OPPOSITE[name[1]])
        if VELOCITY[name[1]][2] != 0:
            return unrolled[UNROLLED[back], x]
        return posts[step, SLOT[back], x + 1, LO:HI, :]

    def stream_inside(step, x, end, last):
        fluid = scalars[0, x + 1, LO:HI, :] > 0.0
        names = [name for name in EVERY if (last or name[0] == "f") and name not in ACROSS_YZ]
        for name in names:
            dx, dy, dz = VELOCITY[name[1]]
            if name[1] == 0:
                value = posts[step, SLOT[name], x + 1, LO:HI, :]
            else:
                if dx != 0 and dx == end:
                    arriving = 0.0
                else:
                    arriving = posts[step, SLOT[name], x + 1 - dx, LO - dy : HI - dy, :]
                value = jnp.where(opened_at(x, (dx, dy, dz)), arriving, bounced_at(step, x, name))
            state[state_at(name), x] = jnp.where(fluid, value, 0.0) if last else value

    def stream_across(step, x, last):
        fluid = scalars[0, x + 1, LO:HI, :] > 0.0
        for name in ACROSS_YZ:
            dx, dy, dz = VELOCITY[name[1]]
            arriving = posts[step, SLOT[name], x + 1, LO - dy : HI - dy, :]
            value = jnp.where(opened_at(x, (dx, dy, dz)), arriving, bounced_at(step, x, name))
            state[state_at(name), x] = jnp.where(fluid, value, 0.0) if last else value

    def add_arrived(step, last):
        def wanted(name):
            return last or name[0] == "f"

        def kept(x, rows, value):
            if not last:
                return value
            return jnp.where(scalars[0, x + 1, LO + rows.start : LO + rows.stop, :] > 0.0, value, 0.0)

        def z_columns(name, dx, column, half):
            dz = VELOCITY[name[1]][2]
            place = Z_FACE[dz].index(name) * 8 + 2 * column + half
            face = post_z_got[step, SIDE[dz], TURN[dx]]
            return jnp.where(lane == edge_lane(dz), unpack_z(face, place, dz), 0.0)

        for dx, end, ghost, column, names in ((1, 0, 0, NX - 1, X_UP), (-1, NX - 1, NX + 1, 0, X_DOWN)):
            for name in names:
                if not wanted(name):
                    continue
                _, dy, dz = VELOCITY[name[1]]
                if dy != 0:
                    row_ghost = LO - 1 if dy == 1 else HI
                    line = post_y_got[step, SIDE[dy], ROWS_Y + ROWS_XY * SIDE[dx]]
                    posts[step, SLOT[name], ghost, row_ghost : row_ghost + 1, :] = line
                for half in range(2):
                    rows = slice(8 * half, 8 * half + 8)
                    first = LO + 8 * half - dy
                    value = posts[step, SLOT[name], ghost, first : first + 8, :]
                    if dz != 0:
                        value = value + z_columns(name, dx, column, half)
                    state[state_at(name), end, rows, :] = state[state_at(name), end, rows, :] + kept(end, rows, value)
        for dz in (1, -1):
            for name in Z_FACE[dz]:
                if name in ACROSS_YZ or not wanted(name):
                    continue
                for x in range(NX):
                    source = x - VELOCITY[name[1]][0]
                    if not 0 <= source < NX:
                        continue
                    for half in range(2):
                        rows = slice(8 * half, 8 * half + 8)
                        value = kept(x, rows, z_columns(name, 0, source, half))
                        state[state_at(name), x, rows, :] = state[state_at(name), x, rows, :] + value
        for dy, edge in ((1, 0), (-1, NY - 1)):
            rows = slice(edge, edge + 1)
            for entry, name in enumerate(Y_FACE[dy]):
                if name in ACROSS_YZ or not wanted(name):
                    continue
                for x in range(NX):
                    source = x - VELOCITY[name[1]][0]
                    if not 0 <= source < NX:
                        continue
                    value = kept(x, rows, post_y_got[step, SIDE[dy], entry * 4 + source])
                    state[state_at(name), x, rows, :] = state[state_at(name), x, rows, :] + value
        for name in ACROSS_YZ:
            _, dy, dz = VELOCITY[name[1]]
            entry, entry_z = Y_FACE[dy].index(name), Z_FACE[dz].index(name)
            half_y = 1 if dy == 1 else 0
            ghost = LO - 1 if dy == 1 else HI
            for x in range(NX):
                for half in range(2):
                    rows = slice(LO + 8 * half, LO + 8 * half + 8)
                    place = entry_z * 8 + 2 * x + half
                    face = post_z_got[step, SIDE[dz], 0]
                    posts[step, SLOT[name], x + 1, rows, :] = jnp.where(
                        lane == edge_lane(dz), unpack_z(face, place, dz), posts[step, SLOT[name], x + 1, rows, :]
                    )
                corner = unpack_z(post_row_got[step, SIDE[dy], SIDE[dz], 0], entry_z * 8 + 2 * x + half_y, dz)
                line = jnp.where(row_lane == edge_lane(dz), corner, post_y_got[step, SIDE[dy], entry * 4 + x])
                posts[step, SLOT[name], x + 1, ghost : ghost + 1, :] = line

    shifted_scalars = {0: scalars, 1: scalars_down, -1: scalars_up}

    def add_up(step, packed):
        up, down = packed
        for x in range(NX):
            for place, kind in enumerate(("r", "b")):
                total = posts[step, SLOT[(kind, 0)], x + 1, LO:HI, :]
                for number in range(1, 7):
                    dx, dy, dz = VELOCITY[number]
                    plane = x + 1 - dx
                    opened = shifted_scalars[dz][0, plane, LO - dy : HI - dy, :] > 0.0
                    back = (kind, OPPOSITE[number])
                    if dz != 0:
                        bounced = unrolled[UNROLLED[back], x]
                    else:
                        bounced = posts[step, SLOT[back], x + 1, LO:HI, :]
                    if 1 <= plane <= NX:
                        arriving = posts[step, SLOT[(kind, number)], plane, LO - dy : HI - dy, :]
                    else:
                        arriving = 0.0
                    total = total + jnp.where(opened, arriving, bounced)
                partial[place, x] = total
                for half in range(2):
                    tile = total[8 * half : 8 * half + 8]
                    lanes = SUM_Z + 8 * place + 2 * x + half
                    up, down = pack_z(tile, lanes, 1, up), pack_z(tile, lanes, -1, down)
                for dx, end in ((1, NX - 1), (-1, 0)):
                    if x == end:
                        post_part[step, SIDE[dx], NY * place : NY * place + NY, :] = total
                for dy, edge in ((1, NY - 1), (-1, 0)):
                    post_y[step, SIDE[dy], SUM_Y + 4 * place + x] = partial[place, x, edge : edge + 1, :]
                for dy, half in ((1, 1), (-1, 0)):
                    rows = slice(LO + 8 * half, LO + 8 * half + 8)
                    tile = posts[step, SLOT[(kind, FACE[(1, dy)])], x + 1, rows, :]
                    lanes = Y_Z + 8 * place + 2 * x + (0 if dy == 1 else 1)
                    up, down = pack_z(tile, lanes, 1, up), pack_z(tile, lanes, -1, down)
        for place, kind in enumerate(("r", "b")):
            for dx, end in ((1, NX - 1), (-1, 0)):
                slot = SLOT[(kind, FACE[(0, dx)])]
                for half in range(2):
                    tile = posts[step, slot, end + 1, LO + 8 * half : LO + 8 * half + 8, :]
                    lanes = X_Z + 8 * place + (0 if dx == 1 else 6) + half
                    up, down = pack_z(tile, lanes, 1, up), pack_z(tile, lanes, -1, down)
                for dy, edge in ((1, HI - 1), (-1, LO)):
                    line = posts[step, slot, end + 1, edge : edge + 1, :]
                    post_y[step, SIDE[dy], X_Y + 2 * SIDE[dx] + place] = line
                    post_xy[step, SIDE[dx], SIDE[dy], X_XY + place] = line
                    post_xy[step, SIDE[dx], SIDE[dy], SUM_XY + place] = partial[place, end, edge - LO : edge - LO + 1, :]
                    line = posts[step, SLOT[(kind, FACE[(1, dy)])], end + 1, edge : edge + 1, :]
                    post_xy[step, SIDE[dx], SIDE[dy], Y_XY + place] = line
                    part = Y_PART + 2 * SIDE[dy] + place
                    post_part[step, SIDE[dx], part : part + 1, :] = line
        return up, down

    def put_edges(step, packed, fused):
        for dx, end in ((1, NX - 1), (-1, 0)):
            for dy, edge in ((1, HI - 1), (-1, LO)):
                slot = SLOT[("f", VELOCITY.index((dx, dy, 0)))]
                post_xy[step, SIDE[dx], SIDE[dy], 0] = posts[step, slot, end + 1, edge : edge + 1, :]
            if fused:
                post_part[step, SIDE[dx], Z_PART : Z_PART + 8, :] = packed[0]
                post_part[step, SIDE[dx], Z_PART + 8 : Z_PART + 16, :] = packed[1]
        for dz in (1, -1):
            post_z[step, SIDE[dz]] = packed[SIDE[dz]]
            for dy, edge in ((1, 7), (-1, 0)):
                line = post_z[step, SIDE[dz], edge : edge + 1, :]
                post_row[step, SIDE[dy], SIDE[dz]] = line
                if fused:
                    post_y[step, SIDE[dy], Z_Y + SIDE[dz]] = line

    def turned(value, lanes):
        return pltpu.roll(value, 128 - lanes, axis=1)

    def ratio(red, blue):
        return (red - blue) / (red + blue)

    def packed_ratio(sums):
        blue = turned(sums, 8)
        return ratio(sums, blue)

    def finish_phase(step):
        here_ = step + 2

        def put(target, entry, plane, rows, value):
            fluid = shifted_scalars[target][0, plane, rows, :] > 0.0
            shifted_scalars[target][entry, plane, rows, :] = jnp.where(fluid, value, WETTING)

        interior = slice(LO, HI)
        z_got = {(dx, dz): post_z_got[step, SIDE[dz], TURN[dx]] for dx in (-1, 0, 1) for dz in (1, -1)}
        row_got = {
            (dx, dy, dz): post_row_got[step, SIDE[dy], SIDE[dz], TURN[dx]]
            for dx in (-1, 0, 1)
            for dy in (1, -1)
            for dz in (1, -1)
        }

        def xy_got(dx, dy, line):
            return post_y_got[step, SIDE[dy], ROWS_Y + ROWS_XY * SIDE[dx] + line]

        def with_columns(value, place, column, dx):
            halves = []
            for half in range(2):
                tile = value[8 * half : 8 * half + 8]
                for dz in (1, -1):
                    lanes = IN_Z + 8 * place + 2 * column + half
                    tile = tile + jnp.where(lane == edge_lane(dz), unpack_z(z_got[(dx, dz)], lanes, dz), 0.0)
                halves.append(tile)
            return jnp.concatenate(halves, axis=0)

        def with_rows(value, rows):
            for dy, edge in ((1, 0), (-1, NY - 1)):
                value = value + jnp.where(wide_row == edge, rows[dy], 0.0)
            return value

        def with_ends(line, offset, place, x):
            dx, dy = offset
            half = 1 if dy == 1 else 0
            for dz in (1, -1):
                lanes = IN_Z + 8 * place + 2 * x + half
                line = line + jnp.where(row_lane == edge_lane(dz), unpack_z(row_got[(dx, dy, dz)], lanes, dz), 0.0)
            return line

        for x in range(NX):
            sums = []
            for place, kind in enumerate(("r", "b")):
                total = partial[place, x]
                for dx, end, ghost in ((1, 0, 0), (-1, NX - 1, NX + 1)):
                    if x == end:
                        total = total + posts[step, SLOT[(kind, FACE[(0, dx)])], ghost, interior, :]
                rows = {}
                for dy in (1, -1):
                    entry = Y_FACE[dy].index((kind, FACE[(1, dy)]))
                    rows[dy] = post_y_got[step, SIDE[dy], entry * 4 + x]
                total = with_columns(with_rows(total, rows), place, x, 0)
                colour[place, x] = total
                sums.append(total)
            put(0, here_, x + 1, interior, ratio(*sums))
        for dx, ghost, end, column in ((1, 0, 0, NX - 1), (-1, NX + 1, NX - 1, 0)):
            sums = []
            lines = {1: [], -1: []}
            for place, kind in enumerate(("r", "b")):
                total = post_part_got[step, SIDE[dx], NY * place : NY * place + NY, :]
                total = total + posts[step, SLOT[(kind, FACE[(0, -dx)])], end + 1, interior, :]
                rows = {dy: xy_got(dx, dy, Y_XY + place) for dy in (1, -1)}
                sums.append(with_columns(with_rows(total, rows), place, column, dx))
                for dy in (1, -1):
                    part = Y_PART + 2 * SIDE[-dy] + place
                    line = (
                        xy_got(dx, dy, SUM_XY + place)
                        + post_part_got[step, SIDE[dx], part : part + 1, :]
                        + post_y_got[step, SIDE[dy], X_Y + 2 * SIDE[-dx] + place]
                    )
                    lines[dy].append(with_ends(line, (dx, dy), place, column))
            put(0, here_, ghost, interior, ratio(*sums))
            for dy, row_ghost in ((1, LO - 1), (-1, HI)):
                put(0, here_, ghost, slice(row_ghost, row_ghost + 1), ratio(*lines[dy]))
        for dy, row_ghost, edge in ((1, LO - 1, LO), (-1, HI, HI - 1)):
            for x in range(NX):
                sums = []
                for place, kind in enumerate(("r", "b")):
                    line = post_y_got[step, SIDE[dy], SUM_Y + 4 * place + x]
                    line = line + posts[step, SLOT[(kind, FACE[(1, -dy)])], x + 1, edge : edge + 1, :]
                    for dx, end in ((1, 0), (-1, NX - 1)):
                        if x == end:
                            line = line + xy_got(dx, dy, X_XY + place)
                    sums.append(with_ends(line, (0, dy), place, x))
                put(0, here_, x + 1, slice(row_ghost, row_ghost + 1), ratio(*sums))
        low_x, high_x = lane % 8 < 2, lane % 8 >= 6
        first_y, last_y = (row == 0) & (lane % 2 == 0), (row == 7) & (lane % 2 == 1)
        row_low_x, row_high_x = row_lane % 8 < 2, row_lane % 8 >= 6
        for dz in (1, -1):

            def with_y(sums, dx):
                sums = sums + jnp.where(first_y, turned(row_got[(dx, 1, dz)], Y_Z), 0.0)
                return sums + jnp.where(last_y, turned(row_got[(dx, -1, dz)], Y_Z), 0.0)

            sums = turned(z_got[(0, dz)], SUM_Z) + turned(post_z[step, SIDE[-dz]], IN_Z)
            sums = sums + jnp.where(low_x, turned(z_got[(1, dz)], X_Z), 0.0)
            sums = sums + jnp.where(high_x, turned(z_got[(-1, dz)], X_Z), 0.0)
            faces = {0: packed_ratio(with_y(sums, 0))}
            for dx in (1, -1):
                part = Z_PART + 8 * SIDE[-dz]
                sums = turned(z_got[(dx, dz)], SUM_Z) + turned(z_got[(0, dz)], X_Z)
                sums = sums + turned(post_part_got[step, SIDE[dx], part : part + 8, :], IN_Z)
                faces[dx] = packed_ratio(with_y(sums, dx))
            for plane in range(NX + 2):
                dx, column = {0: (1, NX - 1), NX + 1: (-1, 0)}.get(plane, (0, plane - 1))
                for half in range(2):
                    rows = slice(LO + 8 * half, LO + 8 * half + 8)
                    value = scalars[here_, plane, rows, :]
                    ghost = unpack_z(faces[dx], 2 * column + half, dz)
                    value = jnp.where(lane == edge_lane(dz), ghost, pltpu.roll(value, 1 if dz == 1 else 127, axis=1))
                    put(dz, 1, plane, rows, value)
            for dy, row_ghost in ((1, LO - 1), (-1, HI)):
                half = 1 if dy == 1 else 0
                edge = 0 if dy == 1 else 7
                sums = turned(row_got[(0, dy, dz)], SUM_Z)
                sums = sums + turned(post_y_got[step, SIDE[dy], Z_Y + SIDE[-dz]], IN_Z)
                sums = sums + turned(post_z_got[step, SIDE[dz], 0, edge : edge + 1, :], Y_Z)
                sums = sums + jnp.where(row_low_x, turned(row_got[(1, dy, dz)], X_Z), 0.0)
                sums = sums + jnp.where(row_high_x, turned(row_got[(-1, dy, dz)], X_Z), 0.0)
                corner = packed_ratio(sums)
                for x in range(NX):
                    line = scalars[here_, x + 1, row_ghost : row_ghost + 1, :]
                    line = pltpu.roll(line, 1 if dz == 1 else 127, axis=1)
                    line = jnp.where(row_lane == edge_lane(dz), unpack_z(corner, 2 * x + half, dz), line)
                    put(dz, 1, x + 1, slice(row_ghost, row_ghost + 1), line)

    blank = jnp.zeros((8, NZ), jnp.float32)

    def first_phase(x, packed):
        fluid = 1.0 - solid[x].astype(jnp.float32)
        phase = jnp.where(fluid > 0.0, -0.9 + 1.8 * labels[x].astype(jnp.float32), WETTING)
        return set_phase(x, [fluid, phase], packed)

    for step in range(STEPS):
        for side in range(2):
            post_y_got[step, side] = jnp.zeros((ROWS_Y_ALL, 1, NZ), jnp.float32)
            for other in range(2):
                post_row_got[step, side, other] = jnp.zeros((3, 1, NZ), jnp.float32)
            for turn in range(3):
                post_z_got[step, side, turn] = blank

    barrier = pltpu.get_barrier_semaphore()

    def greet(dy, dz):
        for dx in (0, 1, -1):
            pl.semaphore_signal(barrier, inc=1, device_id=neighbour((dx, dy, dz)), device_id_type=MESH)

    by_class(greet)
    for dx in (1, -1):
        pl.semaphore_signal(barrier, inc=1, device_id=neighbour((dx, 0, 0)), device_id_type=MESH)
    beside_y = 2 - closed[(1, 1)].astype(jnp.int32) - closed[(1, -1)].astype(jnp.int32)
    beside_z = 2 - closed[(2, 1)].astype(jnp.int32) - closed[(2, -1)].astype(jnp.int32)
    beside = 2 + 3 * (beside_y + beside_z) + 3 * beside_y * beside_z

    for step in range(STEPS):
        for side in range(2):
            post_part[step, side, Y_PART : Y_PART + 8, :] = blank
            if step == STEPS - 1:
                post_y[step, side, SUM_Y:ROWS_Y] = jnp.zeros((ROWS_Y - SUM_Y, 1, NZ), jnp.float32)
                for other in range(2):
                    post_xy[step, side, other, Y_XY:ROWS_XY] = jnp.zeros((ROWS_XY - Y_XY, 1, NZ), jnp.float32)
        for name in Y_FACE[1] + Y_FACE[-1]:
            if name not in ACROSS_YZ:
                ghost = LO - 1 if VELOCITY[name[1]][1] == 1 else HI
                for plane in range(1, NX + 1):
                    posts[step, SLOT[name], plane, ghost : ghost + 1, :] = blank[0:1]

    loads[0].wait()
    loads[1].wait()
    packed = lax.fori_loop(0, NX, first_phase, (blank, blank), unroll=True)
    pl.semaphore_wait(barrier, beside)
    send_phase(packed)
    loads[2].wait()
    lax.fori_loop(0, NX, lambda x, _: relax_body(0, x, True), None, unroll=True)
    unpack_phase()

    def move(step, fused):
        packed = (blank, blank)
        packed = lax.fori_loop(0, 2, lambda turn, p: collide_body(step, 3 - 3 * turn, p), packed, unroll=True)
        for dx, near, far in ((1, NX, 0), (-1, 1, NX + 1)):
            send(post_plane(step, dx, near), post_plane(step, dx, far), step + 1, X_CLASS[dx], (dx, 0, 0))
        packed = lax.fori_loop(1, 3, lambda x, p: collide_body(step, x, p), packed, unroll=True)
        if fused:
            packed = add_up(step, packed)
        put_edges(step, packed, fused)
        by_class(functools.partial(send_post_class, step, fused))
        if fused:
            for dx in (1, -1):
                side = SIDE[dx]
                send(post_part.at[step, side], post_part_got.at[step, side], step + 1, PART_CLASS[dx], (dx, 0, 0))
        last = not fused
        stream_inside(step, 0, 1, last)
        lax.fori_loop(1, NX - 1, lambda x, _: stream_inside(step, x, 0, last), None, unroll=True)
        stream_inside(step, NX - 1, -1, last)

        for sems, backward in ((send_sem, False), (recv_sem, True)):
            by_class(
                lambda dy, dz, sems=sems: await_bytes(
                    sems, step + 1, CLASS[(dy, dz)], post_like(step, fused, dy, dz)
                ),
                backward,
            )
            for dx in (1, -1):
                await_bytes(sems, step + 1, X_CLASS[dx], post_plane(step, dx, 0 if dx == 1 else NX + 1))
                if fused:
                    await_bytes(sems, step + 1, PART_CLASS[dx], post_part_got.at[step, SIDE[dx]])
        if fused:
            finish_phase(step)
        add_arrived(step, last)
        lax.fori_loop(0, NX, lambda x, _: stream_across(step, x, last), None, unroll=True)

    def step_body(step, _):
        move(step, True)
        lax.fori_loop(0, NX, lambda x, _: relax_body(step + 1, x, False), None, unroll=True)

    lax.fori_loop(0, STEPS - 1, step_body, None)
    move(STEPS - 1, False)


def hand_out(every, momentum_out, red_out, blue_out, sem):
    copies = []
    first = 0
    for place, target in enumerate((momentum_out, red_out, blue_out)):
        count = target.shape[0]
        copies.append(pltpu.make_async_copy(every.at[pl.ds(first, count)], target, sem.at[place]))
        first += count
    for copy in copies:
        copy.start()
    for copy in copies:
        copy.wait()


def shards(sizes, momentum_sets, labels, solid_mask):
    block = (NX, NY, NZ)
    f32 = jnp.float32
    vmem = lambda *shape, dtype=f32: pltpu.VMEM(shape, dtype)
    every = pl.pallas_call(
        functools.partial(kernel, sizes=sizes),
        out_shape=vmem(33, *block),
        in_specs=[pl.BlockSpec(memory_space=pltpu.HBM)] * 3,
        out_specs=pl.BlockSpec(memory_space=pltpu.VMEM),
        scratch_shapes=[
            vmem(*block, dtype=jnp.int32),
            vmem(*block, dtype=jnp.int32),
            vmem(1 + STEPS, NX + 2, ROWS, NZ),
            vmem(2, NX + 2, ROWS, NZ),
            vmem(2, NX + 2, ROWS, NZ),
            vmem(STEPS, 33, NX + 2, ROWS, NZ),
            vmem(14, *block),
            vmem(3, *block),
            vmem(2, *block),
            vmem(2, 8, 1, NZ),
            vmem(2, 8, NZ),
            vmem(2, 2, 1, NZ),
            vmem(2, 12, 1, NZ),
            vmem(2, 3, 8, NZ),
            vmem(2, 2, 1, NZ),
            vmem(STEPS, 2, ROWS_Y, 1, NZ),
            vmem(STEPS, 2, 8, NZ),
            vmem(STEPS, 2, 2, 1, NZ),
            vmem(STEPS, 2, 2, ROWS_XY, 1, NZ),
            vmem(STEPS, 2, ROWS_PART, NZ),
            vmem(STEPS, 2, ROWS_Y_ALL, 1, NZ),
            vmem(STEPS, 2, 3, 8, NZ),
            vmem(STEPS, 2, 2, 3, 1, NZ),
            vmem(STEPS, 2, ROWS_PART, NZ),
            vmem(2, *block),
            pltpu.SemaphoreType.DMA((3,)),
            pltpu.SemaphoreType.DMA((1 + STEPS, 12)),
            pltpu.SemaphoreType.DMA((1 + STEPS, 12)),
        ],
        compiler_params=pltpu.CompilerParams(
            collective_id=0, has_side_effects=True, vmem_limit_bytes=VMEM_LIMIT
        ),
        cost_estimate=pl.CostEstimate(flops=15_000_000, bytes_accessed=1_800_000, transcendentals=0),
    )(*(pltpu.with_memory_space_constraint(array, pltpu.HBM) for array in (momentum_sets, labels, solid_mask)))
    return pl.pallas_call(
        hand_out,
        out_shape=[jax.ShapeDtypeStruct((count,) + block, f32) for count in (19, 7, 7)],
        in_specs=[pl.BlockSpec(memory_space=pltpu.VMEM)],
        out_specs=[pl.BlockSpec(memory_space=pltpu.HBM)] * 3,
        scratch_shapes=[pltpu.SemaphoreType.DMA((3,))],
        cost_estimate=pl.CostEstimate(flops=0, bytes_accessed=2_200_000, transcendentals=0),
    )(pltpu.with_memory_space_constraint(every, pltpu.VMEM))


def solution(mesh):
    sizes = tuple(mesh.shape[axis] for axis in ("flow", "gy", "gz"))
    split = P("flow", "gy", "gz")
    split_sets = P(None, "flow", "gy", "gz")
    return jax.shard_map(
        functools.partial(shards, sizes),
        mesh=mesh,
        in_specs=(split_sets, split, split),
        out_specs=(split_sets, split_sets, split_sets),
        check_vma=False,
    )
```

```python
import functools

import jax
import jax.numpy as jnp
from jax import lax
from jax.experimental import pallas as pl
from jax.experimental.pallas import tpu as pltpu
from jax.sharding import PartitionSpec as P

STEPS = 3
NX, NY, NZ = 4, 16, 128
LO, HI = 8, 8 + NY
ROWS = 32
WETTING = 0.3
TENSION = 0.05
MESH = pl.DeviceIdType.MESH
VMEM_LIMIT = 40 * 1024 * 1024

VELOCITY = (
    (0, 0, 0),
    (1, 0, 0),
    (-1, 0, 0),
    (0, 1, 0),
    (0, -1, 0),
    (0, 0, 1),
    (0, 0, -1),
    (1, 1, 0),
    (-1, -1, 0),
    (1, -1, 0),
    (-1, 1, 0),
    (1, 0, 1),
    (-1, 0, -1),
    (1, 0, -1),
    (-1, 0, 1),
    (0, 1, 1),
    (0, -1, -1),
    (0, 1, -1),
    (0, -1, 1),
)
OPPOSITE = (0, 2, 1, 4, 3, 6, 5, 8, 7, 10, 9, 12, 11, 14, 13, 16, 15, 18, 17)
PAIRS = ((1, 2), (3, 4), (5, 6), (7, 8), (9, 10), (11, 12), (13, 14), (15, 16), (17, 18))

X_UP = [("f", i) for i in (1, 7, 9, 11, 13)] + [("r", 1), ("b", 1)]
X_DOWN = [("f", i) for i in (2, 8, 10, 12, 14)] + [("r", 2), ("b", 2)]
EVERY = [("f", i) for i in range(19)] + [("r", i) for i in range(7)] + [("b", i) for i in range(7)]
ORDER = X_UP + X_DOWN + [name for name in EVERY if name not in X_UP + X_DOWN]
SLOT = {name: place for place, name in enumerate(ORDER)}
Y_FACE = {
    1: (("f", 3), ("r", 3), ("f", 7), ("f", 10), ("f", 15), ("f", 17), ("b", 3)),
    -1: (("f", 4), ("r", 4), ("f", 9), ("f", 8), ("f", 18), ("f", 16), ("b", 4)),
}
Z_FACE = {
    1: (("f", 5), ("f", 11), ("f", 14), ("f", 15), ("f", 18), ("r", 5), ("b", 5)),
    -1: (("f", 6), ("f", 13), ("f", 12), ("f", 17), ("f", 16), ("r", 6), ("b", 6)),
}
Z_MOVING = Z_FACE[1] + Z_FACE[-1]
UNROLLED = {name: place for place, name in enumerate(Z_MOVING)}
DIRECTIONS = VELOCITY[1:]
CORNERS = tuple((a, b, c) for a in (1, -1) for b in (1, -1) for c in (1, -1))
NEIGHBOURS = DIRECTIONS + CORNERS
SIDE = {1: 0, -1: 1}
TURN = {0: 0, 1: 1, -1: 2}
FACE = {(1, 1): 3, (1, -1): 4, (0, 1): 1, (0, -1): 2, (2, 1): 5, (2, -1): 6}
IN_Z, SUM_Z, X_Z, Y_Z = 40, 56, 72, 88
SUM_Y, X_Y, Z_Y, ROWS_Y = 28, 36, 40, 42
Y_XY, SUM_XY, X_XY, ROWS_XY = 1, 3, 5, 7
ROWS_Y_ALL = ROWS_Y + 2 * ROWS_XY
Y_PART, Z_PART, ROWS_PART = 32, 40, 56
ON_Y, ON_Z = ((1, 0), (-1, 0)), ((0, 1), (0, -1))
ON_YZ = ((1, 1), (1, -1), (-1, 1), (-1, -1))
CLASSES = ON_Y + ON_Z + ON_YZ
CLASS = {way: place for place, way in enumerate(CLASSES)}
X_CLASS = {1: 8, -1: 9}
PART_CLASS = {1: 10, -1: 11}
CORNER_CLASS = {way: 12 + place for place, way in enumerate(ON_YZ)}
ACROSS_YZ = tuple(("f", number) for number in (15, 16, 17, 18))


def kernel(
    momentum_in,
    labels_in,
    solid_in,
    state,
    labels,
    solid,
    scalars,
    scalars_down,
    scalars_up,
    posts,
    unrolled,
    speed,
    colour,
    phase_y,
    phase_z,
    phase_yz,
    phase_y_got,
    phase_z_got,
    phase_yz_got,
    post_y,
    post_z,
    post_row,
    post_xy,
    post_part,
    post_y_got,
    post_z_got,
    post_row_got,
    post_part_got,
    partial,
    in_sem,
    send_sem,
    recv_sem,
    *,
    sizes,
):
    here = tuple(lax.axis_index(axis) for axis in ("flow", "gy", "gz"))

    flow = {
        0: here[0],
        1: jnp.where(here[0] == sizes[0] - 1, 0, here[0] + 1),
        -1: jnp.where(here[0] == 0, sizes[0] - 1, here[0] - 1),
    }
    lateral = [{0: here[axis], 1: here[axis] + 1, -1: here[axis] - 1} for axis in (1, 2)]

    def neighbour(offset):
        return (flow[offset[0]], lateral[0][offset[1]], lateral[1][offset[2]])

    closed = {
        (1, -1): here[1] == 0,
        (1, 1): here[1] == sizes[1] - 1,
        (2, -1): here[2] == 0,
        (2, 1): here[2] == sizes[2] - 1,
    }
    def has(offset):
        known = [jnp.logical_not(closed[(axis, offset[axis])]) for axis in (1, 2) if offset[axis] != 0]
        return functools.reduce(jnp.logical_and, known) if known else None

    def when(condition, action):
        if condition is None:
            action()
        else:
            pl.when(condition)(action)

    def by_class(action, backward=False, classes=CLASSES):
        for dy, dz in classes:
            when(has((0, -dy, -dz) if backward else (0, dy, dz)), functools.partial(action, dy, dz))

    lane = lax.broadcasted_iota(jnp.int32, (8, NZ), 1)
    wide_lane = lax.broadcasted_iota(jnp.int32, (NY, NZ), 1)
    wide_row = lax.broadcasted_iota(jnp.int32, (NY, NZ), 0)
    row = lax.broadcasted_iota(jnp.int32, (8, NZ), 0)
    row_lane = lax.broadcasted_iota(jnp.int32, (1, NZ), 1)

    loads = [
        pltpu.make_async_copy(solid_in, solid, in_sem.at[0]),
        pltpu.make_async_copy(labels_in, labels, in_sem.at[1]),
        pltpu.make_async_copy(momentum_in, state.at[pl.ds(0, 19)], in_sem.at[2]),
    ]
    for load in loads:
        load.start()

    def send(source, target, turn, place, offset):
        pltpu.make_async_remote_copy(
            src_ref=source,
            dst_ref=target,
            send_sem=send_sem.at[turn, place],
            recv_sem=recv_sem.at[turn, place],
            device_id=neighbour(offset),
            device_id_type=MESH,
        ).start()

    def await_bytes(sems, turn, place, like):
        pltpu.make_async_copy(like, like, sems.at[turn, place]).wait()

    def send_phase_class(dy, dz):
        place = CLASS[(dy, dz)]
        if dz == 0:
            side = SIDE[dy]
            send(phase_y.at[side], phase_y_got.at[side, pl.ds(0, 8)], 0, place, (0, dy, 0))
            for dx, line, target in ((1, 6, 8), (-1, 0, 10)):
                source = phase_y.at[side, pl.ds(line, 2)]
                send(source, phase_y_got.at[side, pl.ds(target, 2)], 0, place, (dx, dy, 0))
        elif dy == 0:
            side = SIDE[dz]
            for dx in (0, 1, -1):
                send(phase_z.at[side], phase_z_got.at[side, TURN[dx]], 0, place, (dx, 0, dz))
        else:
            sides = SIDE[dy], SIDE[dz]
            send(phase_yz.at[sides], phase_yz_got.at[sides], 0, place, (0, dy, dz))

    def phase_like(dy, dz):
        if dz == 0:
            return phase_y_got.at[SIDE[dy]]
        if dy == 0:
            return phase_z_got.at[SIDE[dz]]
        return phase_yz_got.at[SIDE[dy], SIDE[dz]]

    def phase_plane(plane):
        return scalars.at[pl.ds(0, 2), plane, pl.ds(LO, NY)]

    def post_plane(step, dx, plane):
        return posts.at[step, pl.ds(0 if dx == 1 else 7, 7), plane, pl.ds(LO, NY)]

    def send_post_class(step, dy, dz):
        turn, place = step + 1, CLASS[(dy, dz)]
        if dz == 0:
            side = SIDE[dy]
            send(post_y.at[step, side], post_y_got.at[step, side, pl.ds(0, ROWS_Y)], turn, place, (0, dy, 0))
            for dx in (1, -1):
                target = post_y_got.at[step, side, pl.ds(ROWS_Y + ROWS_XY * SIDE[dx], ROWS_XY)]
                send(post_xy.at[step, SIDE[dx], side], target, turn, place, (dx, dy, 0))
        elif dy == 0:
            side = SIDE[dz]
            for dx in (0, 1, -1):
                send(post_z.at[step, side], post_z_got.at[step, side, TURN[dx]], turn, place, (dx, 0, dz))
        else:
            sides = SIDE[dy], SIDE[dz]
            target = post_row_got.at[step, sides[0], sides[1], pl.ds(0, 1)]
            send(post_row.at[step, sides[0], sides[1]], target, turn, place, (0, dy, dz))

    def send_corner_class(step, dy, dz):
        sides = SIDE[dy], SIDE[dz]
        for dx in (1, -1):
            target = post_row_got.at[step, sides[0], sides[1], pl.ds(TURN[dx], 1)]
            send(post_row.at[step, sides[0], sides[1]], target, step + 1, CORNER_CLASS[(dy, dz)], (dx, dy, dz))

    def post_like(step, dy, dz):
        if dz == 0:
            return post_y_got.at[step, SIDE[dy]]
        if dy == 0:
            return post_z_got.at[step, SIDE[dz]]
        return post_row_got.at[step, SIDE[dy], SIDE[dz], pl.ds(0, 1)]

    def corner_like(step, dy, dz):
        return post_row_got.at[step, SIDE[dy], SIDE[dz], pl.ds(1, 2)]

    def await_posts(sems, step, classes, backward):
        by_class(
            lambda dy, dz: await_bytes(sems, step + 1, CLASS[(dy, dz)], post_like(step, dy, dz)), backward, classes
        )

    def await_corners(sems, step, backward):
        by_class(
            lambda dy, dz: await_bytes(sems, step + 1, CORNER_CLASS[(dy, dz)], corner_like(step, dy, dz)),
            backward,
            ON_YZ,
        )

    def await_x(sems, step, fused):
        for dx in (1, -1):
            await_bytes(sems, step + 1, X_CLASS[dx], post_plane(step, dx, 0 if dx == 1 else NX + 1))
            if fused:
                await_bytes(sems, step + 1, PART_CLASS[dx], post_part_got.at[step, SIDE[dx]])

    def pack_z(tile, place, sign, packed):
        moved = pltpu.roll(tile, place + 1 if sign == 1 else place, axis=1)
        return jnp.where(lane == place, moved, packed)

    def unpack_z(packed, place, sign):
        return pltpu.roll(packed, (128 - place) % 128 if sign == 1 else 127 - place, axis=1)

    def edge_lane(sign):
        return 0 if sign == 1 else NZ - 1

    def set_phase(x, values, packed):
        up, down = packed
        for entry, value in enumerate(values):
            scalars[entry, x + 1, LO:HI, :] = value
            for dy, edge in ((1, HI - 1), (-1, LO)):
                phase_y[SIDE[dy], x * 2 + entry] = scalars[entry, x + 1, edge : edge + 1, :]
            for half in range(2):
                tile = value[8 * half : 8 * half + 8]
                place = entry * 8 + 2 * x + half
                up = pack_z(tile, place, 1, up)
                down = pack_z(tile, place, -1, down)
        return up, down

    def send_phase(packed):
        for dz in (1, -1):
            phase_z[SIDE[dz]] = packed[SIDE[dz]]
            for dy, edge in ((1, 7), (-1, 0)):
                phase_yz[SIDE[dy], SIDE[dz]] = phase_z[SIDE[dz], edge : edge + 1, :]
        by_class(send_phase_class)
        for dx, near, far in ((1, NX, 0), (-1, 1, NX + 1)):
            send(phase_plane(near), phase_plane(far), 0, X_CLASS[dx], (dx, 0, 0))

    def unpack_phase():
        first, count = 0, 2
        fills = (0.0, WETTING)
        shifted = {1: scalars_down, -1: scalars_up}

        def place_of(entry):
            return entry

        def cover(offset, value, fill):
            for axis in (1, 2):
                if offset[axis] != 0:
                    value = jnp.where(closed[(axis, -offset[axis])], fill, value)
            return value

        def arrive(sems, backward):
            by_class(lambda dy, dz: await_bytes(sems, 0, CLASS[(dy, dz)], phase_like(dy, dz)), backward)
            for dx in (1, -1):
                await_bytes(sems, 0, X_CLASS[dx], phase_plane(0))

        def shift_plane(entry, plane, dz, face, column):
            for half in range(2):
                rows = slice(LO + 8 * half, LO + 8 * half + 8)
                value = scalars[first + entry, plane, rows, :]
                place = entry * 8 + 2 * column + half
                ghost = cover((0, 0, dz), unpack_z(face, place, dz), fills[entry])
                shifted[dz][place_of(entry), plane, rows, :] = jnp.where(
                    lane == edge_lane(dz), ghost, pltpu.roll(value, 1 if dz == 1 else 127, axis=1)
                )

        arrive(send_sem, False)
        arrive(recv_sem, True)
        for dz in (1, -1):
            face = phase_z_got[SIDE[dz], 0]
            for entry in range(count):
                for x in range(NX):
                    shift_plane(entry, x + 1, dz, face, x)
        for dy, ghost in ((1, LO - 1), (-1, HI)):
            half = 1 if dy == 1 else 0
            for entry in range(count):
                for x in range(NX):
                    line = cover((0, dy, 0), phase_y_got[SIDE[dy], x * count + entry], fills[entry])
                    scalars[first + entry, x + 1, ghost : ghost + 1, :] = line
                    for dz in (1, -1):
                        corner = phase_yz_got[SIDE[dy], SIDE[dz]]
                        place = entry * 8 + 2 * x + half
                        corner = cover((0, dy, dz), unpack_z(corner, place, dz), fills[entry])
                        shifted[dz][place_of(entry), x + 1, ghost : ghost + 1, :] = jnp.where(
                            row_lane == edge_lane(dz), corner, pltpu.roll(line, 1 if dz == 1 else 127, axis=1)
                        )
        for dx, plane, column in ((1, 0, NX - 1), (-1, NX + 1, 0)):
            for dy, ghost in ((1, LO - 1), (-1, HI)):
                for entry in range(count):
                    line = phase_y_got[SIDE[dy], 8 + 2 * SIDE[dx] + entry]
                    scalars[first + entry, plane, ghost : ghost + 1, :] = cover((0, dy, 0), line, fills[entry])
            for dz in (1, -1):
                for entry in range(count):
                    shift_plane(entry, plane, dz, phase_z_got[SIDE[dz], TURN[dx]], column)

    def relax_body(step, x, initial):
        total = state[0, x]
        flux = [0.0, 0.0, 0.0]
        for up, down in PAIRS:
            first, second = state[up, x], state[down, x]
            total = total + (first + second)
            difference = first - second
            for axis in range(3):
                if VELOCITY[up][axis] == 1:
                    flux[axis] = flux[axis] + difference
                elif VELOCITY[up][axis] == -1:
                    flux[axis] = flux[axis] - difference
        inverse = 1.0 / total
        velocity = [part * inverse for part in flux]
        phase = scalars[step + 1, x + 1, LO:HI, :]
        tau = 1.3 - 0.3 * phase
        rate = 1.0 / tau
        keep = 1.0 - rate
        for axis in range(3):
            speed[axis, x] = velocity[axis]
        if initial:
            red = total * (0.05 + 0.9 * labels[x].astype(jnp.float32))
            blue = total - red
            colour[0, x] = red
            colour[1, x] = blue
        shifted = [velocity[0] + tau * inverse * 0.001, velocity[1], velocity[2]]
        square = shifted[0] * shifted[0] + shifted[1] * shifted[1] + shifted[2] * shifted[2]
        scale = rate * total
        base = scale * (1.0 - 1.5 * square)
        state[0, x] = keep * state[0, x] + base * (1.0 / 3.0)
        face, edge = base * (1.0 / 18.0), base * (1.0 / 36.0)
        for up, down in PAIRS:
            along = 0.0
            for axis in range(3):
                if VELOCITY[up][axis] == 1:
                    along = along + shifted[axis]
                elif VELOCITY[up][axis] == -1:
                    along = along - shifted[axis]
            push = scale * along
            if up < 7:
                even, odd = face + 0.25 * (push * along), push * (1.0 / 6.0)
            else:
                even, odd = edge + 0.125 * (push * along), push * (1.0 / 12.0)
            state[up, x] = keep * state[up, x] + (even + odd)
            state[down, x] = keep * state[down, x] + (even - odd)

    def gradient_at(step, x):
        def at(buffer, place, plane, dy):
            return buffer[place, plane, LO + dy : HI + dy, :]

        here_ = step + 1

        def spread(plane):
            return (
                2.0 * at(scalars, here_, plane, 0)
                + (at(scalars, here_, plane, 1) + at(scalars, here_, plane, -1))
                + (at(scalars_up, 1, plane, 0) + at(scalars_down, 1, plane, 0))
            )

        def slope_y(plane):
            return at(scalars, here_, plane, 1) - at(scalars, here_, plane, -1)

        def slope_z(plane):
            return at(scalars_up, 1, plane, 0) - at(scalars_down, 1, plane, 0)

        low, mid, high = x, x + 1, x + 2
        up_up, up_down = at(scalars_up, 1, mid, 1), at(scalars_up, 1, mid, -1)
        down_up, down_down = at(scalars_down, 1, mid, 1), at(scalars_down, 1, mid, -1)
        along_x = spread(high) - spread(low)
        along_y = 2.0 * slope_y(mid) + (slope_y(high) + slope_y(low)) + ((up_up - up_down) + (down_up - down_down))
        along_z = 2.0 * slope_z(mid) + (slope_z(high) + slope_z(low)) + ((up_up - down_up) + (up_down - down_down))
        return [part * (1.0 / 12.0) for part in (along_x, along_y, along_z)]

    def put_post(step, x, name, value, packed, fluid=None):
        kind, number = name
        offset = VELOCITY[number]
        value = jnp.where(fluid, value, 0.0)
        if offset[1] != 0:
            sign = offset[1]
            edge = HI - 1 if sign == 1 else LO
        up, down = packed
        if offset[2] != 0:
            unrolled[UNROLLED[name], x] = value
            sign_z = offset[2]
            first = Z_FACE[sign_z].index(name) * 8
            for half in range(2):
                tile = value[8 * half : 8 * half + 8]
                place = first + 2 * x + half
                if sign_z == 1:
                    up = pack_z(tile, place, 1, up)
                else:
                    down = pack_z(tile, place, -1, down)
            value = pltpu.roll(value, 1 if sign_z == 1 else 127, axis=1)
            if name not in ACROSS_YZ:
                value = jnp.where(wide_lane == edge_lane(sign_z), 0.0, value)
        posts[step, SLOT[name], x + 1, LO:HI, :] = value
        if offset[1] != 0:
            line = Y_FACE[sign].index(name) * 4 + x
            post_y[step, SIDE[sign], line] = posts[step, SLOT[name], x + 1, edge : edge + 1, :]
        return up, down

    def collide_body(step, x, packed):
        gradient = gradient_at(step, x)
        squares = [part * part for part in gradient]
        total = squares[0] + squares[1] + squares[2]
        fluid = scalars[0, x + 1, LO:HI, :] > 0.0
        packed = put_post(step, x, ("f", 0), state[0, x], packed, fluid)
        third = total * (1.0 / 3.0)
        for up, down in PAIRS:
            if up < 7:
                surface = (TENSION / 18.0) * (squares[(up - 1) // 2] - third)
            else:
                slope = 0.0
                for axis in range(3):
                    if VELOCITY[up][axis] == 1:
                        slope = slope + gradient[axis]
                    elif VELOCITY[up][axis] == -1:
                        slope = slope - gradient[axis]
                surface = (TENSION / 36.0) * (slope * slope - 2.0 * third)
            packed = put_post(step, x, ("f", up), state[up, x] + surface, packed, fluid)
            packed = put_post(step, x, ("f", down), state[down, x] + surface, packed, fluid)
        red, blue = colour[0, x], colour[1, x]
        mixing = (0.5 * 0.125) * (red * blue / (red + blue)) * lax.rsqrt(jnp.maximum(total, 0.01))
        packed = put_post(step, x, ("r", 0), 0.25 * red, packed, fluid)
        packed = put_post(step, x, ("b", 0), 0.25 * blue, packed, fluid)
        for axis in range(3):
            drift = 0.5 * speed[axis, x]
            across = mixing * gradient[axis]
            for kind, amount, turn in (("r", red, 1.0), ("b", blue, -1.0)):
                mean = 0.125 * amount
                lean = amount * drift + turn * across
                packed = put_post(step, x, (kind, 2 * axis + 1), mean + lean, packed, fluid)
                packed = put_post(step, x, (kind, 2 * axis + 2), mean - lean, packed, fluid)
        return packed

    def state_at(name):
        return {"f": 0, "r": 19, "b": 26}[name[0]] + name[1]

    def opened_at(x, offset):
        dx, dy, dz = offset
        return shifted_scalars[dz][0, x + 1 - dx, LO - dy : HI - dy, :] > 0.0

    def bounced_at(step, x, name):
        back = (name[0], OPPOSITE[name[1]])
        if VELOCITY[name[1]][2] != 0:
            return unrolled[UNROLLED[back], x]
        return posts[step, SLOT[back], x + 1, LO:HI, :]

    def stream_inside(step, x, end, last):
        fluid = scalars[0, x + 1, LO:HI, :] > 0.0
        names = [name for name in EVERY if (last or name[0] == "f") and name not in ACROSS_YZ]
        for name in names:
            dx, dy, dz = VELOCITY[name[1]]
            if name[1] == 0:
                value = posts[step, SLOT[name], x + 1, LO:HI, :]
            else:
                if dx != 0 and dx == end:
                    arriving = 0.0
                else:
                    arriving = posts[step, SLOT[name], x + 1 - dx, LO - dy : HI - dy, :]
                value = jnp.where(opened_at(x, (dx, dy, dz)), arriving, bounced_at(step, x, name))
            state[state_at(name), x] = jnp.where(fluid, value, 0.0) if last else value

    def stream_across(step, x, last):
        fluid = scalars[0, x + 1, LO:HI, :] > 0.0
        for name in ACROSS_YZ:
            dx, dy, dz = VELOCITY[name[1]]
            arriving = posts[step, SLOT[name], x + 1, LO - dy : HI - dy, :]
            value = jnp.where(opened_at(x, (dx, dy, dz)), arriving, bounced_at(step, x, name))
            state[state_at(name), x] = jnp.where(fluid, value, 0.0) if last else value

    def arrivals(step, last):
        def wanted(name):
            return last or name[0] == "f"

        def kept(x, rows, value):
            if not last:
                return value
            return jnp.where(scalars[0, x + 1, LO + rows.start : LO + rows.stop, :] > 0.0, value, 0.0)

        def z_columns(name, dx, column, half):
            dz = VELOCITY[name[1]][2]
            place = Z_FACE[dz].index(name) * 8 + 2 * column + half
            face = post_z_got[step, SIDE[dz], TURN[dx]]
            return jnp.where(lane == edge_lane(dz), unpack_z(face, place, dz), 0.0)

        def add_z():
            for dz in (1, -1):
                for name in Z_FACE[dz]:
                    if name in ACROSS_YZ or not wanted(name):
                        continue
                    for x in range(NX):
                        source = x - VELOCITY[name[1]][0]
                        if not 0 <= source < NX:
                            continue
                        for half in range(2):
                            rows = slice(8 * half, 8 * half + 8)
                            value = kept(x, rows, z_columns(name, 0, source, half))
                            state[state_at(name), x, rows, :] = state[state_at(name), x, rows, :] + value
            for name in ACROSS_YZ:
                dz = VELOCITY[name[1]][2]
                face = post_z_got[step, SIDE[dz], 0]
                for x in range(NX):
                    for half in range(2):
                        rows = slice(LO + 8 * half, LO + 8 * half + 8)
                        place = Z_FACE[dz].index(name) * 8 + 2 * x + half
                        posts[step, SLOT[name], x + 1, rows, :] = jnp.where(
                            lane == edge_lane(dz), unpack_z(face, place, dz), posts[step, SLOT[name], x + 1, rows, :]
                        )

        def add_xy():
            for dx, end, ghost, column, names in ((1, 0, 0, NX - 1, X_UP), (-1, NX - 1, NX + 1, 0, X_DOWN)):
                for name in names:
                    if not wanted(name):
                        continue
                    _, dy, dz = VELOCITY[name[1]]
                    if dy != 0:
                        row_ghost = LO - 1 if dy == 1 else HI
                        line = post_y_got[step, SIDE[dy], ROWS_Y + ROWS_XY * SIDE[dx]]
                        posts[step, SLOT[name], ghost, row_ghost : row_ghost + 1, :] = line
                    for half in range(2):
                        rows = slice(8 * half, 8 * half + 8)
                        first = LO + 8 * half - dy
                        value = posts[step, SLOT[name], ghost, first : first + 8, :]
                        if dz != 0:
                            value = value + z_columns(name, dx, column, half)
                        state[state_at(name), end, rows, :] = state[state_at(name), end, rows, :] + kept(end, rows, value)
            for dy, edge in ((1, 0), (-1, NY - 1)):
                rows = slice(edge, edge + 1)
                for entry, name in enumerate(Y_FACE[dy]):
                    if name in ACROSS_YZ or not wanted(name):
                        continue
                    for x in range(NX):
                        source = x - VELOCITY[name[1]][0]
                        if not 0 <= source < NX:
                            continue
                        value = kept(x, rows, post_y_got[step, SIDE[dy], entry * 4 + source])
                        state[state_at(name), x, rows, :] = state[state_at(name), x, rows, :] + value

        def add_across():
            for name in ACROSS_YZ:
                _, dy, dz = VELOCITY[name[1]]
                entry, entry_z = Y_FACE[dy].index(name), Z_FACE[dz].index(name)
                half = 1 if dy == 1 else 0
                ghost = LO - 1 if dy == 1 else HI
                for x in range(NX):
                    corner = unpack_z(post_row_got[step, SIDE[dy], SIDE[dz], 0], entry_z * 8 + 2 * x + half, dz)
                    line = jnp.where(row_lane == edge_lane(dz), corner, post_y_got[step, SIDE[dy], entry * 4 + x])
                    posts[step, SLOT[name], x + 1, ghost : ghost + 1, :] = line

        return add_z, add_xy, add_across

    shifted_scalars = {0: scalars, 1: scalars_down, -1: scalars_up}

    def add_up(step, packed):
        up, down = packed
        for x in range(NX):
            for place, kind in enumerate(("r", "b")):
                total = posts[step, SLOT[(kind, 0)], x + 1, LO:HI, :]
                for number in range(1, 7):
                    dx, dy, dz = VELOCITY[number]
                    plane = x + 1 - dx
                    opened = shifted_scalars[dz][0, plane, LO - dy : HI - dy, :] > 0.0
                    back = (kind, OPPOSITE[number])
                    if dz != 0:
                        bounced = unrolled[UNROLLED[back], x]
                    else:
                        bounced = posts[step, SLOT[back], x + 1, LO:HI, :]
                    if 1 <= plane <= NX:
                        arriving = posts[step, SLOT[(kind, number)], plane, LO - dy : HI - dy, :]
                    else:
                        arriving = 0.0
                    total = total + jnp.where(opened, arriving, bounced)
                partial[place, x] = total
                for half in range(2):
                    tile = total[8 * half : 8 * half + 8]
                    lanes = SUM_Z + 8 * place + 2 * x + half
                    up, down = pack_z(tile, lanes, 1, up), pack_z(tile, lanes, -1, down)
                for dx, end in ((1, NX - 1), (-1, 0)):
                    if x == end:
                        post_part[step, SIDE[dx], NY * place : NY * place + NY, :] = total
                for dy, edge in ((1, NY - 1), (-1, 0)):
                    post_y[step, SIDE[dy], SUM_Y + 4 * place + x] = partial[place, x, edge : edge + 1, :]
                for dy, half in ((1, 1), (-1, 0)):
                    rows = slice(LO + 8 * half, LO + 8 * half + 8)
                    tile = posts[step, SLOT[(kind, FACE[(1, dy)])], x + 1, rows, :]
                    lanes = Y_Z + 8 * place + 2 * x + (0 if dy == 1 else 1)
                    up, down = pack_z(tile, lanes, 1, up), pack_z(tile, lanes, -1, down)
        for place, kind in enumerate(("r", "b")):
            for dx, end in ((1, NX - 1), (-1, 0)):
                slot = SLOT[(kind, FACE[(0, dx)])]
                for half in range(2):
                    tile = posts[step, slot, end + 1, LO + 8 * half : LO + 8 * half + 8, :]
                    lanes = X_Z + 8 * place + (0 if dx == 1 else 6) + half
                    up, down = pack_z(tile, lanes, 1, up), pack_z(tile, lanes, -1, down)
                for dy, edge in ((1, HI - 1), (-1, LO)):
                    line = posts[step, slot, end + 1, edge : edge + 1, :]
                    post_y[step, SIDE[dy], X_Y + 2 * SIDE[dx] + place] = line
                    post_xy[step, SIDE[dx], SIDE[dy], X_XY + place] = line
                    post_xy[step, SIDE[dx], SIDE[dy], SUM_XY + place] = partial[place, end, edge - LO : edge - LO + 1, :]
                    line = posts[step, SLOT[(kind, FACE[(1, dy)])], end + 1, edge : edge + 1, :]
                    post_xy[step, SIDE[dx], SIDE[dy], Y_XY + place] = line
                    part = Y_PART + 2 * SIDE[dy] + place
                    post_part[step, SIDE[dx], part : part + 1, :] = line
        return up, down

    def put_edges(step, packed, fused):
        for dx, end in ((1, NX - 1), (-1, 0)):
            for dy, edge in ((1, HI - 1), (-1, LO)):
                slot = SLOT[("f", VELOCITY.index((dx, dy, 0)))]
                post_xy[step, SIDE[dx], SIDE[dy], 0] = posts[step, slot, end + 1, edge : edge + 1, :]
            if fused:
                post_part[step, SIDE[dx], Z_PART : Z_PART + 8, :] = packed[0]
                post_part[step, SIDE[dx], Z_PART + 8 : Z_PART + 16, :] = packed[1]
        for dz in (1, -1):
            post_z[step, SIDE[dz]] = packed[SIDE[dz]]
            for dy, edge in ((1, 7), (-1, 0)):
                line = post_z[step, SIDE[dz], edge : edge + 1, :]
                post_row[step, SIDE[dy], SIDE[dz], 0] = line
                if fused:
                    post_y[step, SIDE[dy], Z_Y + SIDE[dz]] = line

    def turned(value, lanes):
        return pltpu.roll(value, 128 - lanes, axis=1)

    def ratio(red, blue):
        return (red - blue) / (red + blue)

    def packed_ratio(sums):
        blue = turned(sums, 8)
        return ratio(sums, blue)

    def finish_phase(step, inside):
        here_ = step + 2

        def put(target, entry, plane, rows, value):
            fluid = shifted_scalars[target][0, plane, rows, :] > 0.0
            shifted_scalars[target][entry, plane, rows, :] = jnp.where(fluid, value, WETTING)

        interior = slice(LO, HI)
        z_got = {(dx, dz): post_z_got[step, SIDE[dz], TURN[dx]] for dx in (-1, 0, 1) for dz in (1, -1)}
        row_got = {
            (dx, dy, dz): post_row_got[step, SIDE[dy], SIDE[dz], TURN[dx]]
            for dx in (() if inside else (-1, 0, 1))
            for dy in (1, -1)
            for dz in (1, -1)
        }

        def xy_got(dx, dy, line):
            return post_y_got[step, SIDE[dy], ROWS_Y + ROWS_XY * SIDE[dx] + line]

        def with_columns(value, place, column, dx):
            halves = []
            for half in range(2):
                tile = value[8 * half : 8 * half + 8]
                for dz in (1, -1):
                    lanes = IN_Z + 8 * place + 2 * column + half
                    tile = tile + jnp.where(lane == edge_lane(dz), unpack_z(z_got[(dx, dz)], lanes, dz), 0.0)
                halves.append(tile)
            return jnp.concatenate(halves, axis=0)

        def with_rows(value, rows):
            for dy, edge in ((1, 0), (-1, NY - 1)):
                value = value + jnp.where(wide_row == edge, rows[dy], 0.0)
            return value

        def with_ends(line, offset, place, x):
            dx, dy = offset
            half = 1 if dy == 1 else 0
            for dz in (1, -1):
                lanes = IN_Z + 8 * place + 2 * x + half
                line = line + jnp.where(row_lane == edge_lane(dz), unpack_z(row_got[(dx, dy, dz)], lanes, dz), 0.0)
            return line

        for x in range(NX) if inside else ():
            sums = []
            for place, kind in enumerate(("r", "b")):
                total = partial[place, x]
                for dx, end, ghost in ((1, 0, 0), (-1, NX - 1, NX + 1)):
                    if x == end:
                        total = total + posts[step, SLOT[(kind, FACE[(0, dx)])], ghost, interior, :]
                rows = {}
                for dy in (1, -1):
                    entry = Y_FACE[dy].index((kind, FACE[(1, dy)]))
                    rows[dy] = post_y_got[step, SIDE[dy], entry * 4 + x]
                total = with_columns(with_rows(total, rows), place, x, 0)
                colour[place, x] = total
                sums.append(total)
            put(0, here_, x + 1, interior, ratio(*sums))
        if inside:
            return
        for dx, ghost, end, column in ((1, 0, 0, NX - 1), (-1, NX + 1, NX - 1, 0)):
            sums = []
            lines = {1: [], -1: []}
            for place, kind in enumerate(("r", "b")):
                total = post_part_got[step, SIDE[dx], NY * place : NY * place + NY, :]
                total = total + posts[step, SLOT[(kind, FACE[(0, -dx)])], end + 1, interior, :]
                rows = {dy: xy_got(dx, dy, Y_XY + place) for dy in (1, -1)}
                sums.append(with_columns(with_rows(total, rows), place, column, dx))
                for dy in (1, -1):
                    part = Y_PART + 2 * SIDE[-dy] + place
                    line = (
                        xy_got(dx, dy, SUM_XY + place)
                        + post_part_got[step, SIDE[dx], part : part + 1, :]
                        + post_y_got[step, SIDE[dy], X_Y + 2 * SIDE[-dx] + place]
                    )
                    lines[dy].append(with_ends(line, (dx, dy), place, column))
            put(0, here_, ghost, interior, ratio(*sums))
            for dy, row_ghost in ((1, LO - 1), (-1, HI)):
                put(0, here_, ghost, slice(row_ghost, row_ghost + 1), ratio(*lines[dy]))
        for dy, row_ghost, edge in ((1, LO - 1, LO), (-1, HI, HI - 1)):
            for x in range(NX):
                sums = []
                for place, kind in enumerate(("r", "b")):
                    line = post_y_got[step, SIDE[dy], SUM_Y + 4 * place + x]
                    line = line + posts[step, SLOT[(kind, FACE[(1, -dy)])], x + 1, edge : edge + 1, :]
                    for dx, end in ((1, 0), (-1, NX - 1)):
                        if x == end:
                            line = line + xy_got(dx, dy, X_XY + place)
                    sums.append(with_ends(line, (0, dy), place, x))
                put(0, here_, x + 1, slice(row_ghost, row_ghost + 1), ratio(*sums))
        low_x, high_x = lane % 8 < 2, lane % 8 >= 6
        first_y, last_y = (row == 0) & (lane % 2 == 0), (row == 7) & (lane % 2 == 1)
        row_low_x, row_high_x = row_lane % 8 < 2, row_lane % 8 >= 6
        for dz in (1, -1):

            def with_y(sums, dx):
                sums = sums + jnp.where(first_y, turned(row_got[(dx, 1, dz)], Y_Z), 0.0)
                return sums + jnp.where(last_y, turned(row_got[(dx, -1, dz)], Y_Z), 0.0)

            sums = turned(z_got[(0, dz)], SUM_Z) + turned(post_z[step, SIDE[-dz]], IN_Z)
            sums = sums + jnp.where(low_x, turned(z_got[(1, dz)], X_Z), 0.0)
            sums = sums + jnp.where(high_x, turned(z_got[(-1, dz)], X_Z), 0.0)
            faces = {0: packed_ratio(with_y(sums, 0))}
            for dx in (1, -1):
                part = Z_PART + 8 * SIDE[-dz]
                sums = turned(z_got[(dx, dz)], SUM_Z) + turned(z_got[(0, dz)], X_Z)
                sums = sums + turned(post_part_got[step, SIDE[dx], part : part + 8, :], IN_Z)
                faces[dx] = packed_ratio(with_y(sums, dx))
            for plane in range(NX + 2):
                dx, column = {0: (1, NX - 1), NX + 1: (-1, 0)}.get(plane, (0, plane - 1))
                for half in range(2):
                    rows = slice(LO + 8 * half, LO + 8 * half + 8)
                    value = scalars[here_, plane, rows, :]
                    ghost = unpack_z(faces[dx], 2 * column + half, dz)
                    value = jnp.where(lane == edge_lane(dz), ghost, pltpu.roll(value, 1 if dz == 1 else 127, axis=1))
                    put(dz, 1, plane, rows, value)
            for dy, row_ghost in ((1, LO - 1), (-1, HI)):
                half = 1 if dy == 1 else 0
                edge = 0 if dy == 1 else 7
                sums = turned(row_got[(0, dy, dz)], SUM_Z)
                sums = sums + turned(post_y_got[step, SIDE[dy], Z_Y + SIDE[-dz]], IN_Z)
                sums = sums + turned(post_z_got[step, SIDE[dz], 0, edge : edge + 1, :], Y_Z)
                sums = sums + jnp.where(row_low_x, turned(row_got[(1, dy, dz)], X_Z), 0.0)
                sums = sums + jnp.where(row_high_x, turned(row_got[(-1, dy, dz)], X_Z), 0.0)
                corner = packed_ratio(sums)
                for x in range(NX):
                    line = scalars[here_, x + 1, row_ghost : row_ghost + 1, :]
                    line = pltpu.roll(line, 1 if dz == 1 else 127, axis=1)
                    line = jnp.where(row_lane == edge_lane(dz), unpack_z(corner, 2 * x + half, dz), line)
                    put(dz, 1, x + 1, slice(row_ghost, row_ghost + 1), line)

    blank = jnp.zeros((8, NZ), jnp.float32)

    def first_phase(x, packed):
        fluid = 1.0 - solid[x].astype(jnp.float32)
        phase = jnp.where(fluid > 0.0, -0.9 + 1.8 * labels[x].astype(jnp.float32), WETTING)
        return set_phase(x, [fluid, phase], packed)

    barrier = pltpu.get_barrier_semaphore()

    def greet(dy, dz):
        for dx in (0, 1, -1):
            pl.semaphore_signal(barrier, inc=1, device_id=neighbour((dx, dy, dz)), device_id_type=MESH)

    by_class(greet)
    for dx in (1, -1):
        pl.semaphore_signal(barrier, inc=1, device_id=neighbour((dx, 0, 0)), device_id_type=MESH)
    beside_y = 2 - closed[(1, 1)].astype(jnp.int32) - closed[(1, -1)].astype(jnp.int32)
    beside_z = 2 - closed[(2, 1)].astype(jnp.int32) - closed[(2, -1)].astype(jnp.int32)
    beside = 2 + 3 * (beside_y + beside_z) + 3 * beside_y * beside_z

    def clear(dy, dz):
        for step in range(STEPS):
            if dz == 0:
                post_y_got[step, SIDE[dy]] = jnp.zeros((ROWS_Y_ALL, 1, NZ), jnp.float32)
            elif dy == 0:
                post_z_got[step, SIDE[dz]] = jnp.zeros((3, 8, NZ), jnp.float32)
            else:
                post_row_got[step, SIDE[dy], SIDE[dz]] = jnp.zeros((3, 1, NZ), jnp.float32)

    for dy, dz in CLASSES:
        pl.when(jnp.logical_not(has((0, -dy, -dz))))(functools.partial(clear, dy, dz))

    for step in range(STEPS):
        for side in range(2):
            post_part[step, side, Y_PART : Y_PART + 8, :] = blank
            if step == STEPS - 1:
                post_y[step, side, SUM_Y:ROWS_Y] = jnp.zeros((ROWS_Y - SUM_Y, 1, NZ), jnp.float32)
                for other in range(2):
                    post_xy[step, side, other, Y_XY:ROWS_XY] = jnp.zeros((ROWS_XY - Y_XY, 1, NZ), jnp.float32)
        for name in Y_FACE[1] + Y_FACE[-1]:
            if name not in ACROSS_YZ:
                ghost = LO - 1 if VELOCITY[name[1]][1] == 1 else HI
                for plane in range(1, NX + 1):
                    posts[step, SLOT[name], plane, ghost : ghost + 1, :] = blank[0:1]

    loads[0].wait()
    loads[1].wait()
    packed = lax.fori_loop(0, NX, first_phase, (blank, blank), unroll=True)
    pl.semaphore_wait(barrier, beside)
    send_phase(packed)
    loads[2].wait()
    lax.fori_loop(0, NX, lambda x, _: relax_body(0, x, True), None, unroll=True)
    unpack_phase()

    def move(step, fused):
        packed = (blank, blank)
        packed = lax.fori_loop(0, 2, lambda turn, p: collide_body(step, 3 - 3 * turn, p), packed, unroll=True)
        for dx, near, far in ((1, NX, 0), (-1, 1, NX + 1)):
            send(post_plane(step, dx, near), post_plane(step, dx, far), step + 1, X_CLASS[dx], (dx, 0, 0))
        packed = lax.fori_loop(1, 3, lambda x, p: collide_body(step, x, p), packed, unroll=True)
        if fused:
            packed = add_up(step, packed)
        put_edges(step, packed, fused)
        by_class(functools.partial(send_post_class, step))
        if fused:
            for dx in (1, -1):
                side = SIDE[dx]
                send(post_part.at[step, side], post_part_got.at[step, side], step + 1, PART_CLASS[dx], (dx, 0, 0))
            by_class(functools.partial(send_corner_class, step), classes=ON_YZ)
        last = not fused
        stream_inside(step, 0, 1, last)
        lax.fori_loop(1, NX - 1, lambda x, _: stream_inside(step, x, 0, last), None, unroll=True)
        stream_inside(step, NX - 1, -1, last)
        await_posts(send_sem, step, CLASSES, False)
        await_x(send_sem, step, fused)
        if fused:
            await_corners(send_sem, step, False)
        add_z, add_xy, add_across = arrivals(step, last)
        await_posts(recv_sem, step, ON_Z, True)
        add_z()
        await_x(recv_sem, step, fused)
        await_posts(recv_sem, step, ON_Y, True)
        add_xy()
        if fused:
            finish_phase(step, True)
        await_posts(recv_sem, step, ON_YZ, True)
        add_across()
        lax.fori_loop(0, NX, lambda x, _: stream_across(step, x, last), None, unroll=True)
        if fused:
            lax.fori_loop(0, NX, lambda x, _: relax_body(step + 1, x, False), None, unroll=True)
            await_corners(recv_sem, step, True)
            finish_phase(step, False)

    def step_body(step, _):
        move(step, True)

    lax.fori_loop(0, STEPS - 1, step_body, None)
    move(STEPS - 1, False)


def hand_out(every, momentum_out, red_out, blue_out, sem):
    copies = []
    first = 0
    for place, target in enumerate((momentum_out, red_out, blue_out)):
        count = target.shape[0]
        copies.append(pltpu.make_async_copy(every.at[pl.ds(first, count)], target, sem.at[place]))
        first += count
    for copy in copies:
        copy.start()
    for copy in copies:
        copy.wait()


def shards(sizes, momentum_sets, labels, solid_mask):
    block = (NX, NY, NZ)
    f32 = jnp.float32
    vmem = lambda *shape, dtype=f32: pltpu.VMEM(shape, dtype)
    every = pl.pallas_call(
        functools.partial(kernel, sizes=sizes),
        out_shape=vmem(33, *block),
        in_specs=[pl.BlockSpec(memory_space=pltpu.HBM)] * 3,
        out_specs=pl.BlockSpec(memory_space=pltpu.VMEM),
        scratch_shapes=[
            vmem(*block, dtype=jnp.int32),
            vmem(*block, dtype=jnp.int32),
            vmem(1 + STEPS, NX + 2, ROWS, NZ),
            vmem(2, NX + 2, ROWS, NZ),
            vmem(2, NX + 2, ROWS, NZ),
            vmem(STEPS, 33, NX + 2, ROWS, NZ),
            vmem(14, *block),
            vmem(3, *block),
            vmem(2, *block),
            vmem(2, 8, 1, NZ),
            vmem(2, 8, NZ),
            vmem(2, 2, 1, NZ),
            vmem(2, 12, 1, NZ),
            vmem(2, 3, 8, NZ),
            vmem(2, 2, 1, NZ),
            vmem(STEPS, 2, ROWS_Y, 1, NZ),
            vmem(STEPS, 2, 8, NZ),
            vmem(STEPS, 2, 2, 1, 1, NZ),
            vmem(STEPS, 2, 2, ROWS_XY, 1, NZ),
            vmem(STEPS, 2, ROWS_PART, NZ),
            vmem(STEPS, 2, ROWS_Y_ALL, 1, NZ),
            vmem(STEPS, 2, 3, 8, NZ),
            vmem(STEPS, 2, 2, 3, 1, NZ),
            vmem(STEPS, 2, ROWS_PART, NZ),
            vmem(2, *block),
            pltpu.SemaphoreType.DMA((3,)),
            pltpu.SemaphoreType.DMA((1 + STEPS, 16)),
            pltpu.SemaphoreType.DMA((1 + STEPS, 16)),
        ],
        compiler_params=pltpu.CompilerParams(
            collective_id=0, has_side_effects=True, vmem_limit_bytes=VMEM_LIMIT
        ),
        cost_estimate=pl.CostEstimate(flops=15_000_000, bytes_accessed=1_800_000, transcendentals=0),
    )(*(pltpu.with_memory_space_constraint(array, pltpu.HBM) for array in (momentum_sets, labels, solid_mask)))
    return pl.pallas_call(
        hand_out,
        out_shape=[jax.ShapeDtypeStruct((count,) + block, f32) for count in (19, 7, 7)],
        in_specs=[pl.BlockSpec(memory_space=pltpu.VMEM)],
        out_specs=[pl.BlockSpec(memory_space=pltpu.HBM)] * 3,
        scratch_shapes=[pltpu.SemaphoreType.DMA((3,))],
        cost_estimate=pl.CostEstimate(flops=0, bytes_accessed=2_200_000, transcendentals=0),
    )(pltpu.with_memory_space_constraint(every, pltpu.VMEM))


def solution(mesh):
    sizes = tuple(mesh.shape[axis] for axis in ("flow", "gy", "gz"))
    split = P("flow", "gy", "gz")
    split_sets = P(None, "flow", "gy", "gz")
    return jax.shard_map(
        functools.partial(shards, sizes),
        mesh=mesh,
        in_specs=(split_sets, split, split),
        out_specs=(split_sets, split_sets, split_sets),
        check_vma=False,
    )
```

```python
import functools

import jax
import jax.numpy as jnp
from jax import lax
from jax.experimental import pallas as pl
from jax.experimental.pallas import tpu as pltpu
from jax.sharding import PartitionSpec as P

STEPS = 3
NX, NY, NZ = 4, 16, 128
LO, HI = 8, 8 + NY
ROWS = 32
WETTING = 0.3
TENSION = 0.05
MESH = pl.DeviceIdType.MESH
VMEM_LIMIT = 40 * 1024 * 1024

VELOCITY = (
    (0, 0, 0),
    (1, 0, 0),
    (-1, 0, 0),
    (0, 1, 0),
    (0, -1, 0),
    (0, 0, 1),
    (0, 0, -1),
    (1, 1, 0),
    (-1, -1, 0),
    (1, -1, 0),
    (-1, 1, 0),
    (1, 0, 1),
    (-1, 0, -1),
    (1, 0, -1),
    (-1, 0, 1),
    (0, 1, 1),
    (0, -1, -1),
    (0, 1, -1),
    (0, -1, 1),
)
OPPOSITE = (0, 2, 1, 4, 3, 6, 5, 8, 7, 10, 9, 12, 11, 14, 13, 16, 15, 18, 17)
PAIRS = ((1, 2), (3, 4), (5, 6), (7, 8), (9, 10), (11, 12), (13, 14), (15, 16), (17, 18))

X_UP = [("f", i) for i in (1, 7, 9, 11, 13)] + [("r", 1), ("b", 1)]
X_DOWN = [("f", i) for i in (2, 8, 10, 12, 14)] + [("r", 2), ("b", 2)]
EVERY = [("f", i) for i in range(19)] + [("r", i) for i in range(7)] + [("b", i) for i in range(7)]
ORDER = X_UP + X_DOWN + [name for name in EVERY if name not in X_UP + X_DOWN]
SLOT = {name: place for place, name in enumerate(ORDER)}
Y_FACE = {
    1: (("f", 3), ("r", 3), ("f", 7), ("f", 10), ("f", 15), ("f", 17), ("b", 3)),
    -1: (("f", 4), ("r", 4), ("f", 9), ("f", 8), ("f", 18), ("f", 16), ("b", 4)),
}
Z_FACE = {
    1: (("f", 5), ("f", 11), ("f", 14), ("f", 15), ("f", 18), ("r", 5), ("b", 5)),
    -1: (("f", 6), ("f", 13), ("f", 12), ("f", 17), ("f", 16), ("r", 6), ("b", 6)),
}
Z_MOVING = Z_FACE[1] + Z_FACE[-1]
UNROLLED = {name: place for place, name in enumerate(Z_MOVING)}
DIRECTIONS = VELOCITY[1:]
CORNERS = tuple((a, b, c) for a in (1, -1) for b in (1, -1) for c in (1, -1))
NEIGHBOURS = DIRECTIONS + CORNERS
SIDE = {1: 0, -1: 1}
TURN = {0: 0, 1: 1, -1: 2}
FACE = {(1, 1): 3, (1, -1): 4, (0, 1): 1, (0, -1): 2, (2, 1): 5, (2, -1): 6}
IN_Z, SUM_Z, X_Z, Y_Z = 40, 56, 72, 88
SUM_Y, X_Y, Z_Y, ROWS_Y = 28, 36, 40, 42
Y_XY, SUM_XY, X_XY, ROWS_XY = 1, 3, 5, 7
ROWS_Y_ALL = ROWS_Y + 2 * ROWS_XY
Y_PART, Z_PART, ROWS_PART = 32, 40, 48
ON_Y, ON_Z = ((1, 0), (-1, 0)), ((0, 1), (0, -1))
ON_YZ = ((1, 1), (1, -1), (-1, 1), (-1, -1))
CLASSES = ON_YZ + ON_Y + ON_Z
CLASS = {way: place for place, way in enumerate(CLASSES)}
X_CLASS = {1: 8, -1: 9}
PART_CLASS = {1: 10, -1: 11}
CORNER_CLASS = {way: 12 + place for place, way in enumerate(ON_YZ)}
ACROSS_YZ = tuple(("f", number) for number in (15, 16, 17, 18))


def kernel(
    momentum_in,
    labels_in,
    solid_in,
    state,
    labels,
    solid,
    scalars,
    scalars_down,
    scalars_up,
    posts,
    unrolled,
    speed,
    colour,
    phase_y,
    phase_z,
    phase_yz,
    phase_y_got,
    phase_z_got,
    phase_yz_got,
    post_y,
    post_z,
    post_row,
    post_xy,
    post_part,
    post_y_got,
    post_z_got,
    post_row_got,
    post_part_got,
    partial,
    in_sem,
    send_sem,
    recv_sem,
    *,
    sizes,
):
    here = tuple(lax.axis_index(axis) for axis in ("flow", "gy", "gz"))

    flow = {
        0: here[0],
        1: jnp.where(here[0] == sizes[0] - 1, 0, here[0] + 1),
        -1: jnp.where(here[0] == 0, sizes[0] - 1, here[0] - 1),
    }
    lateral = [{0: here[axis], 1: here[axis] + 1, -1: here[axis] - 1} for axis in (1, 2)]

    def neighbour(offset):
        return (flow[offset[0]], lateral[0][offset[1]], lateral[1][offset[2]])

    closed = {
        (1, -1): here[1] == 0,
        (1, 1): here[1] == sizes[1] - 1,
        (2, -1): here[2] == 0,
        (2, 1): here[2] == sizes[2] - 1,
    }
    def has(offset):
        known = [jnp.logical_not(closed[(axis, offset[axis])]) for axis in (1, 2) if offset[axis] != 0]
        return functools.reduce(jnp.logical_and, known) if known else None

    def when(condition, action):
        if condition is None:
            action()
        else:
            pl.when(condition)(action)

    def by_class(action, backward=False, classes=CLASSES):
        for dy, dz in classes:
            when(has((0, -dy, -dz) if backward else (0, dy, dz)), functools.partial(action, dy, dz))

    lane = lax.broadcasted_iota(jnp.int32, (8, NZ), 1)
    wide_lane = lax.broadcasted_iota(jnp.int32, (NY, NZ), 1)
    wide_row = lax.broadcasted_iota(jnp.int32, (NY, NZ), 0)
    row = lax.broadcasted_iota(jnp.int32, (8, NZ), 0)
    row_lane = lax.broadcasted_iota(jnp.int32, (1, NZ), 1)

    loads = [
        pltpu.make_async_copy(solid_in, solid, in_sem.at[0]),
        pltpu.make_async_copy(labels_in, labels, in_sem.at[1]),
        pltpu.make_async_copy(momentum_in, state.at[pl.ds(0, 19)], in_sem.at[2]),
    ]
    for load in loads:
        load.start()

    def send(source, target, turn, place, offset):
        pltpu.make_async_remote_copy(
            src_ref=source,
            dst_ref=target,
            send_sem=send_sem.at[turn, place],
            recv_sem=recv_sem.at[turn, place],
            device_id=neighbour(offset),
            device_id_type=MESH,
        ).start()

    def await_bytes(sems, turn, place, like):
        pltpu.make_async_copy(like, like, sems.at[turn, place]).wait()

    def send_phase_class(dy, dz):
        place = CLASS[(dy, dz)]
        if dz == 0:
            side = SIDE[dy]
            send(phase_y.at[side], phase_y_got.at[side, pl.ds(0, 8)], 0, place, (0, dy, 0))
            for dx, line, target in ((1, 6, 8), (-1, 0, 10)):
                source = phase_y.at[side, pl.ds(line, 2)]
                send(source, phase_y_got.at[side, pl.ds(target, 2)], 0, place, (dx, dy, 0))
        elif dy == 0:
            side = SIDE[dz]
            for dx in (0, 1, -1):
                send(phase_z.at[side], phase_z_got.at[side, TURN[dx]], 0, place, (dx, 0, dz))
        else:
            sides = SIDE[dy], SIDE[dz]
            send(phase_yz.at[sides], phase_yz_got.at[sides], 0, place, (0, dy, dz))

    def phase_like(dy, dz):
        if dz == 0:
            return phase_y_got.at[SIDE[dy]]
        if dy == 0:
            return phase_z_got.at[SIDE[dz]]
        return phase_yz_got.at[SIDE[dy], SIDE[dz]]

    def phase_plane(plane):
        return scalars.at[pl.ds(0, 2), plane, pl.ds(LO, NY)]

    def post_plane(step, dx, plane):
        return posts.at[step, pl.ds(0 if dx == 1 else 7, 7), plane, pl.ds(LO, NY)]

    def xy_place(dx, fused):
        return ROWS_Y + ROWS_XY * SIDE[dx] if fused else SUM_Y + SIDE[dx]

    def send_post_class(step, fused, dy, dz):
        turn, place = step + 1, CLASS[(dy, dz)]
        if dz == 0:
            side = SIDE[dy]
            rows, rows_xy = pl.ds(0, ROWS_Y if fused else SUM_Y), ROWS_XY if fused else 1
            send(post_y.at[step, side, rows], post_y_got.at[step, side, rows], turn, place, (0, dy, 0))
            for dx in (1, -1):
                source = post_xy.at[step, SIDE[dx], side, pl.ds(0, rows_xy)]
                target = post_y_got.at[step, side, pl.ds(xy_place(dx, fused), rows_xy)]
                send(source, target, turn, place, (dx, dy, 0))
        elif dy == 0:
            side = SIDE[dz]
            for dx in (0, 1, -1):
                send(post_z.at[step, side], post_z_got.at[step, side, TURN[dx]], turn, place, (dx, 0, dz))
        else:
            sides = SIDE[dy], SIDE[dz]
            target = post_row_got.at[step, sides[0], sides[1], pl.ds(0, 1)]
            send(post_row.at[step, sides[0], sides[1]], target, turn, place, (0, dy, dz))

    def send_corner_class(step, dy, dz):
        sides = SIDE[dy], SIDE[dz]
        for dx in (1, -1):
            target = post_row_got.at[step, sides[0], sides[1], pl.ds(TURN[dx], 1)]
            send(post_row.at[step, sides[0], sides[1]], target, step + 1, CORNER_CLASS[(dy, dz)], (dx, dy, dz))

    def post_like(step, fused, dy, dz):
        if dz == 0:
            return post_y_got.at[step, SIDE[dy], pl.ds(0, ROWS_Y_ALL if fused else SUM_Y + 2)]
        if dy == 0:
            return post_z_got.at[step, SIDE[dz]]
        return post_row_got.at[step, SIDE[dy], SIDE[dz], pl.ds(0, 1)]

    def corner_like(step, dy, dz):
        return post_row_got.at[step, SIDE[dy], SIDE[dz], pl.ds(1, 2)]

    def await_posts(sems, step, fused, classes, backward):
        by_class(
            lambda dy, dz: await_bytes(sems, step + 1, CLASS[(dy, dz)], post_like(step, fused, dy, dz)),
            backward,
            classes,
        )

    def await_corners(sems, step, backward):
        by_class(
            lambda dy, dz: await_bytes(sems, step + 1, CORNER_CLASS[(dy, dz)], corner_like(step, dy, dz)),
            backward,
            ON_YZ,
        )

    def await_x(sems, step):
        for dx in (1, -1):
            await_bytes(sems, step + 1, X_CLASS[dx], post_plane(step, dx, 0 if dx == 1 else NX + 1))

    def await_parts(sems, step):
        for dx in (1, -1):
            await_bytes(sems, step + 1, PART_CLASS[dx], post_part_got.at[step, SIDE[dx]])

    def pack_z(tile, place, sign, packed):
        moved = pltpu.roll(tile, place + 1 if sign == 1 else place, axis=1)
        return jnp.where(lane == place, moved, packed)

    def unpack_z(packed, place, sign):
        return pltpu.roll(packed, (128 - place) % 128 if sign == 1 else 127 - place, axis=1)

    def edge_lane(sign):
        return 0 if sign == 1 else NZ - 1

    def set_phase(x, values, packed):
        up, down = packed
        for entry, value in enumerate(values):
            scalars[entry, x + 1, LO:HI, :] = value
            for dy, edge in ((1, HI - 1), (-1, LO)):
                phase_y[SIDE[dy], x * 2 + entry] = scalars[entry, x + 1, edge : edge + 1, :]
            for half in range(2):
                tile = value[8 * half : 8 * half + 8]
                place = entry * 8 + 2 * x + half
                up = pack_z(tile, place, 1, up)
                down = pack_z(tile, place, -1, down)
        return up, down

    def send_phase(packed):
        for dz in (1, -1):
            phase_z[SIDE[dz]] = packed[SIDE[dz]]
            for dy, edge in ((1, 7), (-1, 0)):
                phase_yz[SIDE[dy], SIDE[dz]] = phase_z[SIDE[dz], edge : edge + 1, :]
        by_class(send_phase_class)
        for dx, near, far in ((1, NX, 0), (-1, 1, NX + 1)):
            send(phase_plane(near), phase_plane(far), 0, X_CLASS[dx], (dx, 0, 0))

    def unpack_phase():
        first, count = 0, 2
        fills = (0.0, WETTING)
        shifted = {1: scalars_down, -1: scalars_up}

        def place_of(entry):
            return entry

        def cover(offset, value, fill):
            for axis in (1, 2):
                if offset[axis] != 0:
                    value = jnp.where(closed[(axis, -offset[axis])], fill, value)
            return value

        def arrive(sems, backward):
            by_class(lambda dy, dz: await_bytes(sems, 0, CLASS[(dy, dz)], phase_like(dy, dz)), backward)
            for dx in (1, -1):
                await_bytes(sems, 0, X_CLASS[dx], phase_plane(0))

        def shift_plane(entry, plane, dz, face, column):
            for half in range(2):
                rows = slice(LO + 8 * half, LO + 8 * half + 8)
                value = scalars[first + entry, plane, rows, :]
                place = entry * 8 + 2 * column + half
                ghost = cover((0, 0, dz), unpack_z(face, place, dz), fills[entry])
                shifted[dz][place_of(entry), plane, rows, :] = jnp.where(
                    lane == edge_lane(dz), ghost, pltpu.roll(value, 1 if dz == 1 else 127, axis=1)
                )

        arrive(send_sem, False)
        arrive(recv_sem, True)
        for dz in (1, -1):
            face = phase_z_got[SIDE[dz], 0]
            for entry in range(count):
                for x in range(NX):
                    shift_plane(entry, x + 1, dz, face, x)
        for dy, ghost in ((1, LO - 1), (-1, HI)):
            half = 1 if dy == 1 else 0
            for entry in range(count):
                for x in range(NX):
                    line = cover((0, dy, 0), phase_y_got[SIDE[dy], x * count + entry], fills[entry])
                    scalars[first + entry, x + 1, ghost : ghost + 1, :] = line
                    for dz in (1, -1):
                        corner = phase_yz_got[SIDE[dy], SIDE[dz]]
                        place = entry * 8 + 2 * x + half
                        corner = cover((0, dy, dz), unpack_z(corner, place, dz), fills[entry])
                        shifted[dz][place_of(entry), x + 1, ghost : ghost + 1, :] = jnp.where(
                            row_lane == edge_lane(dz), corner, pltpu.roll(line, 1 if dz == 1 else 127, axis=1)
                        )
        for dx, plane, column in ((1, 0, NX - 1), (-1, NX + 1, 0)):
            for dy, ghost in ((1, LO - 1), (-1, HI)):
                for entry in range(count):
                    line = phase_y_got[SIDE[dy], 8 + 2 * SIDE[dx] + entry]
                    scalars[first + entry, plane, ghost : ghost + 1, :] = cover((0, dy, 0), line, fills[entry])
            for dz in (1, -1):
                for entry in range(count):
                    shift_plane(entry, plane, dz, phase_z_got[SIDE[dz], TURN[dx]], column)

    def relax_body(step, x, initial):
        total = state[0, x]
        flux = [0.0, 0.0, 0.0]
        for up, down in PAIRS:
            first, second = state[up, x], state[down, x]
            total = total + (first + second)
            difference = first - second
            for axis in range(3):
                if VELOCITY[up][axis] == 1:
                    flux[axis] = flux[axis] + difference
                elif VELOCITY[up][axis] == -1:
                    flux[axis] = flux[axis] - difference
        inverse = 1.0 / total
        velocity = [part * inverse for part in flux]
        phase = scalars[step + 1, x + 1, LO:HI, :]
        tau = 1.3 - 0.3 * phase
        rate = 1.0 / tau
        keep = 1.0 - rate
        for axis in range(3):
            speed[axis, x] = velocity[axis]
        if initial:
            red = total * (0.05 + 0.9 * labels[x].astype(jnp.float32))
            blue = total - red
            colour[0, x] = red
            colour[1, x] = blue
        shifted = [velocity[0] + tau * inverse * 0.001, velocity[1], velocity[2]]
        square = shifted[0] * shifted[0] + shifted[1] * shifted[1] + shifted[2] * shifted[2]
        scale = rate * total
        base = scale * (1.0 - 1.5 * square)
        state[0, x] = keep * state[0, x] + base * (1.0 / 3.0)
        face, edge = base * (1.0 / 18.0), base * (1.0 / 36.0)
        for up, down in PAIRS:
            along = 0.0
            for axis in range(3):
                if VELOCITY[up][axis] == 1:
                    along = along + shifted[axis]
                elif VELOCITY[up][axis] == -1:
                    along = along - shifted[axis]
            push = scale * along
            if up < 7:
                even, odd = face + 0.25 * (push * along), push * (1.0 / 6.0)
            else:
                even, odd = edge + 0.125 * (push * along), push * (1.0 / 12.0)
            state[up, x] = keep * state[up, x] + (even + odd)
            state[down, x] = keep * state[down, x] + (even - odd)

    def gradient_at(step, x):
        def at(buffer, place, plane, dy):
            return buffer[place, plane, LO + dy : HI + dy, :]

        here_ = step + 1

        def spread(plane):
            return (
                2.0 * at(scalars, here_, plane, 0)
                + (at(scalars, here_, plane, 1) + at(scalars, here_, plane, -1))
                + (at(scalars_up, 1, plane, 0) + at(scalars_down, 1, plane, 0))
            )

        def slope_y(plane):
            return at(scalars, here_, plane, 1) - at(scalars, here_, plane, -1)

        def slope_z(plane):
            return at(scalars_up, 1, plane, 0) - at(scalars_down, 1, plane, 0)

        low, mid, high = x, x + 1, x + 2
        up_up, up_down = at(scalars_up, 1, mid, 1), at(scalars_up, 1, mid, -1)
        down_up, down_down = at(scalars_down, 1, mid, 1), at(scalars_down, 1, mid, -1)
        along_x = spread(high) - spread(low)
        along_y = 2.0 * slope_y(mid) + (slope_y(high) + slope_y(low)) + ((up_up - up_down) + (down_up - down_down))
        along_z = 2.0 * slope_z(mid) + (slope_z(high) + slope_z(low)) + ((up_up - down_up) + (up_down - down_down))
        return [part * (1.0 / 12.0) for part in (along_x, along_y, along_z)]

    def put_post(step, x, name, value, packed, fluid=None):
        kind, number = name
        offset = VELOCITY[number]
        value = jnp.where(fluid, value, 0.0)
        if offset[1] != 0:
            sign = offset[1]
            edge = HI - 1 if sign == 1 else LO
        up, down = packed
        if offset[2] != 0:
            unrolled[UNROLLED[name], x] = value
            sign_z = offset[2]
            first = Z_FACE[sign_z].index(name) * 8
            for half in range(2):
                tile = value[8 * half : 8 * half + 8]
                place = first + 2 * x + half
                if sign_z == 1:
                    up = pack_z(tile, place, 1, up)
                else:
                    down = pack_z(tile, place, -1, down)
            value = pltpu.roll(value, 1 if sign_z == 1 else 127, axis=1)
            if name not in ACROSS_YZ:
                value = jnp.where(wide_lane == edge_lane(sign_z), 0.0, value)
        posts[step, SLOT[name], x + 1, LO:HI, :] = value
        if offset[1] != 0:
            line = Y_FACE[sign].index(name) * 4 + x
            post_y[step, SIDE[sign], line] = posts[step, SLOT[name], x + 1, edge : edge + 1, :]
        return up, down

    def collide_body(step, x, packed):
        gradient = gradient_at(step, x)
        squares = [part * part for part in gradient]
        total = squares[0] + squares[1] + squares[2]
        fluid = scalars[0, x + 1, LO:HI, :] > 0.0
        packed = put_post(step, x, ("f", 0), state[0, x], packed, fluid)
        third = total * (1.0 / 3.0)
        for up, down in PAIRS:
            if up < 7:
                surface = (TENSION / 18.0) * (squares[(up - 1) // 2] - third)
            else:
                slope = 0.0
                for axis in range(3):
                    if VELOCITY[up][axis] == 1:
                        slope = slope + gradient[axis]
                    elif VELOCITY[up][axis] == -1:
                        slope = slope - gradient[axis]
                surface = (TENSION / 36.0) * (slope * slope - 2.0 * third)
            packed = put_post(step, x, ("f", up), state[up, x] + surface, packed, fluid)
            packed = put_post(step, x, ("f", down), state[down, x] + surface, packed, fluid)
        red, blue = colour[0, x], colour[1, x]
        mixing = (0.5 * 0.125) * (red * blue / (red + blue)) * lax.rsqrt(jnp.maximum(total, 0.01))
        packed = put_post(step, x, ("r", 0), 0.25 * red, packed, fluid)
        packed = put_post(step, x, ("b", 0), 0.25 * blue, packed, fluid)
        for axis in range(3):
            drift = 0.5 * speed[axis, x]
            across = mixing * gradient[axis]
            for kind, amount, turn in (("r", red, 1.0), ("b", blue, -1.0)):
                mean = 0.125 * amount
                lean = amount * drift + turn * across
                packed = put_post(step, x, (kind, 2 * axis + 1), mean + lean, packed, fluid)
                packed = put_post(step, x, (kind, 2 * axis + 2), mean - lean, packed, fluid)
        return packed

    def state_at(name):
        return {"f": 0, "r": 19, "b": 26}[name[0]] + name[1]

    def opened_at(x, offset):
        dx, dy, dz = offset
        return shifted_scalars[dz][0, x + 1 - dx, LO - dy : HI - dy, :] > 0.0

    def bounced_at(step, x, name):
        back = (name[0], OPPOSITE[name[1]])
        if VELOCITY[name[1]][2] != 0:
            return unrolled[UNROLLED[back], x]
        return posts[step, SLOT[back], x + 1, LO:HI, :]

    def stream_inside(step, x, end, last):
        fluid = scalars[0, x + 1, LO:HI, :] > 0.0
        names = [name for name in EVERY if (last or name[0] == "f") and name not in ACROSS_YZ]
        for name in names:
            dx, dy, dz = VELOCITY[name[1]]
            if name[1] == 0:
                value = posts[step, SLOT[name], x + 1, LO:HI, :]
            else:
                if dx != 0 and dx == end:
                    arriving = 0.0
                else:
                    arriving = posts[step, SLOT[name], x + 1 - dx, LO - dy : HI - dy, :]
                value = jnp.where(opened_at(x, (dx, dy, dz)), arriving, bounced_at(step, x, name))
            state[state_at(name), x] = jnp.where(fluid, value, 0.0) if last else value

    def stream_across(step, x, last):
        fluid = scalars[0, x + 1, LO:HI, :] > 0.0
        for name in ACROSS_YZ:
            dx, dy, dz = VELOCITY[name[1]]
            arriving = posts[step, SLOT[name], x + 1, LO - dy : HI - dy, :]
            value = jnp.where(opened_at(x, (dx, dy, dz)), arriving, bounced_at(step, x, name))
            state[state_at(name), x] = jnp.where(fluid, value, 0.0) if last else value

    def arrivals(step, last):
        def wanted(name):
            return last or name[0] == "f"

        def kept(x, rows, value):
            if not last:
                return value
            return jnp.where(scalars[0, x + 1, LO + rows.start : LO + rows.stop, :] > 0.0, value, 0.0)

        def z_columns(name, dx, column, half):
            dz = VELOCITY[name[1]][2]
            place = Z_FACE[dz].index(name) * 8 + 2 * column + half
            face = post_z_got[step, SIDE[dz], TURN[dx]]
            return jnp.where(lane == edge_lane(dz), unpack_z(face, place, dz), 0.0)

        def add_z():
            for dz in (1, -1):
                for name in Z_FACE[dz]:
                    if name in ACROSS_YZ or not wanted(name):
                        continue
                    for x in range(NX):
                        source = x - VELOCITY[name[1]][0]
                        if not 0 <= source < NX:
                            continue
                        for half in range(2):
                            rows = slice(8 * half, 8 * half + 8)
                            value = kept(x, rows, z_columns(name, 0, source, half))
                            state[state_at(name), x, rows, :] = state[state_at(name), x, rows, :] + value
            for name in ACROSS_YZ:
                dz = VELOCITY[name[1]][2]
                face = post_z_got[step, SIDE[dz], 0]
                for x in range(NX):
                    for half in range(2):
                        rows = slice(LO + 8 * half, LO + 8 * half + 8)
                        place = Z_FACE[dz].index(name) * 8 + 2 * x + half
                        posts[step, SLOT[name], x + 1, rows, :] = jnp.where(
                            lane == edge_lane(dz), unpack_z(face, place, dz), posts[step, SLOT[name], x + 1, rows, :]
                        )

        def add_x():
            for dx, end, ghost, column, names in ((1, 0, 0, NX - 1, X_UP), (-1, NX - 1, NX + 1, 0, X_DOWN)):
                for name in names:
                    if not wanted(name):
                        continue
                    _, dy, dz = VELOCITY[name[1]]
                    if dy != 0:
                        row_ghost = LO - 1 if dy == 1 else HI
                        line = post_y_got[step, SIDE[dy], xy_place(dx, not last)]
                        posts[step, SLOT[name], ghost, row_ghost : row_ghost + 1, :] = line
                    for half in range(2):
                        rows = slice(8 * half, 8 * half + 8)
                        first = LO + 8 * half - dy
                        value = posts[step, SLOT[name], ghost, first : first + 8, :]
                        if dz != 0:
                            value = value + z_columns(name, dx, column, half)
                        state[state_at(name), end, rows, :] = state[state_at(name), end, rows, :] + kept(end, rows, value)
        def add_y():
            for dy, edge in ((1, 0), (-1, NY - 1)):
                rows = slice(edge, edge + 1)
                for entry, name in enumerate(Y_FACE[dy]):
                    if name in ACROSS_YZ or not wanted(name):
                        continue
                    for x in range(NX):
                        source = x - VELOCITY[name[1]][0]
                        if not 0 <= source < NX:
                            continue
                        value = kept(x, rows, post_y_got[step, SIDE[dy], entry * 4 + source])
                        state[state_at(name), x, rows, :] = state[state_at(name), x, rows, :] + value

        def add_across():
            for name in ACROSS_YZ:
                _, dy, dz = VELOCITY[name[1]]
                entry, entry_z = Y_FACE[dy].index(name), Z_FACE[dz].index(name)
                half = 1 if dy == 1 else 0
                ghost = LO - 1 if dy == 1 else HI
                for x in range(NX):
                    corner = unpack_z(post_row_got[step, SIDE[dy], SIDE[dz], 0], entry_z * 8 + 2 * x + half, dz)
                    line = jnp.where(row_lane == edge_lane(dz), corner, post_y_got[step, SIDE[dy], entry * 4 + x])
                    posts[step, SLOT[name], x + 1, ghost : ghost + 1, :] = line

        return add_x, add_y, add_z, add_across

    shifted_scalars = {0: scalars, 1: scalars_down, -1: scalars_up}

    def add_up(step, packed):
        up, down = packed
        for x in range(NX):
            for place, kind in enumerate(("r", "b")):
                total = posts[step, SLOT[(kind, 0)], x + 1, LO:HI, :]
                for number in range(1, 7):
                    dx, dy, dz = VELOCITY[number]
                    plane = x + 1 - dx
                    opened = shifted_scalars[dz][0, plane, LO - dy : HI - dy, :] > 0.0
                    back = (kind, OPPOSITE[number])
                    if dz != 0:
                        bounced = unrolled[UNROLLED[back], x]
                    else:
                        bounced = posts[step, SLOT[back], x + 1, LO:HI, :]
                    if 1 <= plane <= NX:
                        arriving = posts[step, SLOT[(kind, number)], plane, LO - dy : HI - dy, :]
                    else:
                        arriving = 0.0
                    total = total + jnp.where(opened, arriving, bounced)
                partial[place, x] = total
                for half in range(2):
                    tile = total[8 * half : 8 * half + 8]
                    lanes = SUM_Z + 8 * place + 2 * x + half
                    up, down = pack_z(tile, lanes, 1, up), pack_z(tile, lanes, -1, down)
                for dx, end in ((1, NX - 1), (-1, 0)):
                    if x == end:
                        post_part[step, SIDE[dx], NY * place : NY * place + NY, :] = total
                for dy, edge in ((1, NY - 1), (-1, 0)):
                    post_y[step, SIDE[dy], SUM_Y + 4 * place + x] = partial[place, x, edge : edge + 1, :]
                for dy, half in ((1, 1), (-1, 0)):
                    rows = slice(LO + 8 * half, LO + 8 * half + 8)
                    tile = posts[step, SLOT[(kind, FACE[(1, dy)])], x + 1, rows, :]
                    lanes = Y_Z + 8 * place + 2 * x + (0 if dy == 1 else 1)
                    up, down = pack_z(tile, lanes, 1, up), pack_z(tile, lanes, -1, down)
        for place, kind in enumerate(("r", "b")):
            for dx, end in ((1, NX - 1), (-1, 0)):
                slot = SLOT[(kind, FACE[(0, dx)])]
                for half in range(2):
                    tile = posts[step, slot, end + 1, LO + 8 * half : LO + 8 * half + 8, :]
                    lanes = X_Z + 8 * place + (0 if dx == 1 else 6) + half
                    up, down = pack_z(tile, lanes, 1, up), pack_z(tile, lanes, -1, down)
                for dy, edge in ((1, HI - 1), (-1, LO)):
                    line = posts[step, slot, end + 1, edge : edge + 1, :]
                    post_y[step, SIDE[dy], X_Y + 2 * SIDE[dx] + place] = line
                    post_xy[step, SIDE[dx], SIDE[dy], X_XY + place] = line
                    post_xy[step, SIDE[dx], SIDE[dy], SUM_XY + place] = partial[place, end, edge - LO : edge - LO + 1, :]
                    line = posts[step, SLOT[(kind, FACE[(1, dy)])], end + 1, edge : edge + 1, :]
                    post_xy[step, SIDE[dx], SIDE[dy], Y_XY + place] = line
                    part = Y_PART + 2 * SIDE[dy] + place
                    post_part[step, SIDE[dx], part : part + 1, :] = line
        return up, down

    def put_edges(step, packed, fused):
        for dx, end in ((1, NX - 1), (-1, 0)):
            for dy, edge in ((1, HI - 1), (-1, LO)):
                slot = SLOT[("f", VELOCITY.index((dx, dy, 0)))]
                post_xy[step, SIDE[dx], SIDE[dy], 0] = posts[step, slot, end + 1, edge : edge + 1, :]
            if fused:
                both = jnp.where(lane < 64, packed[0], pltpu.roll(packed[1], 64, axis=1))
                post_part[step, SIDE[dx], Z_PART : Z_PART + 8, :] = both
        for dz in (1, -1):
            post_z[step, SIDE[dz]] = packed[SIDE[dz]]
            for dy, edge in ((1, 7), (-1, 0)):
                line = post_z[step, SIDE[dz], edge : edge + 1, :]
                post_row[step, SIDE[dy], SIDE[dz], 0] = line
                if fused:
                    post_y[step, SIDE[dy], Z_Y + SIDE[dz]] = line

    def turned(value, lanes):
        return pltpu.roll(value, 128 - lanes, axis=1)

    def ratio(red, blue):
        return (red - blue) / (red + blue)

    def packed_ratio(sums):
        blue = turned(sums, 8)
        return ratio(sums, blue)

    def finish_phase(step, planes=(), corners=False):
        inside = len(planes) > 0
        here_ = step + 2

        def put(target, entry, plane, rows, value):
            fluid = shifted_scalars[target][0, plane, rows, :] > 0.0
            shifted_scalars[target][entry, plane, rows, :] = jnp.where(fluid, value, WETTING)

        interior = slice(LO, HI)
        z_got = {(dx, dz): post_z_got[step, SIDE[dz], TURN[dx]] for dx in (-1, 0, 1) for dz in (1, -1)}
        row_got = {
            (dx, dy, dz): post_row_got[step, SIDE[dy], SIDE[dz], TURN[dx]]
            for dx in (() if inside else (-1, 0, 1) if corners else (0,))
            for dy in (1, -1)
            for dz in (1, -1)
        }

        def xy_got(dx, dy, line):
            return post_y_got[step, SIDE[dy], ROWS_Y + ROWS_XY * SIDE[dx] + line]

        def with_columns(value, place, column, dx):
            halves = []
            for half in range(2):
                tile = value[8 * half : 8 * half + 8]
                for dz in (1, -1):
                    lanes = IN_Z + 8 * place + 2 * column + half
                    tile = tile + jnp.where(lane == edge_lane(dz), unpack_z(z_got[(dx, dz)], lanes, dz), 0.0)
                halves.append(tile)
            return jnp.concatenate(halves, axis=0)

        def with_rows(value, rows):
            for dy, edge in ((1, 0), (-1, NY - 1)):
                value = value + jnp.where(wide_row == edge, rows[dy], 0.0)
            return value

        def with_ends(line, offset, place, x):
            dx, dy = offset
            half = 1 if dy == 1 else 0
            for dz in (1, -1):
                lanes = IN_Z + 8 * place + 2 * x + half
                line = line + jnp.where(row_lane == edge_lane(dz), unpack_z(row_got[(dx, dy, dz)], lanes, dz), 0.0)
            return line

        for x in planes:
            sums = []
            for place, kind in enumerate(("r", "b")):
                total = partial[place, x]
                for dx, end, ghost in ((1, 0, 0), (-1, NX - 1, NX + 1)):
                    if x == end:
                        total = total + posts[step, SLOT[(kind, FACE[(0, dx)])], ghost, interior, :]
                rows = {}
                for dy in (1, -1):
                    entry = Y_FACE[dy].index((kind, FACE[(1, dy)]))
                    rows[dy] = post_y_got[step, SIDE[dy], entry * 4 + x]
                total = with_columns(with_rows(total, rows), place, x, 0)
                colour[place, x] = total
                sums.append(total)
            put(0, here_, x + 1, interior, ratio(*sums))
        if inside:
            return
        for dx, ghost, end, column in ((1, 0, 0, NX - 1), (-1, NX + 1, NX - 1, 0)):
            sums = []
            lines = {1: [], -1: []}
            for place, kind in enumerate(("r", "b")):
                if not corners:
                    total = post_part_got[step, SIDE[dx], NY * place : NY * place + NY, :]
                    total = total + posts[step, SLOT[(kind, FACE[(0, -dx)])], end + 1, interior, :]
                    rows = {dy: xy_got(dx, dy, Y_XY + place) for dy in (1, -1)}
                    sums.append(with_columns(with_rows(total, rows), place, column, dx))
                    continue
                for dy in (1, -1):
                    part = Y_PART + 2 * SIDE[-dy] + place
                    line = (
                        xy_got(dx, dy, SUM_XY + place)
                        + post_part_got[step, SIDE[dx], part : part + 1, :]
                        + post_y_got[step, SIDE[dy], X_Y + 2 * SIDE[-dx] + place]
                    )
                    lines[dy].append(with_ends(line, (dx, dy), place, column))
            if not corners:
                put(0, here_, ghost, interior, ratio(*sums))
                continue
            for dy, row_ghost in ((1, LO - 1), (-1, HI)):
                put(0, here_, ghost, slice(row_ghost, row_ghost + 1), ratio(*lines[dy]))
        for dy, row_ghost, edge in ((1, LO - 1, LO), (-1, HI, HI - 1)):
            for x in () if corners else range(NX):
                sums = []
                for place, kind in enumerate(("r", "b")):
                    line = post_y_got[step, SIDE[dy], SUM_Y + 4 * place + x]
                    line = line + posts[step, SLOT[(kind, FACE[(1, -dy)])], x + 1, edge : edge + 1, :]
                    for dx, end in ((1, 0), (-1, NX - 1)):
                        if x == end:
                            line = line + xy_got(dx, dy, X_XY + place)
                    sums.append(with_ends(line, (0, dy), place, x))
                put(0, here_, x + 1, slice(row_ghost, row_ghost + 1), ratio(*sums))
        low_x, high_x = lane % 8 < 2, lane % 8 >= 6
        first_y, last_y = (row == 0) & (lane % 2 == 0), (row == 7) & (lane % 2 == 1)
        row_low_x, row_high_x = row_lane % 8 < 2, row_lane % 8 >= 6
        for dz in (1, -1):

            def with_y(sums, dx):
                sums = sums + jnp.where(first_y, turned(row_got[(dx, 1, dz)], Y_Z), 0.0)
                return sums + jnp.where(last_y, turned(row_got[(dx, -1, dz)], Y_Z), 0.0)

            faces = {}
            if not corners:
                sums = turned(z_got[(0, dz)], SUM_Z) + turned(post_z[step, SIDE[-dz]], IN_Z)
                sums = sums + jnp.where(low_x, turned(z_got[(1, dz)], X_Z), 0.0)
                sums = sums + jnp.where(high_x, turned(z_got[(-1, dz)], X_Z), 0.0)
                faces[0] = packed_ratio(with_y(sums, 0))
            for dx in (1, -1) if corners else ():
                sums = turned(z_got[(dx, dz)], SUM_Z) + turned(z_got[(0, dz)], X_Z)
                sums = sums + turned(post_part_got[step, SIDE[dx], Z_PART : Z_PART + 8, :], IN_Z + 64 * SIDE[-dz])
                faces[dx] = packed_ratio(with_y(sums, dx))
            for plane in (0, NX + 1) if corners else range(1, NX + 1):
                dx, column = {0: (1, NX - 1), NX + 1: (-1, 0)}.get(plane, (0, plane - 1))
                for half in range(2):
                    rows = slice(LO + 8 * half, LO + 8 * half + 8)
                    value = scalars[here_, plane, rows, :]
                    ghost = unpack_z(faces[dx], 2 * column + half, dz)
                    value = jnp.where(lane == edge_lane(dz), ghost, pltpu.roll(value, 1 if dz == 1 else 127, axis=1))
                    put(dz, 1, plane, rows, value)
            for dy, row_ghost in ((1, LO - 1), (-1, HI)):
                half = 1 if dy == 1 else 0
                edge = 0 if dy == 1 else 7
                sums = turned(row_got[(0, dy, dz)], SUM_Z)
                sums = sums + turned(post_y_got[step, SIDE[dy], Z_Y + SIDE[-dz]], IN_Z)
                sums = sums + turned(post_z_got[step, SIDE[dz], 0, edge : edge + 1, :], Y_Z)
                if corners:
                    sums = sums + jnp.where(row_low_x, turned(row_got[(1, dy, dz)], X_Z), 0.0)
                    sums = sums + jnp.where(row_high_x, turned(row_got[(-1, dy, dz)], X_Z), 0.0)
                corner = packed_ratio(sums)
                for x in (0, NX - 1) if corners else range(1, NX - 1):
                    line = scalars[here_, x + 1, row_ghost : row_ghost + 1, :]
                    line = pltpu.roll(line, 1 if dz == 1 else 127, axis=1)
                    line = jnp.where(row_lane == edge_lane(dz), unpack_z(corner, 2 * x + half, dz), line)
                    put(dz, 1, x + 1, slice(row_ghost, row_ghost + 1), line)

    blank = jnp.zeros((8, NZ), jnp.float32)

    def first_phase(x, packed):
        fluid = 1.0 - solid[x].astype(jnp.float32)
        phase = jnp.where(fluid > 0.0, -0.9 + 1.8 * labels[x].astype(jnp.float32), WETTING)
        return set_phase(x, [fluid, phase], packed)

    barrier = pltpu.get_barrier_semaphore()

    def greet(dy, dz):
        for dx in (0, 1, -1) if 0 in (dy, dz) else (0,):
            pl.semaphore_signal(barrier, inc=1, device_id=neighbour((dx, dy, dz)), device_id_type=MESH)

    by_class(greet)
    for dx in (1, -1):
        pl.semaphore_signal(barrier, inc=1, device_id=neighbour((dx, 0, 0)), device_id_type=MESH)
    beside_y = 2 - closed[(1, 1)].astype(jnp.int32) - closed[(1, -1)].astype(jnp.int32)
    beside_z = 2 - closed[(2, 1)].astype(jnp.int32) - closed[(2, -1)].astype(jnp.int32)
    beside = 2 + 3 * (beside_y + beside_z) + beside_y * beside_z

    def clear(dy, dz):
        for step in range(STEPS):
            if dz == 0:
                post_y_got[step, SIDE[dy]] = jnp.zeros((ROWS_Y_ALL, 1, NZ), jnp.float32)
            elif dy == 0:
                post_z_got[step, SIDE[dz]] = jnp.zeros((3, 8, NZ), jnp.float32)
            else:
                post_row_got[step, SIDE[dy], SIDE[dz]] = jnp.zeros((3, 1, NZ), jnp.float32)

    for dy, dz in CLASSES:
        pl.when(jnp.logical_not(has((0, -dy, -dz))))(functools.partial(clear, dy, dz))

    for step in range(STEPS):
        for side in range(2):
            post_part[step, side, Y_PART : Y_PART + 8, :] = blank
        for name in Y_FACE[1] + Y_FACE[-1]:
            if name not in ACROSS_YZ:
                ghost = LO - 1 if VELOCITY[name[1]][1] == 1 else HI
                for plane in range(1, NX + 1):
                    posts[step, SLOT[name], plane, ghost : ghost + 1, :] = blank[0:1]

    loads[0].wait()
    loads[1].wait()
    packed = lax.fori_loop(0, NX, first_phase, (blank, blank), unroll=True)
    pl.semaphore_wait(barrier, beside)
    send_phase(packed)
    loads[2].wait()
    lax.fori_loop(0, NX, lambda x, _: relax_body(0, x, True), None, unroll=True)
    unpack_phase()

    def collide_middle(step):
        return lax.fori_loop(1, NX - 1, lambda x, p: collide_body(step, x, p), (blank, blank), unroll=True)

    def move(step, packed, fused):
        packed = lax.fori_loop(0, 2, lambda turn, p: collide_body(step, 3 - 3 * turn, p), packed, unroll=True)
        if fused:
            packed = add_up(step, packed)
        put_edges(step, packed, fused)
        by_class(functools.partial(send_post_class, step, fused), classes=ON_Y + ON_YZ)
        for dx, near, far in ((1, NX, 0), (-1, 1, NX + 1)):
            send(post_plane(step, dx, near), post_plane(step, dx, far), step + 1, X_CLASS[dx], (dx, 0, 0))
        if fused:
            by_class(functools.partial(send_corner_class, step), classes=ON_YZ)
        by_class(functools.partial(send_post_class, step, fused), classes=ON_Z)
        if fused:
            for dx in (1, -1):
                side = SIDE[dx]
                send(post_part.at[step, side], post_part_got.at[step, side], step + 1, PART_CLASS[dx], (dx, 0, 0))
        last = not fused
        stream_inside(step, 0, 1, last)
        lax.fori_loop(1, NX - 1, lambda x, _: stream_inside(step, x, 0, last), None, unroll=True)
        stream_inside(step, NX - 1, -1, last)
        await_posts(send_sem, step, fused, CLASSES, False)
        await_x(send_sem, step)
        if fused:
            await_parts(send_sem, step)
            await_corners(send_sem, step, False)
        add_x, add_y, add_z, add_across = arrivals(step, last)
        await_posts(recv_sem, step, fused, ON_Z, True)
        add_z()
        await_posts(recv_sem, step, fused, ON_Y, True)
        add_y()
        if fused:
            finish_phase(step, (1, 2))
        await_posts(recv_sem, step, fused, ON_YZ, True)
        add_across()
        lax.fori_loop(0, NX, lambda x, _: stream_across(step, x, last), None, unroll=True)
        if fused:
            lax.fori_loop(1, 3, lambda x, _: relax_body(step + 1, x, False), None, unroll=True)
        await_x(recv_sem, step)
        add_x()
        if fused:
            finish_phase(step, (0, 3))
            lax.fori_loop(0, 2, lambda turn, _: relax_body(step + 1, 3 - 3 * turn, False), None, unroll=True)
            await_parts(recv_sem, step)
            finish_phase(step)
            packed = collide_middle(step + 1)
            await_corners(recv_sem, step, True)
            finish_phase(step, corners=True)
        return packed

    packed = lax.fori_loop(0, STEPS - 1, lambda step, p: move(step, p, True), collide_middle(0))
    move(STEPS - 1, packed, False)


def hand_out(every, momentum_out, red_out, blue_out, sem):
    copies = []
    first = 0
    for place, target in enumerate((momentum_out, red_out, blue_out)):
        count = target.shape[0]
        copies.append(pltpu.make_async_copy(every.at[pl.ds(first, count)], target, sem.at[place]))
        first += count
    for copy in copies:
        copy.start()
    for copy in copies:
        copy.wait()


def shards(sizes, momentum_sets, labels, solid_mask):
    block = (NX, NY, NZ)
    f32 = jnp.float32
    vmem = lambda *shape, dtype=f32: pltpu.VMEM(shape, dtype)
    every = pl.pallas_call(
        functools.partial(kernel, sizes=sizes),
        out_shape=vmem(33, *block),
        in_specs=[pl.BlockSpec(memory_space=pltpu.HBM)] * 3,
        out_specs=pl.BlockSpec(memory_space=pltpu.VMEM),
        scratch_shapes=[
            vmem(*block, dtype=jnp.int32),
            vmem(*block, dtype=jnp.int32),
            vmem(1 + STEPS, NX + 2, ROWS, NZ),
            vmem(2, NX + 2, ROWS, NZ),
            vmem(2, NX + 2, ROWS, NZ),
            vmem(STEPS, 33, NX + 2, ROWS, NZ),
            vmem(14, *block),
            vmem(3, *block),
            vmem(2, *block),
            vmem(2, 8, 1, NZ),
            vmem(2, 8, NZ),
            vmem(2, 2, 1, NZ),
            vmem(2, 12, 1, NZ),
            vmem(2, 3, 8, NZ),
            vmem(2, 2, 1, NZ),
            vmem(STEPS, 2, ROWS_Y, 1, NZ),
            vmem(STEPS, 2, 8, NZ),
            vmem(STEPS, 2, 2, 1, 1, NZ),
            vmem(STEPS, 2, 2, ROWS_XY, 1, NZ),
            vmem(STEPS, 2, ROWS_PART, NZ),
            vmem(STEPS, 2, ROWS_Y_ALL, 1, NZ),
            vmem(STEPS, 2, 3, 8, NZ),
            vmem(STEPS, 2, 2, 3, 1, NZ),
            vmem(STEPS, 2, ROWS_PART, NZ),
            vmem(2, *block),
            pltpu.SemaphoreType.DMA((3,)),
            pltpu.SemaphoreType.DMA((1 + STEPS, 16)),
            pltpu.SemaphoreType.DMA((1 + STEPS, 16)),
        ],
        compiler_params=pltpu.CompilerParams(
            collective_id=0, has_side_effects=True, vmem_limit_bytes=VMEM_LIMIT
        ),
        cost_estimate=pl.CostEstimate(flops=15_000_000, bytes_accessed=1_800_000, transcendentals=0),
    )(*(pltpu.with_memory_space_constraint(array, pltpu.HBM) for array in (momentum_sets, labels, solid_mask)))
    return pl.pallas_call(
        hand_out,
        out_shape=[jax.ShapeDtypeStruct((count,) + block, f32) for count in (19, 7, 7)],
        in_specs=[pl.BlockSpec(memory_space=pltpu.VMEM)],
        out_specs=[pl.BlockSpec(memory_space=pltpu.HBM)] * 3,
        scratch_shapes=[pltpu.SemaphoreType.DMA((3,))],
        cost_estimate=pl.CostEstimate(flops=0, bytes_accessed=2_200_000, transcendentals=0),
    )(pltpu.with_memory_space_constraint(every, pltpu.VMEM))


def solution(mesh):
    sizes = tuple(mesh.shape[axis] for axis in ("flow", "gy", "gz"))
    split = P("flow", "gy", "gz")
    split_sets = P(None, "flow", "gy", "gz")
    return jax.shard_map(
        functools.partial(shards, sizes),
        mesh=mesh,
        in_specs=(split_sets, split, split),
        out_specs=(split_sets, split_sets, split_sets),
        check_vma=False,
    )
```

```python
import functools

import jax
import jax.numpy as jnp
from jax import lax
from jax.experimental import pallas as pl
from jax.experimental.pallas import tpu as pltpu
from jax.sharding import PartitionSpec as P

STEPS = 3
NX, NY, NZ = 4, 16, 128
LO, HI = 8, 8 + NY
ROWS = 32
WETTING = 0.3
TENSION = 0.05
MESH = pl.DeviceIdType.MESH
VMEM_LIMIT = 40 * 1024 * 1024

VELOCITY = (
    (0, 0, 0),
    (1, 0, 0),
    (-1, 0, 0),
    (0, 1, 0),
    (0, -1, 0),
    (0, 0, 1),
    (0, 0, -1),
    (1, 1, 0),
    (-1, -1, 0),
    (1, -1, 0),
    (-1, 1, 0),
    (1, 0, 1),
    (-1, 0, -1),
    (1, 0, -1),
    (-1, 0, 1),
    (0, 1, 1),
    (0, -1, -1),
    (0, 1, -1),
    (0, -1, 1),
)
OPPOSITE = (0, 2, 1, 4, 3, 6, 5, 8, 7, 10, 9, 12, 11, 14, 13, 16, 15, 18, 17)
PAIRS = ((1, 2), (3, 4), (5, 6), (7, 8), (9, 10), (11, 12), (13, 14), (15, 16), (17, 18))

X_UP = [("f", i) for i in (1, 7, 9, 11, 13)] + [("r", 1), ("b", 1)]
X_DOWN = [("f", i) for i in (2, 8, 10, 12, 14)] + [("r", 2), ("b", 2)]
EVERY = [("f", i) for i in range(19)] + [("r", i) for i in range(7)] + [("b", i) for i in range(7)]
ORDER = X_UP + X_DOWN + [name for name in EVERY if name not in X_UP + X_DOWN]
SLOT = {name: place for place, name in enumerate(ORDER)}
Y_FACE = {
    1: (("f", 3), ("r", 3), ("f", 7), ("f", 10), ("f", 15), ("f", 17), ("b", 3)),
    -1: (("f", 4), ("r", 4), ("f", 9), ("f", 8), ("f", 18), ("f", 16), ("b", 4)),
}
Z_FACE = {
    1: (("f", 5), ("f", 11), ("f", 14), ("f", 15), ("f", 18), ("r", 5), ("b", 5)),
    -1: (("f", 6), ("f", 13), ("f", 12), ("f", 17), ("f", 16), ("r", 6), ("b", 6)),
}
Z_MOVING = Z_FACE[1] + Z_FACE[-1]
UNROLLED = {name: place for place, name in enumerate(Z_MOVING)}
DIRECTIONS = VELOCITY[1:]
CORNERS = tuple((a, b, c) for a in (1, -1) for b in (1, -1) for c in (1, -1))
NEIGHBOURS = DIRECTIONS + CORNERS
SIDE = {1: 0, -1: 1}
TURN = {0: 0, 1: 1, -1: 2}
FACE = {(1, 1): 3, (1, -1): 4, (0, 1): 1, (0, -1): 2, (2, 1): 5, (2, -1): 6}
IN_Z, SUM_Z, X_Z, Y_Z = 40, 56, 72, 88
SUM_Y, X_Y, Z_Y, ROWS_Y = 28, 36, 40, 42
Y_XY, SUM_XY, X_XY, ROWS_XY = 1, 3, 5, 7
ROWS_Y_ALL = ROWS_Y + 2 * ROWS_XY
Y_PART, Z_PART, ROWS_PART = 32, 40, 48
ON_Y, ON_Z = ((1, 0), (-1, 0)), ((0, 1), (0, -1))
ON_YZ = ((1, 1), (1, -1), (-1, 1), (-1, -1))
CLASSES = ON_YZ + ON_Y + ON_Z
CLASS = {way: place for place, way in enumerate(CLASSES)}
X_CLASS = {1: 8, -1: 9}
PART_CLASS = {1: 10, -1: 11}
CORNER_CLASS = {way: 12 + place for place, way in enumerate(ON_YZ)}
ACROSS_YZ = tuple(("f", number) for number in (15, 16, 17, 18))


def kernel(
    momentum_in,
    labels_in,
    solid_in,
    state,
    labels,
    solid,
    scalars,
    scalars_down,
    scalars_up,
    posts,
    unrolled,
    speed,
    colour,
    phase_y,
    phase_z,
    phase_yz,
    phase_y_got,
    phase_z_got,
    phase_yz_got,
    post_y,
    post_z,
    post_row,
    post_xy,
    post_part,
    post_y_got,
    post_z_got,
    post_row_got,
    post_part_got,
    partial,
    zero_rows,
    zero_tiles,
    in_sem,
    send_sem,
    recv_sem,
    *,
    sizes,
):
    here = tuple(lax.axis_index(axis) for axis in ("flow", "gy", "gz"))

    flow = {
        0: here[0],
        1: jnp.where(here[0] == sizes[0] - 1, 0, here[0] + 1),
        -1: jnp.where(here[0] == 0, sizes[0] - 1, here[0] - 1),
    }
    lateral = [{0: here[axis], 1: here[axis] + 1, -1: here[axis] - 1} for axis in (1, 2)]

    def neighbour(offset):
        return (flow[offset[0]], lateral[0][offset[1]], lateral[1][offset[2]])

    closed = {
        (1, -1): here[1] == 0,
        (1, 1): here[1] == sizes[1] - 1,
        (2, -1): here[2] == 0,
        (2, 1): here[2] == sizes[2] - 1,
    }
    def has(offset):
        known = [jnp.logical_not(closed[(axis, offset[axis])]) for axis in (1, 2) if offset[axis] != 0]
        return functools.reduce(jnp.logical_and, known) if known else None

    def when(condition, action):
        if condition is None:
            action()
        else:
            pl.when(condition)(action)

    def by_class(action, always=False, classes=CLASSES):
        for dy, dz in classes:
            when(None if always else has((0, dy, dz)), functools.partial(action, dy, dz))

    lane = lax.broadcasted_iota(jnp.int32, (8, NZ), 1)
    wide_lane = lax.broadcasted_iota(jnp.int32, (NY, NZ), 1)
    wide_row = lax.broadcasted_iota(jnp.int32, (NY, NZ), 0)
    row = lax.broadcasted_iota(jnp.int32, (8, NZ), 0)
    row_lane = lax.broadcasted_iota(jnp.int32, (1, NZ), 1)

    loads = [
        pltpu.make_async_copy(solid_in, solid, in_sem.at[0]),
        pltpu.make_async_copy(labels_in, labels, in_sem.at[1]),
        pltpu.make_async_copy(momentum_in, state.at[pl.ds(0, 19)], in_sem.at[2]),
    ]
    for load in loads:
        load.start()

    def send(source, target, turn, place, offset):
        pltpu.make_async_remote_copy(
            src_ref=source,
            dst_ref=target,
            send_sem=send_sem.at[turn, place],
            recv_sem=recv_sem.at[turn, place],
            device_id=neighbour(offset),
            device_id_type=MESH,
        ).start()

    def await_bytes(sems, turn, place, like):
        pltpu.make_async_copy(like, like, sems.at[turn, place]).wait()

    def send_phase_class(dy, dz):
        place = CLASS[(dy, dz)]
        if dz == 0:
            side = SIDE[dy]
            send(phase_y.at[side], phase_y_got.at[side, pl.ds(0, 8)], 0, place, (0, dy, 0))
            for dx, line, target in ((1, 6, 8), (-1, 0, 10)):
                source = phase_y.at[side, pl.ds(line, 2)]
                send(source, phase_y_got.at[side, pl.ds(target, 2)], 0, place, (dx, dy, 0))
        elif dy == 0:
            side = SIDE[dz]
            for dx in (0, 1, -1):
                send(phase_z.at[side], phase_z_got.at[side, TURN[dx]], 0, place, (dx, 0, dz))
        else:
            sides = SIDE[dy], SIDE[dz]
            send(phase_yz.at[sides], phase_yz_got.at[sides], 0, place, (0, dy, dz))

    def phase_like(dy, dz):
        if dz == 0:
            return phase_y_got.at[SIDE[dy]]
        if dy == 0:
            return phase_z_got.at[SIDE[dz]]
        return phase_yz_got.at[SIDE[dy], SIDE[dz]]

    def phase_plane(plane):
        return scalars.at[pl.ds(0, 2), plane, pl.ds(LO, NY)]

    def post_plane(step, dx, plane):
        return posts.at[step, pl.ds(0 if dx == 1 else 7, 7), plane, pl.ds(LO, NY)]

    def xy_place(dx, fused):
        return ROWS_Y + ROWS_XY * SIDE[dx] if fused else SUM_Y + SIDE[dx]

    def send_post_class(step, fused, dy, dz):
        turn, place = step + 1, CLASS[(dy, dz)]
        if dz == 0:
            side = SIDE[dy]
            rows, rows_xy = pl.ds(0, ROWS_Y if fused else SUM_Y), ROWS_XY if fused else 1
            send(post_y.at[step, side, rows], post_y_got.at[step, side, rows], turn, place, (0, dy, 0))
            for dx in (1, -1):
                source = post_xy.at[step, SIDE[dx], side, pl.ds(0, rows_xy)]
                target = post_y_got.at[step, side, pl.ds(xy_place(dx, fused), rows_xy)]
                send(source, target, turn, place, (dx, dy, 0))
        elif dy == 0:
            side = SIDE[dz]
            for dx in (0, 1, -1):
                send(post_z.at[step, side], post_z_got.at[step, side, TURN[dx]], turn, place, (dx, 0, dz))
        else:
            sides = SIDE[dy], SIDE[dz]
            target = post_row_got.at[step, sides[0], sides[1], pl.ds(0, 1)]
            send(post_row.at[step, sides[0], sides[1]], target, turn, place, (0, dy, dz))

    def send_corner_class(step, dy, dz):
        sides = SIDE[dy], SIDE[dz]
        for dx in (1, -1):
            target = post_row_got.at[step, sides[0], sides[1], pl.ds(TURN[dx], 1)]
            send(post_row.at[step, sides[0], sides[1]], target, step + 1, CORNER_CLASS[(dy, dz)], (dx, dy, dz))

    def post_like(step, fused, dy, dz):
        if dz == 0:
            return post_y_got.at[step, SIDE[dy], pl.ds(0, ROWS_Y_ALL if fused else SUM_Y + 2)]
        if dy == 0:
            return post_z_got.at[step, SIDE[dz]]
        return post_row_got.at[step, SIDE[dy], SIDE[dz], pl.ds(0, 1)]

    def corner_like(step, dy, dz):
        return post_row_got.at[step, SIDE[dy], SIDE[dz], pl.ds(1, 2)]

    def await_posts(sems, step, fused, classes, backward):
        by_class(
            lambda dy, dz: await_bytes(sems, step + 1, CLASS[(dy, dz)], post_like(step, fused, dy, dz)),
            backward,
            classes,
        )

    def await_corners(sems, step, backward):
        by_class(
            lambda dy, dz: await_bytes(sems, step + 1, CORNER_CLASS[(dy, dz)], corner_like(step, dy, dz)),
            backward,
            ON_YZ,
        )

    def await_x(sems, step):
        for dx in (1, -1):
            await_bytes(sems, step + 1, X_CLASS[dx], post_plane(step, dx, 0 if dx == 1 else NX + 1))

    def await_parts(sems, step):
        for dx in (1, -1):
            await_bytes(sems, step + 1, PART_CLASS[dx], post_part_got.at[step, SIDE[dx]])

    def pack_z(tile, place, sign, packed):
        moved = pltpu.roll(tile, place + 1 if sign == 1 else place, axis=1)
        return jnp.where(lane == place, moved, packed)

    def unpack_z(packed, place, sign):
        return pltpu.roll(packed, (128 - place) % 128 if sign == 1 else 127 - place, axis=1)

    def edge_lane(sign):
        return 0 if sign == 1 else NZ - 1

    def set_phase(x, values, packed):
        up, down = packed
        for entry, value in enumerate(values):
            scalars[entry, x + 1, LO:HI, :] = value
            for dy, edge in ((1, HI - 1), (-1, LO)):
                phase_y[SIDE[dy], x * 2 + entry] = scalars[entry, x + 1, edge : edge + 1, :]
            for half in range(2):
                tile = value[8 * half : 8 * half + 8]
                place = entry * 8 + 2 * x + half
                up = pack_z(tile, place, 1, up)
                down = pack_z(tile, place, -1, down)
        return up, down

    def send_phase(packed):
        for dz in (1, -1):
            phase_z[SIDE[dz]] = packed[SIDE[dz]]
            for dy, edge in ((1, 7), (-1, 0)):
                phase_yz[SIDE[dy], SIDE[dz], 0] = phase_z[SIDE[dz], edge : edge + 1, :]
        by_class(send_phase_class)
        for dx, near, far in ((1, NX, 0), (-1, 1, NX + 1)):
            send(phase_plane(near), phase_plane(far), 0, X_CLASS[dx], (dx, 0, 0))

    def unpack_phase():
        first, count = 0, 2
        fills = (0.0, WETTING)
        shifted = {1: scalars_down, -1: scalars_up}

        def place_of(entry):
            return entry

        def cover(offset, value, fill):
            for axis in (1, 2):
                if offset[axis] != 0:
                    value = jnp.where(closed[(axis, -offset[axis])], fill, value)
            return value

        def arrive(sems, backward):
            by_class(lambda dy, dz: await_bytes(sems, 0, CLASS[(dy, dz)], phase_like(dy, dz)), backward)
            for dx in (1, -1):
                await_bytes(sems, 0, X_CLASS[dx], phase_plane(0))

        def shift_plane(entry, plane, dz, face, column):
            for half in range(2):
                rows = slice(LO + 8 * half, LO + 8 * half + 8)
                value = scalars[first + entry, plane, rows, :]
                place = entry * 8 + 2 * column + half
                ghost = cover((0, 0, dz), unpack_z(face, place, dz), fills[entry])
                shifted[dz][place_of(entry), plane, rows, :] = jnp.where(
                    lane == edge_lane(dz), ghost, pltpu.roll(value, 1 if dz == 1 else 127, axis=1)
                )

        arrive(send_sem, False)
        arrive(recv_sem, True)
        for dz in (1, -1):
            face = phase_z_got[SIDE[dz], 0]
            for entry in range(count):
                for x in range(NX):
                    shift_plane(entry, x + 1, dz, face, x)
        for dy, ghost in ((1, LO - 1), (-1, HI)):
            half = 1 if dy == 1 else 0
            for entry in range(count):
                for x in range(NX):
                    line = cover((0, dy, 0), phase_y_got[SIDE[dy], x * count + entry], fills[entry])
                    scalars[first + entry, x + 1, ghost : ghost + 1, :] = line
                    for dz in (1, -1):
                        corner = phase_yz_got[SIDE[dy], SIDE[dz], 0]
                        place = entry * 8 + 2 * x + half
                        corner = cover((0, dy, dz), unpack_z(corner, place, dz), fills[entry])
                        shifted[dz][place_of(entry), x + 1, ghost : ghost + 1, :] = jnp.where(
                            row_lane == edge_lane(dz), corner, pltpu.roll(line, 1 if dz == 1 else 127, axis=1)
                        )
        for dx, plane, column in ((1, 0, NX - 1), (-1, NX + 1, 0)):
            for dy, ghost in ((1, LO - 1), (-1, HI)):
                for entry in range(count):
                    line = phase_y_got[SIDE[dy], 8 + 2 * SIDE[dx] + entry]
                    scalars[first + entry, plane, ghost : ghost + 1, :] = cover((0, dy, 0), line, fills[entry])
            for dz in (1, -1):
                for entry in range(count):
                    shift_plane(entry, plane, dz, phase_z_got[SIDE[dz], TURN[dx]], column)

    def relax_body(step, x, initial):
        total = state[0, x]
        flux = [0.0, 0.0, 0.0]
        for up, down in PAIRS:
            first, second = state[up, x], state[down, x]
            total = total + (first + second)
            difference = first - second
            for axis in range(3):
                if VELOCITY[up][axis] == 1:
                    flux[axis] = flux[axis] + difference
                elif VELOCITY[up][axis] == -1:
                    flux[axis] = flux[axis] - difference
        inverse = 1.0 / total
        velocity = [part * inverse for part in flux]
        phase = scalars[step + 1, x + 1, LO:HI, :]
        tau = 1.3 - 0.3 * phase
        rate = 1.0 / tau
        keep = 1.0 - rate
        for axis in range(3):
            speed[axis, x] = velocity[axis]
        if initial:
            red = total * (0.05 + 0.9 * labels[x].astype(jnp.float32))
            blue = total - red
            colour[0, x] = red
            colour[1, x] = blue
        shifted = [velocity[0] + tau * inverse * 0.001, velocity[1], velocity[2]]
        square = shifted[0] * shifted[0] + shifted[1] * shifted[1] + shifted[2] * shifted[2]
        scale = rate * total
        base = scale * (1.0 - 1.5 * square)
        state[0, x] = keep * state[0, x] + base * (1.0 / 3.0)
        face, edge = base * (1.0 / 18.0), base * (1.0 / 36.0)
        for up, down in PAIRS:
            along = 0.0
            for axis in range(3):
                if VELOCITY[up][axis] == 1:
                    along = along + shifted[axis]
                elif VELOCITY[up][axis] == -1:
                    along = along - shifted[axis]
            push = scale * along
            if up < 7:
                even, odd = face + 0.25 * (push * along), push * (1.0 / 6.0)
            else:
                even, odd = edge + 0.125 * (push * along), push * (1.0 / 12.0)
            state[up, x] = keep * state[up, x] + (even + odd)
            state[down, x] = keep * state[down, x] + (even - odd)

    def gradient_at(step, x):
        def at(buffer, place, plane, dy):
            return buffer[place, plane, LO + dy : HI + dy, :]

        here_ = step + 1

        def spread(plane):
            return (
                2.0 * at(scalars, here_, plane, 0)
                + (at(scalars, here_, plane, 1) + at(scalars, here_, plane, -1))
                + (at(scalars_up, 1, plane, 0) + at(scalars_down, 1, plane, 0))
            )

        def slope_y(plane):
            return at(scalars, here_, plane, 1) - at(scalars, here_, plane, -1)

        def slope_z(plane):
            return at(scalars_up, 1, plane, 0) - at(scalars_down, 1, plane, 0)

        low, mid, high = x, x + 1, x + 2
        up_up, up_down = at(scalars_up, 1, mid, 1), at(scalars_up, 1, mid, -1)
        down_up, down_down = at(scalars_down, 1, mid, 1), at(scalars_down, 1, mid, -1)
        along_x = spread(high) - spread(low)
        along_y = 2.0 * slope_y(mid) + (slope_y(high) + slope_y(low)) + ((up_up - up_down) + (down_up - down_down))
        along_z = 2.0 * slope_z(mid) + (slope_z(high) + slope_z(low)) + ((up_up - down_up) + (up_down - down_down))
        return [part * (1.0 / 12.0) for part in (along_x, along_y, along_z)]

    def put_post(step, x, name, value, packed, fluid=None):
        kind, number = name
        offset = VELOCITY[number]
        value = jnp.where(fluid, value, 0.0)
        if offset[1] != 0:
            sign = offset[1]
            edge = HI - 1 if sign == 1 else LO
        up, down = packed
        if offset[2] != 0:
            unrolled[UNROLLED[name], x] = value
            sign_z = offset[2]
            first = Z_FACE[sign_z].index(name) * 8
            for half in range(2):
                tile = value[8 * half : 8 * half + 8]
                place = first + 2 * x + half
                if sign_z == 1:
                    up = pack_z(tile, place, 1, up)
                else:
                    down = pack_z(tile, place, -1, down)
            value = pltpu.roll(value, 1 if sign_z == 1 else 127, axis=1)
            if name not in ACROSS_YZ:
                value = jnp.where(wide_lane == edge_lane(sign_z), 0.0, value)
        posts[step, SLOT[name], x + 1, LO:HI, :] = value
        if offset[1] != 0:
            line = Y_FACE[sign].index(name) * 4 + x
            post_y[step, SIDE[sign], line] = posts[step, SLOT[name], x + 1, edge : edge + 1, :]
        return up, down

    def collide_body(step, x, packed):
        gradient = gradient_at(step, x)
        squares = [part * part for part in gradient]
        total = squares[0] + squares[1] + squares[2]
        fluid = scalars[0, x + 1, LO:HI, :] > 0.0
        packed = put_post(step, x, ("f", 0), state[0, x], packed, fluid)
        third = total * (1.0 / 3.0)
        for up, down in PAIRS:
            if up < 7:
                surface = (TENSION / 18.0) * (squares[(up - 1) // 2] - third)
            else:
                slope = 0.0
                for axis in range(3):
                    if VELOCITY[up][axis] == 1:
                        slope = slope + gradient[axis]
                    elif VELOCITY[up][axis] == -1:
                        slope = slope - gradient[axis]
                surface = (TENSION / 36.0) * (slope * slope - 2.0 * third)
            packed = put_post(step, x, ("f", up), state[up, x] + surface, packed, fluid)
            packed = put_post(step, x, ("f", down), state[down, x] + surface, packed, fluid)
        red, blue = colour[0, x], colour[1, x]
        mixing = (0.5 * 0.125) * (red * blue / (red + blue)) * lax.rsqrt(jnp.maximum(total, 0.01))
        packed = put_post(step, x, ("r", 0), 0.25 * red, packed, fluid)
        packed = put_post(step, x, ("b", 0), 0.25 * blue, packed, fluid)
        for axis in range(3):
            drift = 0.5 * speed[axis, x]
            across = mixing * gradient[axis]
            for kind, amount, turn in (("r", red, 1.0), ("b", blue, -1.0)):
                mean = 0.125 * amount
                lean = amount * drift + turn * across
                packed = put_post(step, x, (kind, 2 * axis + 1), mean + lean, packed, fluid)
                packed = put_post(step, x, (kind, 2 * axis + 2), mean - lean, packed, fluid)
        return packed

    def state_at(name):
        return {"f": 0, "r": 19, "b": 26}[name[0]] + name[1]

    def opened_at(x, offset):
        dx, dy, dz = offset
        return shifted_scalars[dz][0, x + 1 - dx, LO - dy : HI - dy, :] > 0.0

    def bounced_at(step, x, name):
        back = (name[0], OPPOSITE[name[1]])
        if VELOCITY[name[1]][2] != 0:
            return unrolled[UNROLLED[back], x]
        return posts[step, SLOT[back], x + 1, LO:HI, :]

    def stream_inside(step, x, end, last):
        fluid = scalars[0, x + 1, LO:HI, :] > 0.0
        names = [name for name in EVERY if (last or name[0] == "f") and name not in ACROSS_YZ]
        for name in names:
            dx, dy, dz = VELOCITY[name[1]]
            if name[1] == 0:
                value = posts[step, SLOT[name], x + 1, LO:HI, :]
            else:
                if dx != 0 and dx == end:
                    arriving = 0.0
                else:
                    arriving = posts[step, SLOT[name], x + 1 - dx, LO - dy : HI - dy, :]
                value = jnp.where(opened_at(x, (dx, dy, dz)), arriving, bounced_at(step, x, name))
            state[state_at(name), x] = jnp.where(fluid, value, 0.0) if last else value

    def stream_across(step, x, last):
        fluid = scalars[0, x + 1, LO:HI, :] > 0.0
        for name in ACROSS_YZ:
            dx, dy, dz = VELOCITY[name[1]]
            arriving = posts[step, SLOT[name], x + 1, LO - dy : HI - dy, :]
            value = jnp.where(opened_at(x, (dx, dy, dz)), arriving, bounced_at(step, x, name))
            state[state_at(name), x] = jnp.where(fluid, value, 0.0) if last else value

    def arrivals(step, last):
        def wanted(name):
            return last or name[0] == "f"

        def kept(x, rows, value):
            if not last:
                return value
            return jnp.where(scalars[0, x + 1, LO + rows.start : LO + rows.stop, :] > 0.0, value, 0.0)

        def z_columns(name, dx, column, half):
            dz = VELOCITY[name[1]][2]
            place = Z_FACE[dz].index(name) * 8 + 2 * column + half
            face = post_z_got[step, SIDE[dz], TURN[dx]]
            return jnp.where(lane == edge_lane(dz), unpack_z(face, place, dz), 0.0)

        def add_z():
            for dz in (1, -1):
                for name in Z_FACE[dz]:
                    if name in ACROSS_YZ or not wanted(name):
                        continue
                    for x in range(NX):
                        source = x - VELOCITY[name[1]][0]
                        if not 0 <= source < NX:
                            continue
                        for half in range(2):
                            rows = slice(8 * half, 8 * half + 8)
                            value = kept(x, rows, z_columns(name, 0, source, half))
                            state[state_at(name), x, rows, :] = state[state_at(name), x, rows, :] + value
            for name in ACROSS_YZ:
                dz = VELOCITY[name[1]][2]
                face = post_z_got[step, SIDE[dz], 0]
                for x in range(NX):
                    for half in range(2):
                        rows = slice(LO + 8 * half, LO + 8 * half + 8)
                        place = Z_FACE[dz].index(name) * 8 + 2 * x + half
                        posts[step, SLOT[name], x + 1, rows, :] = jnp.where(
                            lane == edge_lane(dz), unpack_z(face, place, dz), posts[step, SLOT[name], x + 1, rows, :]
                        )

        def add_x():
            for dx, end, ghost, column, names in ((1, 0, 0, NX - 1, X_UP), (-1, NX - 1, NX + 1, 0, X_DOWN)):
                for name in names:
                    if not wanted(name):
                        continue
                    _, dy, dz = VELOCITY[name[1]]
                    if dy != 0:
                        row_ghost = LO - 1 if dy == 1 else HI
                        line = post_y_got[step, SIDE[dy], xy_place(dx, not last)]
                        posts[step, SLOT[name], ghost, row_ghost : row_ghost + 1, :] = line
                    for half in range(2):
                        rows = slice(8 * half, 8 * half + 8)
                        first = LO + 8 * half - dy
                        value = posts[step, SLOT[name], ghost, first : first + 8, :]
                        if dz != 0:
                            value = value + z_columns(name, dx, column, half)
                        state[state_at(name), end, rows, :] = state[state_at(name), end, rows, :] + kept(end, rows, value)
        def add_y():
            for dy, edge in ((1, 0), (-1, NY - 1)):
                rows = slice(edge, edge + 1)
                for entry, name in enumerate(Y_FACE[dy]):
                    if name in ACROSS_YZ or not wanted(name):
                        continue
                    for x in range(NX):
                        source = x - VELOCITY[name[1]][0]
                        if not 0 <= source < NX:
                            continue
                        value = kept(x, rows, post_y_got[step, SIDE[dy], entry * 4 + source])
                        state[state_at(name), x, rows, :] = state[state_at(name), x, rows, :] + value

        def add_across():
            for name in ACROSS_YZ:
                _, dy, dz = VELOCITY[name[1]]
                entry, entry_z = Y_FACE[dy].index(name), Z_FACE[dz].index(name)
                half = 1 if dy == 1 else 0
                ghost = LO - 1 if dy == 1 else HI
                for x in range(NX):
                    corner = unpack_z(post_row_got[step, SIDE[dy], SIDE[dz], 0], entry_z * 8 + 2 * x + half, dz)
                    line = jnp.where(row_lane == edge_lane(dz), corner, post_y_got[step, SIDE[dy], entry * 4 + x])
                    posts[step, SLOT[name], x + 1, ghost : ghost + 1, :] = line

        return add_x, add_y, add_z, add_across

    shifted_scalars = {0: scalars, 1: scalars_down, -1: scalars_up}

    def add_up(step, packed):
        up, down = packed
        for x in range(NX):
            for place, kind in enumerate(("r", "b")):
                total = posts[step, SLOT[(kind, 0)], x + 1, LO:HI, :]
                for number in range(1, 7):
                    dx, dy, dz = VELOCITY[number]
                    plane = x + 1 - dx
                    opened = shifted_scalars[dz][0, plane, LO - dy : HI - dy, :] > 0.0
                    back = (kind, OPPOSITE[number])
                    if dz != 0:
                        bounced = unrolled[UNROLLED[back], x]
                    else:
                        bounced = posts[step, SLOT[back], x + 1, LO:HI, :]
                    if 1 <= plane <= NX:
                        arriving = posts[step, SLOT[(kind, number)], plane, LO - dy : HI - dy, :]
                    else:
                        arriving = 0.0
                    total = total + jnp.where(opened, arriving, bounced)
                partial[place, x] = total
                for half in range(2):
                    tile = total[8 * half : 8 * half + 8]
                    lanes = SUM_Z + 8 * place + 2 * x + half
                    up, down = pack_z(tile, lanes, 1, up), pack_z(tile, lanes, -1, down)
                for dx, end in ((1, NX - 1), (-1, 0)):
                    if x == end:
                        post_part[step, SIDE[dx], NY * place : NY * place + NY, :] = total
                for dy, edge in ((1, NY - 1), (-1, 0)):
                    post_y[step, SIDE[dy], SUM_Y + 4 * place + x] = partial[place, x, edge : edge + 1, :]
                for dy, half in ((1, 1), (-1, 0)):
                    rows = slice(LO + 8 * half, LO + 8 * half + 8)
                    tile = posts[step, SLOT[(kind, FACE[(1, dy)])], x + 1, rows, :]
                    lanes = Y_Z + 8 * place + 2 * x + (0 if dy == 1 else 1)
                    up, down = pack_z(tile, lanes, 1, up), pack_z(tile, lanes, -1, down)
        for place, kind in enumerate(("r", "b")):
            for dx, end in ((1, NX - 1), (-1, 0)):
                slot = SLOT[(kind, FACE[(0, dx)])]
                for half in range(2):
                    tile = posts[step, slot, end + 1, LO + 8 * half : LO + 8 * half + 8, :]
                    lanes = X_Z + 8 * place + (0 if dx == 1 else 6) + half
                    up, down = pack_z(tile, lanes, 1, up), pack_z(tile, lanes, -1, down)
                for dy, edge in ((1, HI - 1), (-1, LO)):
                    line = posts[step, slot, end + 1, edge : edge + 1, :]
                    post_y[step, SIDE[dy], X_Y + 2 * SIDE[dx] + place] = line
                    post_xy[step, SIDE[dx], SIDE[dy], X_XY + place] = line
                    post_xy[step, SIDE[dx], SIDE[dy], SUM_XY + place] = partial[place, end, edge - LO : edge - LO + 1, :]
                    line = posts[step, SLOT[(kind, FACE[(1, dy)])], end + 1, edge : edge + 1, :]
                    post_xy[step, SIDE[dx], SIDE[dy], Y_XY + place] = line
                    part = Y_PART + 2 * SIDE[dy] + place
                    post_part[step, SIDE[dx], part : part + 1, :] = line
        return up, down

    def put_edges(step, packed, fused):
        for dx, end in ((1, NX - 1), (-1, 0)):
            for dy, edge in ((1, HI - 1), (-1, LO)):
                slot = SLOT[("f", VELOCITY.index((dx, dy, 0)))]
                post_xy[step, SIDE[dx], SIDE[dy], 0] = posts[step, slot, end + 1, edge : edge + 1, :]
            if fused:
                both = jnp.where(lane < 64, packed[0], pltpu.roll(packed[1], 64, axis=1))
                post_part[step, SIDE[dx], Z_PART : Z_PART + 8, :] = both
        for dz in (1, -1):
            post_z[step, SIDE[dz]] = packed[SIDE[dz]]
            for dy, edge in ((1, 7), (-1, 0)):
                line = post_z[step, SIDE[dz], edge : edge + 1, :]
                post_row[step, SIDE[dy], SIDE[dz], 0] = line
                if fused:
                    post_y[step, SIDE[dy], Z_Y + SIDE[dz]] = line

    def turned(value, lanes):
        return pltpu.roll(value, 128 - lanes, axis=1)

    def ratio(red, blue):
        return (red - blue) / (red + blue)

    def packed_ratio(sums):
        blue = turned(sums, 8)
        return ratio(sums, blue)

    def finish_phase(step, planes=(), corners=False):
        inside = len(planes) > 0
        here_ = step + 2

        def put(target, entry, plane, rows, value):
            fluid = shifted_scalars[target][0, plane, rows, :] > 0.0
            shifted_scalars[target][entry, plane, rows, :] = jnp.where(fluid, value, WETTING)

        interior = slice(LO, HI)
        z_got = {(dx, dz): post_z_got[step, SIDE[dz], TURN[dx]] for dx in (-1, 0, 1) for dz in (1, -1)}
        row_got = {
            (dx, dy, dz): post_row_got[step, SIDE[dy], SIDE[dz], TURN[dx]]
            for dx in (() if inside else (-1, 0, 1) if corners else (0,))
            for dy in (1, -1)
            for dz in (1, -1)
        }

        def xy_got(dx, dy, line):
            return post_y_got[step, SIDE[dy], ROWS_Y + ROWS_XY * SIDE[dx] + line]

        def with_columns(value, place, column, dx):
            halves = []
            for half in range(2):
                tile = value[8 * half : 8 * half + 8]
                for dz in (1, -1):
                    lanes = IN_Z + 8 * place + 2 * column + half
                    tile = tile + jnp.where(lane == edge_lane(dz), unpack_z(z_got[(dx, dz)], lanes, dz), 0.0)
                halves.append(tile)
            return jnp.concatenate(halves, axis=0)

        def with_rows(value, rows):
            for dy, edge in ((1, 0), (-1, NY - 1)):
                value = value + jnp.where(wide_row == edge, rows[dy], 0.0)
            return value

        def with_ends(line, offset, place, x):
            dx, dy = offset
            half = 1 if dy == 1 else 0
            for dz in (1, -1):
                lanes = IN_Z + 8 * place + 2 * x + half
                line = line + jnp.where(row_lane == edge_lane(dz), unpack_z(row_got[(dx, dy, dz)], lanes, dz), 0.0)
            return line

        for x in planes:
            sums = []
            for place, kind in enumerate(("r", "b")):
                total = partial[place, x]
                for dx, end, ghost in ((1, 0, 0), (-1, NX - 1, NX + 1)):
                    if x == end:
                        total = total + posts[step, SLOT[(kind, FACE[(0, dx)])], ghost, interior, :]
                rows = {}
                for dy in (1, -1):
                    entry = Y_FACE[dy].index((kind, FACE[(1, dy)]))
                    rows[dy] = post_y_got[step, SIDE[dy], entry * 4 + x]
                total = with_columns(with_rows(total, rows), place, x, 0)
                colour[place, x] = total
                sums.append(total)
            put(0, here_, x + 1, interior, ratio(*sums))
        if inside:
            return
        for dx, ghost, end, column in ((1, 0, 0, NX - 1), (-1, NX + 1, NX - 1, 0)):
            sums = []
            lines = {1: [], -1: []}
            for place, kind in enumerate(("r", "b")):
                if not corners:
                    total = post_part_got[step, SIDE[dx], NY * place : NY * place + NY, :]
                    total = total + posts[step, SLOT[(kind, FACE[(0, -dx)])], end + 1, interior, :]
                    rows = {dy: xy_got(dx, dy, Y_XY + place) for dy in (1, -1)}
                    sums.append(with_columns(with_rows(total, rows), place, column, dx))
                    continue
                for dy in (1, -1):
                    part = Y_PART + 2 * SIDE[-dy] + place
                    line = (
                        xy_got(dx, dy, SUM_XY + place)
                        + post_part_got[step, SIDE[dx], part : part + 1, :]
                        + post_y_got[step, SIDE[dy], X_Y + 2 * SIDE[-dx] + place]
                    )
                    lines[dy].append(with_ends(line, (dx, dy), place, column))
            if not corners:
                put(0, here_, ghost, interior, ratio(*sums))
                continue
            for dy, row_ghost in ((1, LO - 1), (-1, HI)):
                put(0, here_, ghost, slice(row_ghost, row_ghost + 1), ratio(*lines[dy]))
        for dy, row_ghost, edge in ((1, LO - 1, LO), (-1, HI, HI - 1)):
            for x in () if corners else range(NX):
                sums = []
                for place, kind in enumerate(("r", "b")):
                    line = post_y_got[step, SIDE[dy], SUM_Y + 4 * place + x]
                    line = line + posts[step, SLOT[(kind, FACE[(1, -dy)])], x + 1, edge : edge + 1, :]
                    for dx, end in ((1, 0), (-1, NX - 1)):
                        if x == end:
                            line = line + xy_got(dx, dy, X_XY + place)
                    sums.append(with_ends(line, (0, dy), place, x))
                put(0, here_, x + 1, slice(row_ghost, row_ghost + 1), ratio(*sums))
        low_x, high_x = lane % 8 < 2, lane % 8 >= 6
        first_y, last_y = (row == 0) & (lane % 2 == 0), (row == 7) & (lane % 2 == 1)
        row_low_x, row_high_x = row_lane % 8 < 2, row_lane % 8 >= 6
        for dz in (1, -1):

            def with_y(sums, dx):
                sums = sums + jnp.where(first_y, turned(row_got[(dx, 1, dz)], Y_Z), 0.0)
                return sums + jnp.where(last_y, turned(row_got[(dx, -1, dz)], Y_Z), 0.0)

            faces = {}
            if not corners:
                sums = turned(z_got[(0, dz)], SUM_Z) + turned(post_z[step, SIDE[-dz]], IN_Z)
                sums = sums + jnp.where(low_x, turned(z_got[(1, dz)], X_Z), 0.0)
                sums = sums + jnp.where(high_x, turned(z_got[(-1, dz)], X_Z), 0.0)
                faces[0] = packed_ratio(with_y(sums, 0))
            for dx in (1, -1) if corners else ():
                sums = turned(z_got[(dx, dz)], SUM_Z) + turned(z_got[(0, dz)], X_Z)
                sums = sums + turned(post_part_got[step, SIDE[dx], Z_PART : Z_PART + 8, :], IN_Z + 64 * SIDE[-dz])
                faces[dx] = packed_ratio(with_y(sums, dx))
            for plane in (0, NX + 1) if corners else range(1, NX + 1):
                dx, column = {0: (1, NX - 1), NX + 1: (-1, 0)}.get(plane, (0, plane - 1))
                for half in range(2):
                    rows = slice(LO + 8 * half, LO + 8 * half + 8)
                    value = scalars[here_, plane, rows, :]
                    ghost = unpack_z(faces[dx], 2 * column + half, dz)
                    value = jnp.where(lane == edge_lane(dz), ghost, pltpu.roll(value, 1 if dz == 1 else 127, axis=1))
                    put(dz, 1, plane, rows, value)
            for dy, row_ghost in ((1, LO - 1), (-1, HI)):
                half = 1 if dy == 1 else 0
                edge = 0 if dy == 1 else 7
                sums = turned(row_got[(0, dy, dz)], SUM_Z)
                sums = sums + turned(post_y_got[step, SIDE[dy], Z_Y + SIDE[-dz]], IN_Z)
                sums = sums + turned(post_z_got[step, SIDE[dz], 0, edge : edge + 1, :], Y_Z)
                if corners:
                    sums = sums + jnp.where(row_low_x, turned(row_got[(1, dy, dz)], X_Z), 0.0)
                    sums = sums + jnp.where(row_high_x, turned(row_got[(-1, dy, dz)], X_Z), 0.0)
                corner = packed_ratio(sums)
                for x in (0, NX - 1) if corners else range(1, NX - 1):
                    line = scalars[here_, x + 1, row_ghost : row_ghost + 1, :]
                    line = pltpu.roll(line, 1 if dz == 1 else 127, axis=1)
                    line = jnp.where(row_lane == edge_lane(dz), unpack_z(corner, 2 * x + half, dz), line)
                    put(dz, 1, x + 1, slice(row_ghost, row_ghost + 1), line)

    blank = jnp.zeros((8, NZ), jnp.float32)

    def first_phase(x, packed):
        fluid = 1.0 - solid[x].astype(jnp.float32)
        phase = jnp.where(fluid > 0.0, -0.9 + 1.8 * labels[x].astype(jnp.float32), WETTING)
        return set_phase(x, [fluid, phase], packed)

    barrier = pltpu.get_barrier_semaphore()

    def greet(dy, dz):
        for dx in (0, 1, -1) if 0 in (dy, dz) else (0,):
            pl.semaphore_signal(barrier, inc=1, device_id=neighbour((dx, dy, dz)), device_id_type=MESH)

    by_class(greet)
    for dx in (1, -1):
        pl.semaphore_signal(barrier, inc=1, device_id=neighbour((dx, 0, 0)), device_id_type=MESH)
    beside_y = 2 - closed[(1, 1)].astype(jnp.int32) - closed[(1, -1)].astype(jnp.int32)
    beside_z = 2 - closed[(2, 1)].astype(jnp.int32) - closed[(2, -1)].astype(jnp.int32)
    beside = 2 + 3 * (beside_y + beside_z) + beside_y * beside_z

    zero_rows[...] = jnp.zeros((ROWS_Y_ALL, 1, NZ), jnp.float32)
    zero_tiles[...] = jnp.zeros((3, 8, NZ), jnp.float32)

    def clear(dy, dz):
        def fill(target, turn, place):
            source = zero_tiles if dy == 0 else zero_rows.at[pl.ds(0, target.shape[0])]
            pltpu.make_async_copy(source, target, recv_sem.at[turn, place]).start()

        fill(phase_like(dy, dz), 0, CLASS[(dy, dz)])
        for step in range(STEPS):
            fused = step < STEPS - 1
            fill(post_like(step, fused, dy, dz), step + 1, CLASS[(dy, dz)])
            if fused and dy != 0 and dz != 0:
                fill(corner_like(step, dy, dz), step + 1, CORNER_CLASS[(dy, dz)])

    for dy, dz in CLASSES:
        pl.when(jnp.logical_not(has((0, -dy, -dz))))(functools.partial(clear, dy, dz))

    for step in range(STEPS):
        for side in range(2):
            post_part[step, side, Y_PART : Y_PART + 8, :] = blank
        for name in Y_FACE[1] + Y_FACE[-1]:
            if name not in ACROSS_YZ:
                ghost = LO - 1 if VELOCITY[name[1]][1] == 1 else HI
                for plane in range(1, NX + 1):
                    posts[step, SLOT[name], plane, ghost : ghost + 1, :] = blank[0:1]

    loads[0].wait()
    loads[1].wait()
    packed = lax.fori_loop(0, NX, first_phase, (blank, blank), unroll=True)
    pl.semaphore_wait(barrier, beside)
    send_phase(packed)
    loads[2].wait()
    lax.fori_loop(0, NX, lambda x, _: relax_body(0, x, True), None, unroll=True)
    unpack_phase()

    def collide_middle(step):
        return lax.fori_loop(1, NX - 1, lambda x, p: collide_body(step, x, p), (blank, blank), unroll=True)

    def move(step, packed, fused):
        packed = lax.fori_loop(0, 2, lambda turn, p: collide_body(step, 3 - 3 * turn, p), packed, unroll=True)
        if fused:
            packed = add_up(step, packed)
        put_edges(step, packed, fused)
        by_class(functools.partial(send_post_class, step, fused), classes=ON_Y + ON_YZ)
        for dx, near, far in ((1, NX, 0), (-1, 1, NX + 1)):
            send(post_plane(step, dx, near), post_plane(step, dx, far), step + 1, X_CLASS[dx], (dx, 0, 0))
        if fused:
            by_class(functools.partial(send_corner_class, step), classes=ON_YZ)
        by_class(functools.partial(send_post_class, step, fused), classes=ON_Z)
        if fused:
            for dx in (1, -1):
                side = SIDE[dx]
                send(post_part.at[step, side], post_part_got.at[step, side], step + 1, PART_CLASS[dx], (dx, 0, 0))
        last = not fused
        stream_inside(step, 0, 1, last)
        lax.fori_loop(1, NX - 1, lambda x, _: stream_inside(step, x, 0, last), None, unroll=True)
        stream_inside(step, NX - 1, -1, last)
        await_posts(send_sem, step, fused, CLASSES, False)
        await_x(send_sem, step)
        if fused:
            await_parts(send_sem, step)
            await_corners(send_sem, step, False)
        add_x, add_y, add_z, add_across = arrivals(step, last)
        await_posts(recv_sem, step, fused, ON_Z, True)
        add_z()
        await_posts(recv_sem, step, fused, ON_Y, True)
        add_y()
        if fused:
            finish_phase(step, (1, 2))
        await_posts(recv_sem, step, fused, ON_YZ, True)
        add_across()
        lax.fori_loop(0, NX, lambda x, _: stream_across(step, x, last), None, unroll=True)
        if fused:
            lax.fori_loop(1, 3, lambda x, _: relax_body(step + 1, x, False), None, unroll=True)
        await_x(recv_sem, step)
        add_x()
        if fused:
            finish_phase(step, (0, 3))
            lax.fori_loop(0, 2, lambda turn, _: relax_body(step + 1, 3 - 3 * turn, False), None, unroll=True)
            await_parts(recv_sem, step)
            finish_phase(step)
            packed = collide_middle(step + 1)
            await_corners(recv_sem, step, True)
            finish_phase(step, corners=True)
        return packed

    packed = lax.fori_loop(0, STEPS - 1, lambda step, p: move(step, p, True), collide_middle(0))
    move(STEPS - 1, packed, False)


def hand_out(every, momentum_out, red_out, blue_out, sem):
    copies = []
    first = 0
    for place, target in enumerate((momentum_out, red_out, blue_out)):
        count = target.shape[0]
        copies.append(pltpu.make_async_copy(every.at[pl.ds(first, count)], target, sem.at[place]))
        first += count
    for copy in copies:
        copy.start()
    for copy in copies:
        copy.wait()


def shards(sizes, momentum_sets, labels, solid_mask):
    block = (NX, NY, NZ)
    f32 = jnp.float32
    vmem = lambda *shape, dtype=f32: pltpu.VMEM(shape, dtype)
    every = pl.pallas_call(
        functools.partial(kernel, sizes=sizes),
        out_shape=vmem(33, *block),
        in_specs=[pl.BlockSpec(memory_space=pltpu.HBM)] * 3,
        out_specs=pl.BlockSpec(memory_space=pltpu.VMEM),
        scratch_shapes=[
            vmem(*block, dtype=jnp.int32),
            vmem(*block, dtype=jnp.int32),
            vmem(1 + STEPS, NX + 2, ROWS, NZ),
            vmem(2, NX + 2, ROWS, NZ),
            vmem(2, NX + 2, ROWS, NZ),
            vmem(STEPS, 33, NX + 2, ROWS, NZ),
            vmem(14, *block),
            vmem(3, *block),
            vmem(2, *block),
            vmem(2, 8, 1, NZ),
            vmem(2, 8, NZ),
            vmem(2, 2, 1, 1, NZ),
            vmem(2, 12, 1, NZ),
            vmem(2, 3, 8, NZ),
            vmem(2, 2, 1, 1, NZ),
            vmem(STEPS, 2, ROWS_Y, 1, NZ),
            vmem(STEPS, 2, 8, NZ),
            vmem(STEPS, 2, 2, 1, 1, NZ),
            vmem(STEPS, 2, 2, ROWS_XY, 1, NZ),
            vmem(STEPS, 2, ROWS_PART, NZ),
            vmem(STEPS, 2, ROWS_Y_ALL, 1, NZ),
            vmem(STEPS, 2, 3, 8, NZ),
            vmem(STEPS, 2, 2, 3, 1, NZ),
            vmem(STEPS, 2, ROWS_PART, NZ),
            vmem(2, *block),
            vmem(ROWS_Y_ALL, 1, NZ),
            vmem(3, 8, NZ),
            pltpu.SemaphoreType.DMA((3,)),
            pltpu.SemaphoreType.DMA((1 + STEPS, 16)),
            pltpu.SemaphoreType.DMA((1 + STEPS, 16)),
        ],
        compiler_params=pltpu.CompilerParams(
            collective_id=0, has_side_effects=True, vmem_limit_bytes=VMEM_LIMIT
        ),
        cost_estimate=pl.CostEstimate(flops=15_000_000, bytes_accessed=1_800_000, transcendentals=0),
    )(*(pltpu.with_memory_space_constraint(array, pltpu.HBM) for array in (momentum_sets, labels, solid_mask)))
    return pl.pallas_call(
        hand_out,
        out_shape=[jax.ShapeDtypeStruct((count,) + block, f32) for count in (19, 7, 7)],
        in_specs=[pl.BlockSpec(memory_space=pltpu.VMEM)],
        out_specs=[pl.BlockSpec(memory_space=pltpu.HBM)] * 3,
        scratch_shapes=[pltpu.SemaphoreType.DMA((3,))],
        cost_estimate=pl.CostEstimate(flops=0, bytes_accessed=2_200_000, transcendentals=0),
    )(pltpu.with_memory_space_constraint(every, pltpu.VMEM))


def solution(mesh):
    sizes = tuple(mesh.shape[axis] for axis in ("flow", "gy", "gz"))
    split = P("flow", "gy", "gz")
    split_sets = P(None, "flow", "gy", "gz")
    return jax.shard_map(
        functools.partial(shards, sizes),
        mesh=mesh,
        in_specs=(split_sets, split, split),
        out_specs=(split_sets, split_sets, split_sets),
        check_vma=False,
    )
```

```python
import functools

import jax
import jax.numpy as jnp
from jax import lax
from jax.experimental import pallas as pl
from jax.experimental.pallas import tpu as pltpu
from jax.sharding import PartitionSpec as P

STEPS = 3
NX, NY, NZ = 4, 16, 128
LO, HI = 8, 8 + NY
ROWS = 32
WETTING = 0.3
TENSION = 0.05
MESH = pl.DeviceIdType.MESH
VMEM_LIMIT = 40 * 1024 * 1024

VELOCITY = (
    (0, 0, 0),
    (1, 0, 0),
    (-1, 0, 0),
    (0, 1, 0),
    (0, -1, 0),
    (0, 0, 1),
    (0, 0, -1),
    (1, 1, 0),
    (-1, -1, 0),
    (1, -1, 0),
    (-1, 1, 0),
    (1, 0, 1),
    (-1, 0, -1),
    (1, 0, -1),
    (-1, 0, 1),
    (0, 1, 1),
    (0, -1, -1),
    (0, 1, -1),
    (0, -1, 1),
)
OPPOSITE = (0, 2, 1, 4, 3, 6, 5, 8, 7, 10, 9, 12, 11, 14, 13, 16, 15, 18, 17)
PAIRS = ((1, 2), (3, 4), (5, 6), (7, 8), (9, 10), (11, 12), (13, 14), (15, 16), (17, 18))

X_UP = [("f", i) for i in (1, 7, 9, 11, 13)] + [("r", 1), ("b", 1)]
X_DOWN = [("f", i) for i in (2, 8, 10, 12, 14)] + [("r", 2), ("b", 2)]
EVERY = [("f", i) for i in range(19)] + [("r", i) for i in range(7)] + [("b", i) for i in range(7)]
ORDER = X_UP + X_DOWN + [name for name in EVERY if name not in X_UP + X_DOWN]
SLOT = {name: place for place, name in enumerate(ORDER)}
Y_FACE = {
    1: (("f", 3), ("r", 3), ("f", 7), ("f", 10), ("f", 15), ("f", 17), ("b", 3)),
    -1: (("f", 4), ("r", 4), ("f", 9), ("f", 8), ("f", 18), ("f", 16), ("b", 4)),
}
Z_FACE = {
    1: (("f", 5), ("f", 11), ("f", 14), ("f", 15), ("f", 18), ("r", 5), ("b", 5)),
    -1: (("f", 6), ("f", 13), ("f", 12), ("f", 17), ("f", 16), ("r", 6), ("b", 6)),
}
Z_MOVING = Z_FACE[1] + Z_FACE[-1]
UNROLLED = {name: place for place, name in enumerate(Z_MOVING)}
DIRECTIONS = VELOCITY[1:]
CORNERS = tuple((a, b, c) for a in (1, -1) for b in (1, -1) for c in (1, -1))
NEIGHBOURS = DIRECTIONS + CORNERS
SIDE = {1: 0, -1: 1}
TURN = {0: 0, 1: 1, -1: 2}
FACE = {(1, 1): 3, (1, -1): 4, (0, 1): 1, (0, -1): 2, (2, 1): 5, (2, -1): 6}
IN_Z, SUM_Z, X_Z, Y_Z = 40, 56, 72, 88
SUM_Y, X_Y, Z_Y, ROWS_Y = 28, 36, 40, 42
Y_XY, SUM_XY, X_XY, ROWS_XY = 1, 3, 5, 7
ROWS_Y_ALL = ROWS_Y + 2 * ROWS_XY
Y_PART, Z_PART, ROWS_PART = 32, 40, 48
ON_Y, ON_Z = ((1, 0), (-1, 0)), ((0, 1), (0, -1))
ON_YZ = ((1, 1), (1, -1), (-1, 1), (-1, -1))
CLASSES = ON_YZ + ON_Y + ON_Z
CLASS = {way: place for place, way in enumerate(CLASSES)}
X_CLASS = {1: 8, -1: 9}
PART_CLASS = {1: 10, -1: 11}
CORNER_CLASS = {way: 12 + place for place, way in enumerate(ON_YZ)}
ACROSS_YZ = tuple(("f", number) for number in (15, 16, 17, 18))


def kernel(
    momentum_in,
    labels_in,
    solid_in,
    state,
    labels,
    solid,
    scalars,
    scalars_down,
    scalars_up,
    posts,
    unrolled,
    speed,
    colour,
    phase_y,
    phase_z,
    phase_yz,
    phase_y_got,
    phase_z_got,
    phase_yz_got,
    post_y,
    post_z,
    post_row,
    post_xy,
    post_part,
    post_y_got,
    post_z_got,
    post_row_got,
    post_part_got,
    partial,
    in_sem,
    send_sem,
    recv_sem,
    *,
    sizes,
):
    here = tuple(lax.axis_index(axis) for axis in ("flow", "gy", "gz"))

    flow = {
        0: here[0],
        1: jnp.where(here[0] == sizes[0] - 1, 0, here[0] + 1),
        -1: jnp.where(here[0] == 0, sizes[0] - 1, here[0] - 1),
    }
    lateral = [{0: here[axis], 1: here[axis] + 1, -1: here[axis] - 1} for axis in (1, 2)]

    def neighbour(offset):
        return (flow[offset[0]], lateral[0][offset[1]], lateral[1][offset[2]])

    closed = {
        (1, -1): here[1] == 0,
        (1, 1): here[1] == sizes[1] - 1,
        (2, -1): here[2] == 0,
        (2, 1): here[2] == sizes[2] - 1,
    }
    def has(offset):
        known = [jnp.logical_not(closed[(axis, offset[axis])]) for axis in (1, 2) if offset[axis] != 0]
        return functools.reduce(jnp.logical_and, known) if known else None

    def when(condition, action):
        if condition is None:
            action()
        else:
            pl.when(condition)(action)

    def by_class(action, backward=False, classes=CLASSES):
        for dy, dz in classes:
            when(has((0, -dy, -dz) if backward else (0, dy, dz)), functools.partial(action, dy, dz))

    lane = lax.broadcasted_iota(jnp.int32, (8, NZ), 1)
    wide_lane = lax.broadcasted_iota(jnp.int32, (NY, NZ), 1)
    wide_row = lax.broadcasted_iota(jnp.int32, (NY, NZ), 0)
    row = lax.broadcasted_iota(jnp.int32, (8, NZ), 0)
    row_lane = lax.broadcasted_iota(jnp.int32, (1, NZ), 1)

    loads = [
        pltpu.make_async_copy(solid_in, solid, in_sem.at[0]),
        pltpu.make_async_copy(labels_in, labels, in_sem.at[1]),
        pltpu.make_async_copy(momentum_in, state.at[pl.ds(0, 19)], in_sem.at[2]),
    ]
    for load in loads:
        load.start()

    def send(source, target, turn, place, offset):
        pltpu.make_async_remote_copy(
            src_ref=source,
            dst_ref=target,
            send_sem=send_sem.at[turn, place],
            recv_sem=recv_sem.at[turn, place],
            device_id=neighbour(offset),
            device_id_type=MESH,
        ).start()

    def await_bytes(sems, turn, place, like):
        pltpu.make_async_copy(like, like, sems.at[turn, place]).wait()

    def send_phase_class(dy, dz):
        place = CLASS[(dy, dz)]
        if dz == 0:
            side = SIDE[dy]
            send(phase_y.at[side], phase_y_got.at[side, pl.ds(0, 8)], 0, place, (0, dy, 0))
            for dx, line, target in ((1, 6, 8), (-1, 0, 10)):
                source = phase_y.at[side, pl.ds(line, 2)]
                send(source, phase_y_got.at[side, pl.ds(target, 2)], 0, place, (dx, dy, 0))
        elif dy == 0:
            side = SIDE[dz]
            for dx in (0, 1, -1):
                send(phase_z.at[side], phase_z_got.at[side, TURN[dx]], 0, place, (dx, 0, dz))
        else:
            sides = SIDE[dy], SIDE[dz]
            send(phase_yz.at[sides], phase_yz_got.at[sides], 0, place, (0, dy, dz))

    def phase_like(dy, dz):
        if dz == 0:
            return phase_y_got.at[SIDE[dy]]
        if dy == 0:
            return phase_z_got.at[SIDE[dz]]
        return phase_yz_got.at[SIDE[dy], SIDE[dz]]

    def phase_plane(plane):
        return scalars.at[pl.ds(0, 2), plane, pl.ds(LO, NY)]

    def post_plane(step, dx, plane):
        return posts.at[step, pl.ds(0 if dx == 1 else 7, 7), plane, pl.ds(LO, NY)]

    def xy_place(dx, fused):
        return ROWS_Y + ROWS_XY * SIDE[dx] if fused else SUM_Y + SIDE[dx]

    def send_post_class(step, fused, dy, dz):
        turn, place = step + 1, CLASS[(dy, dz)]
        if dz == 0:
            side = SIDE[dy]
            rows, rows_xy = pl.ds(0, ROWS_Y if fused else SUM_Y), ROWS_XY if fused else 1
            send(post_y.at[step, side, rows], post_y_got.at[step, side, rows], turn, place, (0, dy, 0))
            for dx in (1, -1):
                source = post_xy.at[step, SIDE[dx], side, pl.ds(0, rows_xy)]
                target = post_y_got.at[step, side, pl.ds(xy_place(dx, fused), rows_xy)]
                send(source, target, turn, place, (dx, dy, 0))
        elif dy == 0:
            side = SIDE[dz]
            for dx in (0, 1, -1):
                send(post_z.at[step, side], post_z_got.at[step, side, TURN[dx]], turn, place, (dx, 0, dz))
        else:
            sides = SIDE[dy], SIDE[dz]
            target = post_row_got.at[step, sides[0], sides[1], pl.ds(0, 1)]
            send(post_row.at[step, sides[0], sides[1]], target, turn, place, (0, dy, dz))

    def send_corner_class(step, dy, dz):
        sides = SIDE[dy], SIDE[dz]
        for dx in (1, -1):
            target = post_row_got.at[step, sides[0], sides[1], pl.ds(TURN[dx], 1)]
            send(post_row.at[step, sides[0], sides[1]], target, step + 1, CORNER_CLASS[(dy, dz)], (dx, dy, dz))

    def post_like(step, fused, dy, dz):
        if dz == 0:
            return post_y_got.at[step, SIDE[dy], pl.ds(0, ROWS_Y_ALL if fused else SUM_Y + 2)]
        if dy == 0:
            return post_z_got.at[step, SIDE[dz]]
        return post_row_got.at[step, SIDE[dy], SIDE[dz], pl.ds(0, 1)]

    def corner_like(step, dy, dz):
        return post_row_got.at[step, SIDE[dy], SIDE[dz], pl.ds(1, 2)]

    def await_posts(sems, step, fused, classes, backward):
        by_class(
            lambda dy, dz: await_bytes(sems, step + 1, CLASS[(dy, dz)], post_like(step, fused, dy, dz)),
            backward,
            classes,
        )

    def await_corners(sems, step, backward):
        by_class(
            lambda dy, dz: await_bytes(sems, step + 1, CORNER_CLASS[(dy, dz)], corner_like(step, dy, dz)),
            backward,
            ON_YZ,
        )

    def await_x(sems, step):
        for dx in (1, -1):
            await_bytes(sems, step + 1, X_CLASS[dx], post_plane(step, dx, 0 if dx == 1 else NX + 1))

    def await_parts(sems, step):
        for dx in (1, -1):
            await_bytes(sems, step + 1, PART_CLASS[dx], post_part_got.at[step, SIDE[dx]])

    def pack_z(tile, place, sign, packed):
        moved = pltpu.roll(tile, place + 1 if sign == 1 else place, axis=1)
        return jnp.where(lane == place, moved, packed)

    def unpack_z(packed, place, sign):
        return pltpu.roll(packed, (128 - place) % 128 if sign == 1 else 127 - place, axis=1)

    def edge_lane(sign):
        return 0 if sign == 1 else NZ - 1

    def set_phase(x, values, packed):
        up, down = packed
        for entry, value in enumerate(values):
            scalars[entry, x + 1, LO:HI, :] = value
            for dy, edge in ((1, HI - 1), (-1, LO)):
                phase_y[SIDE[dy], x * 2 + entry] = scalars[entry, x + 1, edge : edge + 1, :]
            for half in range(2):
                tile = value[8 * half : 8 * half + 8]
                place = entry * 8 + 2 * x + half
                up = pack_z(tile, place, 1, up)
                down = pack_z(tile, place, -1, down)
        return up, down

    def send_phase(packed):
        for dz in (1, -1):
            phase_z[SIDE[dz]] = packed[SIDE[dz]]
            for dy, edge in ((1, 7), (-1, 0)):
                phase_yz[SIDE[dy], SIDE[dz]] = phase_z[SIDE[dz], edge : edge + 1, :]
        by_class(send_phase_class)
        for dx, near, far in ((1, NX, 0), (-1, 1, NX + 1)):
            send(phase_plane(near), phase_plane(far), 0, X_CLASS[dx], (dx, 0, 0))

    def unpack_phase():
        first, count = 0, 2
        fills = (0.0, WETTING)
        shifted = {1: scalars_down, -1: scalars_up}

        def place_of(entry):
            return entry

        def cover(offset, value, fill):
            for axis in (1, 2):
                if offset[axis] != 0:
                    value = jnp.where(closed[(axis, -offset[axis])], fill, value)
            return value

        def arrive(sems, backward):
            by_class(lambda dy, dz: await_bytes(sems, 0, CLASS[(dy, dz)], phase_like(dy, dz)), backward)
            for dx in (1, -1):
                await_bytes(sems, 0, X_CLASS[dx], phase_plane(0))

        def shift_plane(entry, plane, dz, face, column):
            for half in range(2):
                rows = slice(LO + 8 * half, LO + 8 * half + 8)
                value = scalars[first + entry, plane, rows, :]
                place = entry * 8 + 2 * column + half
                ghost = cover((0, 0, dz), unpack_z(face, place, dz), fills[entry])
                shifted[dz][place_of(entry), plane, rows, :] = jnp.where(
                    lane == edge_lane(dz), ghost, pltpu.roll(value, 1 if dz == 1 else 127, axis=1)
                )

        arrive(send_sem, False)
        arrive(recv_sem, True)
        for dz in (1, -1):
            face = phase_z_got[SIDE[dz], 0]
            for entry in range(count):
                for x in range(NX):
                    shift_plane(entry, x + 1, dz, face, x)
        for dy, ghost in ((1, LO - 1), (-1, HI)):
            half = 1 if dy == 1 else 0
            for entry in range(count):
                for x in range(NX):
                    line = cover((0, dy, 0), phase_y_got[SIDE[dy], x * count + entry], fills[entry])
                    scalars[first + entry, x + 1, ghost : ghost + 1, :] = line
                    for dz in (1, -1):
                        corner = phase_yz_got[SIDE[dy], SIDE[dz]]
                        place = entry * 8 + 2 * x + half
                        corner = cover((0, dy, dz), unpack_z(corner, place, dz), fills[entry])
                        shifted[dz][place_of(entry), x + 1, ghost : ghost + 1, :] = jnp.where(
                            row_lane == edge_lane(dz), corner, pltpu.roll(line, 1 if dz == 1 else 127, axis=1)
                        )
        for dx, plane, column in ((1, 0, NX - 1), (-1, NX + 1, 0)):
            for dy, ghost in ((1, LO - 1), (-1, HI)):
                for entry in range(count):
                    line = phase_y_got[SIDE[dy], 8 + 2 * SIDE[dx] + entry]
                    scalars[first + entry, plane, ghost : ghost + 1, :] = cover((0, dy, 0), line, fills[entry])
            for dz in (1, -1):
                for entry in range(count):
                    shift_plane(entry, plane, dz, phase_z_got[SIDE[dz], TURN[dx]], column)

    def relax_body(step, x, initial):
        total = state[0, x]
        flux = [0.0, 0.0, 0.0]
        for up, down in PAIRS:
            first, second = state[up, x], state[down, x]
            total = total + (first + second)
            difference = first - second
            for axis in range(3):
                if VELOCITY[up][axis] == 1:
                    flux[axis] = flux[axis] + difference
                elif VELOCITY[up][axis] == -1:
                    flux[axis] = flux[axis] - difference
        inverse = 1.0 / total
        velocity = [part * inverse for part in flux]
        phase = scalars[step + 1, x + 1, LO:HI, :]
        tau = 1.3 - 0.3 * phase
        rate = 1.0 / tau
        keep = 1.0 - rate
        for axis in range(3):
            speed[axis, x] = velocity[axis]
        if initial:
            red = total * (0.05 + 0.9 * labels[x].astype(jnp.float32))
            blue = total - red
            colour[0, x] = red
            colour[1, x] = blue
        shifted = [velocity[0] + tau * inverse * 0.001, velocity[1], velocity[2]]
        square = shifted[0] * shifted[0] + shifted[1] * shifted[1] + shifted[2] * shifted[2]
        scale = rate * total
        base = scale * (1.0 - 1.5 * square)
        state[0, x] = keep * state[0, x] + base * (1.0 / 3.0)
        face, edge = base * (1.0 / 18.0), base * (1.0 / 36.0)
        for up, down in PAIRS:
            along = 0.0
            for axis in range(3):
                if VELOCITY[up][axis] == 1:
                    along = along + shifted[axis]
                elif VELOCITY[up][axis] == -1:
                    along = along - shifted[axis]
            push = scale * along
            if up < 7:
                even, odd = face + 0.25 * (push * along), push * (1.0 / 6.0)
            else:
                even, odd = edge + 0.125 * (push * along), push * (1.0 / 12.0)
            state[up, x] = keep * state[up, x] + (even + odd)
            state[down, x] = keep * state[down, x] + (even - odd)

    def gradient_at(step, x):
        def at(buffer, place, plane, dy):
            return buffer[place, plane, LO + dy : HI + dy, :]

        here_ = step + 1

        def spread(plane):
            return (
                2.0 * at(scalars, here_, plane, 0)
                + (at(scalars, here_, plane, 1) + at(scalars, here_, plane, -1))
                + (at(scalars_up, 1, plane, 0) + at(scalars_down, 1, plane, 0))
            )

        def slope_y(plane):
            return at(scalars, here_, plane, 1) - at(scalars, here_, plane, -1)

        def slope_z(plane):
            return at(scalars_up, 1, plane, 0) - at(scalars_down, 1, plane, 0)

        low, mid, high = x, x + 1, x + 2
        up_up, up_down = at(scalars_up, 1, mid, 1), at(scalars_up, 1, mid, -1)
        down_up, down_down = at(scalars_down, 1, mid, 1), at(scalars_down, 1, mid, -1)
        along_x = spread(high) - spread(low)
        along_y = 2.0 * slope_y(mid) + (slope_y(high) + slope_y(low)) + ((up_up - up_down) + (down_up - down_down))
        along_z = 2.0 * slope_z(mid) + (slope_z(high) + slope_z(low)) + ((up_up - down_up) + (up_down - down_down))
        return [part * (1.0 / 12.0) for part in (along_x, along_y, along_z)]

    def put_post(step, x, name, value, packed, fluid=None):
        kind, number = name
        offset = VELOCITY[number]
        value = jnp.where(fluid, value, 0.0)
        if offset[1] != 0:
            sign = offset[1]
            edge = HI - 1 if sign == 1 else LO
        up, down = packed
        if offset[2] != 0:
            unrolled[UNROLLED[name], x] = value
            sign_z = offset[2]
            first = Z_FACE[sign_z].index(name) * 8
            for half in range(2):
                tile = value[8 * half : 8 * half + 8]
                place = first + 2 * x + half
                if sign_z == 1:
                    up = pack_z(tile, place, 1, up)
                else:
                    down = pack_z(tile, place, -1, down)
            value = pltpu.roll(value, 1 if sign_z == 1 else 127, axis=1)
            if name not in ACROSS_YZ:
                value = jnp.where(wide_lane == edge_lane(sign_z), 0.0, value)
        posts[step, SLOT[name], x + 1, LO:HI, :] = value
        if offset[1] != 0:
            line = Y_FACE[sign].index(name) * 4 + x
            post_y[step, SIDE[sign], line] = posts[step, SLOT[name], x + 1, edge : edge + 1, :]
        return up, down

    def collide_body(step, x, packed):
        gradient = gradient_at(step, x)
        squares = [part * part for part in gradient]
        total = squares[0] + squares[1] + squares[2]
        fluid = scalars[0, x + 1, LO:HI, :] > 0.0
        packed = put_post(step, x, ("f", 0), state[0, x], packed, fluid)
        third = total * (1.0 / 3.0)
        for up, down in PAIRS:
            if up < 7:
                surface = (TENSION / 18.0) * (squares[(up - 1) // 2] - third)
            else:
                slope = 0.0
                for axis in range(3):
                    if VELOCITY[up][axis] == 1:
                        slope = slope + gradient[axis]
                    elif VELOCITY[up][axis] == -1:
                        slope = slope - gradient[axis]
                surface = (TENSION / 36.0) * (slope * slope - 2.0 * third)
            packed = put_post(step, x, ("f", up), state[up, x] + surface, packed, fluid)
            packed = put_post(step, x, ("f", down), state[down, x] + surface, packed, fluid)
        red, blue = colour[0, x], colour[1, x]
        mixing = (0.5 * 0.125) * (red * blue / (red + blue)) * lax.rsqrt(jnp.maximum(total, 0.01))
        packed = put_post(step, x, ("r", 0), 0.25 * red, packed, fluid)
        packed = put_post(step, x, ("b", 0), 0.25 * blue, packed, fluid)
        for axis in range(3):
            drift = 0.5 * speed[axis, x]
            across = mixing * gradient[axis]
            for kind, amount, turn in (("r", red, 1.0), ("b", blue, -1.0)):
                mean = 0.125 * amount
                lean = amount * drift + turn * across
                packed = put_post(step, x, (kind, 2 * axis + 1), mean + lean, packed, fluid)
                packed = put_post(step, x, (kind, 2 * axis + 2), mean - lean, packed, fluid)
        return packed

    def state_at(name):
        return {"f": 0, "r": 19, "b": 26}[name[0]] + name[1]

    def opened_at(x, offset):
        dx, dy, dz = offset
        return shifted_scalars[dz][0, x + 1 - dx, LO - dy : HI - dy, :] > 0.0

    def bounced_at(step, x, name):
        back = (name[0], OPPOSITE[name[1]])
        if VELOCITY[name[1]][2] != 0:
            return unrolled[UNROLLED[back], x]
        return posts[step, SLOT[back], x + 1, LO:HI, :]

    def stream_inside(step, x, end, last):
        fluid = scalars[0, x + 1, LO:HI, :] > 0.0
        names = [name for name in EVERY if (last or name[0] == "f") and name not in ACROSS_YZ]
        for name in names:
            dx, dy, dz = VELOCITY[name[1]]
            if name[1] == 0:
                value = posts[step, SLOT[name], x + 1, LO:HI, :]
            else:
                if dx != 0 and dx == end:
                    arriving = 0.0
                else:
                    arriving = posts[step, SLOT[name], x + 1 - dx, LO - dy : HI - dy, :]
                value = jnp.where(opened_at(x, (dx, dy, dz)), arriving, bounced_at(step, x, name))
            state[state_at(name), x] = jnp.where(fluid, value, 0.0) if last else value

    def stream_across(step, x, last):
        fluid = scalars[0, x + 1, LO:HI, :] > 0.0
        for name in ACROSS_YZ:
            dx, dy, dz = VELOCITY[name[1]]
            arriving = posts[step, SLOT[name], x + 1, LO - dy : HI - dy, :]
            value = jnp.where(opened_at(x, (dx, dy, dz)), arriving, bounced_at(step, x, name))
            state[state_at(name), x] = jnp.where(fluid, value, 0.0) if last else value

    def arrivals(step, last):
        def wanted(name):
            return last or name[0] == "f"

        def kept(x, rows, value):
            if not last:
                return value
            return jnp.where(scalars[0, x + 1, LO + rows.start : LO + rows.stop, :] > 0.0, value, 0.0)

        def z_columns(name, dx, column, half):
            dz = VELOCITY[name[1]][2]
            place = Z_FACE[dz].index(name) * 8 + 2 * column + half
            face = post_z_got[step, SIDE[dz], TURN[dx]]
            return jnp.where(lane == edge_lane(dz), unpack_z(face, place, dz), 0.0)

        def add_z():
            for dz in (1, -1):
                for name in Z_FACE[dz]:
                    if name in ACROSS_YZ or not wanted(name):
                        continue
                    for x in range(NX):
                        source = x - VELOCITY[name[1]][0]
                        if not 0 <= source < NX:
                            continue
                        for half in range(2):
                            rows = slice(8 * half, 8 * half + 8)
                            value = kept(x, rows, z_columns(name, 0, source, half))
                            state[state_at(name), x, rows, :] = state[state_at(name), x, rows, :] + value
            for name in ACROSS_YZ:
                dz = VELOCITY[name[1]][2]
                face = post_z_got[step, SIDE[dz], 0]
                for x in range(NX):
                    for half in range(2):
                        rows = slice(LO + 8 * half, LO + 8 * half + 8)
                        place = Z_FACE[dz].index(name) * 8 + 2 * x + half
                        posts[step, SLOT[name], x + 1, rows, :] = jnp.where(
                            lane == edge_lane(dz), unpack_z(face, place, dz), posts[step, SLOT[name], x + 1, rows, :]
                        )

        def add_x():
            for dx, end, ghost, column, names in ((1, 0, 0, NX - 1, X_UP), (-1, NX - 1, NX + 1, 0, X_DOWN)):
                for name in names:
                    if not wanted(name):
                        continue
                    _, dy, dz = VELOCITY[name[1]]
                    if dy != 0:
                        row_ghost = LO - 1 if dy == 1 else HI
                        line = post_y_got[step, SIDE[dy], xy_place(dx, not last)]
                        posts[step, SLOT[name], ghost, row_ghost : row_ghost + 1, :] = line
                    for half in range(2):
                        rows = slice(8 * half, 8 * half + 8)
                        first = LO + 8 * half - dy
                        value = posts[step, SLOT[name], ghost, first : first + 8, :]
                        if dz != 0:
                            value = value + z_columns(name, dx, column, half)
                        state[state_at(name), end, rows, :] = state[state_at(name), end, rows, :] + kept(end, rows, value)
        def add_y():
            for dy, edge in ((1, 0), (-1, NY - 1)):
                rows = slice(edge, edge + 1)
                for entry, name in enumerate(Y_FACE[dy]):
                    if name in ACROSS_YZ or not wanted(name):
                        continue
                    for x in range(NX):
                        source = x - VELOCITY[name[1]][0]
                        if not 0 <= source < NX:
                            continue
                        value = kept(x, rows, post_y_got[step, SIDE[dy], entry * 4 + source])
                        state[state_at(name), x, rows, :] = state[state_at(name), x, rows, :] + value

        def add_across():
            for name in ACROSS_YZ:
                _, dy, dz = VELOCITY[name[1]]
                entry, entry_z = Y_FACE[dy].index(name), Z_FACE[dz].index(name)
                half = 1 if dy == 1 else 0
                ghost = LO - 1 if dy == 1 else HI
                for x in range(NX):
                    corner = unpack_z(post_row_got[step, SIDE[dy], SIDE[dz], 0], entry_z * 8 + 2 * x + half, dz)
                    line = jnp.where(row_lane == edge_lane(dz), corner, post_y_got[step, SIDE[dy], entry * 4 + x])
                    posts[step, SLOT[name], x + 1, ghost : ghost + 1, :] = line

        return add_x, add_y, add_z, add_across

    shifted_scalars = {0: scalars, 1: scalars_down, -1: scalars_up}

    def add_up(step, packed):
        up, down = packed
        for x in range(NX):
            for place, kind in enumerate(("r", "b")):
                total = posts[step, SLOT[(kind, 0)], x + 1, LO:HI, :]
                for number in range(1, 7):
                    dx, dy, dz = VELOCITY[number]
                    plane = x + 1 - dx
                    opened = shifted_scalars[dz][0, plane, LO - dy : HI - dy, :] > 0.0
                    back = (kind, OPPOSITE[number])
                    if dz != 0:
                        bounced = unrolled[UNROLLED[back], x]
                    else:
                        bounced = posts[step, SLOT[back], x + 1, LO:HI, :]
                    if 1 <= plane <= NX:
                        arriving = posts[step, SLOT[(kind, number)], plane, LO - dy : HI - dy, :]
                    else:
                        arriving = 0.0
                    total = total + jnp.where(opened, arriving, bounced)
                partial[place, x] = total
                for half in range(2):
                    tile = total[8 * half : 8 * half + 8]
                    lanes = SUM_Z + 8 * place + 2 * x + half
                    up, down = pack_z(tile, lanes, 1, up), pack_z(tile, lanes, -1, down)
                for dx, end in ((1, NX - 1), (-1, 0)):
                    if x == end:
                        post_part[step, SIDE[dx], NY * place : NY * place + NY, :] = total
                for dy, edge in ((1, NY - 1), (-1, 0)):
                    post_y[step, SIDE[dy], SUM_Y + 4 * place + x] = partial[place, x, edge : edge + 1, :]
                for dy, half in ((1, 1), (-1, 0)):
                    rows = slice(LO + 8 * half, LO + 8 * half + 8)
                    tile = posts[step, SLOT[(kind, FACE[(1, dy)])], x + 1, rows, :]
                    lanes = Y_Z + 8 * place + 2 * x + (0 if dy == 1 else 1)
                    up, down = pack_z(tile, lanes, 1, up), pack_z(tile, lanes, -1, down)
        for place, kind in enumerate(("r", "b")):
            for dx, end in ((1, NX - 1), (-1, 0)):
                slot = SLOT[(kind, FACE[(0, dx)])]
                for half in range(2):
                    tile = posts[step, slot, end + 1, LO + 8 * half : LO + 8 * half + 8, :]
                    lanes = X_Z + 8 * place + (0 if dx == 1 else 6) + half
                    up, down = pack_z(tile, lanes, 1, up), pack_z(tile, lanes, -1, down)
                for dy, edge in ((1, HI - 1), (-1, LO)):
                    line = posts[step, slot, end + 1, edge : edge + 1, :]
                    post_y[step, SIDE[dy], X_Y + 2 * SIDE[dx] + place] = line
                    post_xy[step, SIDE[dx], SIDE[dy], X_XY + place] = line
                    post_xy[step, SIDE[dx], SIDE[dy], SUM_XY + place] = partial[place, end, edge - LO : edge - LO + 1, :]
                    line = posts[step, SLOT[(kind, FACE[(1, dy)])], end + 1, edge : edge + 1, :]
                    post_xy[step, SIDE[dx], SIDE[dy], Y_XY + place] = line
                    part = Y_PART + 2 * SIDE[dy] + place
                    post_part[step, SIDE[dx], part : part + 1, :] = line
        return up, down

    def put_edges(step, packed, fused):
        for dx, end in ((1, NX - 1), (-1, 0)):
            for dy, edge in ((1, HI - 1), (-1, LO)):
                slot = SLOT[("f", VELOCITY.index((dx, dy, 0)))]
                post_xy[step, SIDE[dx], SIDE[dy], 0] = posts[step, slot, end + 1, edge : edge + 1, :]
            if fused:
                both = jnp.where(lane < 64, packed[0], pltpu.roll(packed[1], 64, axis=1))
                post_part[step, SIDE[dx], Z_PART : Z_PART + 8, :] = both
        for dz in (1, -1):
            post_z[step, SIDE[dz]] = packed[SIDE[dz]]
            for dy, edge in ((1, 7), (-1, 0)):
                line = post_z[step, SIDE[dz], edge : edge + 1, :]
                post_row[step, SIDE[dy], SIDE[dz], 0] = line
                if fused:
                    post_y[step, SIDE[dy], Z_Y + SIDE[dz]] = line

    def turned(value, lanes):
        return pltpu.roll(value, 128 - lanes, axis=1)

    def ratio(red, blue):
        return (red - blue) / (red + blue)

    def packed_ratio(sums):
        blue = turned(sums, 8)
        return ratio(sums, blue)

    def finish_phase(step, planes=(), corners=False):
        inside = len(planes) > 0
        here_ = step + 2

        def put(target, entry, plane, rows, value):
            fluid = shifted_scalars[target][0, plane, rows, :] > 0.0
            shifted_scalars[target][entry, plane, rows, :] = jnp.where(fluid, value, WETTING)

        interior = slice(LO, HI)
        z_got = {(dx, dz): post_z_got[step, SIDE[dz], TURN[dx]] for dx in (-1, 0, 1) for dz in (1, -1)}
        row_got = {
            (dx, dy, dz): post_row_got[step, SIDE[dy], SIDE[dz], TURN[dx]]
            for dx in (() if inside else (-1, 0, 1) if corners else (0,))
            for dy in (1, -1)
            for dz in (1, -1)
        }

        def xy_got(dx, dy, line):
            return post_y_got[step, SIDE[dy], ROWS_Y + ROWS_XY * SIDE[dx] + line]

        def with_columns(value, place, column, dx):
            halves = []
            for half in range(2):
                tile = value[8 * half : 8 * half + 8]
                for dz in (1, -1):
                    lanes = IN_Z + 8 * place + 2 * column + half
                    tile = tile + jnp.where(lane == edge_lane(dz), unpack_z(z_got[(dx, dz)], lanes, dz), 0.0)
                halves.append(tile)
            return jnp.concatenate(halves, axis=0)

        def with_rows(value, rows):
            for dy, edge in ((1, 0), (-1, NY - 1)):
                value = value + jnp.where(wide_row == edge, rows[dy], 0.0)
            return value

        def with_ends(line, offset, place, x):
            dx, dy = offset
            half = 1 if dy == 1 else 0
            for dz in (1, -1):
                lanes = IN_Z + 8 * place + 2 * x + half
                line = line + jnp.where(row_lane == edge_lane(dz), unpack_z(row_got[(dx, dy, dz)], lanes, dz), 0.0)
            return line

        for x in planes:
            sums = []
            for place, kind in enumerate(("r", "b")):
                total = partial[place, x]
                for dx, end, ghost in ((1, 0, 0), (-1, NX - 1, NX + 1)):
                    if x == end:
                        total = total + posts[step, SLOT[(kind, FACE[(0, dx)])], ghost, interior, :]
                rows = {}
                for dy in (1, -1):
                    entry = Y_FACE[dy].index((kind, FACE[(1, dy)]))
                    rows[dy] = post_y_got[step, SIDE[dy], entry * 4 + x]
                total = with_columns(with_rows(total, rows), place, x, 0)
                colour[place, x] = total
                sums.append(total)
            put(0, here_, x + 1, interior, ratio(*sums))
        if inside:
            return
        for dx, ghost, end, column in ((1, 0, 0, NX - 1), (-1, NX + 1, NX - 1, 0)):
            sums = []
            lines = {1: [], -1: []}
            for place, kind in enumerate(("r", "b")):
                if not corners:
                    total = post_part_got[step, SIDE[dx], NY * place : NY * place + NY, :]
                    total = total + posts[step, SLOT[(kind, FACE[(0, -dx)])], end + 1, interior, :]
                    rows = {dy: xy_got(dx, dy, Y_XY + place) for dy in (1, -1)}
                    sums.append(with_columns(with_rows(total, rows), place, column, dx))
                    continue
                for dy in (1, -1):
                    part = Y_PART + 2 * SIDE[-dy] + place
                    line = (
                        xy_got(dx, dy, SUM_XY + place)
                        + post_part_got[step, SIDE[dx], part : part + 1, :]
                        + post_y_got[step, SIDE[dy], X_Y + 2 * SIDE[-dx] + place]
                    )
                    lines[dy].append(with_ends(line, (dx, dy), place, column))
            if not corners:
                put(0, here_, ghost, interior, ratio(*sums))
                continue
            for dy, row_ghost in ((1, LO - 1), (-1, HI)):
                put(0, here_, ghost, slice(row_ghost, row_ghost + 1), ratio(*lines[dy]))
        for dy, row_ghost, edge in ((1, LO - 1, LO), (-1, HI, HI - 1)):
            for x in () if corners else range(NX):
                sums = []
                for place, kind in enumerate(("r", "b")):
                    line = post_y_got[step, SIDE[dy], SUM_Y + 4 * place + x]
                    line = line + posts[step, SLOT[(kind, FACE[(1, -dy)])], x + 1, edge : edge + 1, :]
                    for dx, end in ((1, 0), (-1, NX - 1)):
                        if x == end:
                            line = line + xy_got(dx, dy, X_XY + place)
                    sums.append(with_ends(line, (0, dy), place, x))
                put(0, here_, x + 1, slice(row_ghost, row_ghost + 1), ratio(*sums))
        low_x, high_x = lane % 8 < 2, lane % 8 >= 6
        first_y, last_y = (row == 0) & (lane % 2 == 0), (row == 7) & (lane % 2 == 1)
        row_low_x, row_high_x = row_lane % 8 < 2, row_lane % 8 >= 6
        for dz in (1, -1):

            def with_y(sums, dx):
                sums = sums + jnp.where(first_y, turned(row_got[(dx, 1, dz)], Y_Z), 0.0)
                return sums + jnp.where(last_y, turned(row_got[(dx, -1, dz)], Y_Z), 0.0)

            faces = {}
            if not corners:
                sums = turned(z_got[(0, dz)], SUM_Z) + turned(post_z[step, SIDE[-dz]], IN_Z)
                sums = sums + jnp.where(low_x, turned(z_got[(1, dz)], X_Z), 0.0)
                sums = sums + jnp.where(high_x, turned(z_got[(-1, dz)], X_Z), 0.0)
                faces[0] = packed_ratio(with_y(sums, 0))
            for dx in (1, -1) if corners else ():
                sums = turned(z_got[(dx, dz)], SUM_Z) + turned(z_got[(0, dz)], X_Z)
                sums = sums + turned(post_part_got[step, SIDE[dx], Z_PART : Z_PART + 8, :], IN_Z + 64 * SIDE[-dz])
                faces[dx] = packed_ratio(with_y(sums, dx))
            for plane in (0, NX + 1) if corners else range(1, NX + 1):
                dx, column = {0: (1, NX - 1), NX + 1: (-1, 0)}.get(plane, (0, plane - 1))
                for half in range(2):
                    rows = slice(LO + 8 * half, LO + 8 * half + 8)
                    value = scalars[here_, plane, rows, :]
                    ghost = unpack_z(faces[dx], 2 * column + half, dz)
                    value = jnp.where(lane == edge_lane(dz), ghost, pltpu.roll(value, 1 if dz == 1 else 127, axis=1))
                    put(dz, 1, plane, rows, value)
            for dy, row_ghost in ((1, LO - 1), (-1, HI)):
                half = 1 if dy == 1 else 0
                edge = 0 if dy == 1 else 7
                sums = turned(row_got[(0, dy, dz)], SUM_Z)
                sums = sums + turned(post_y_got[step, SIDE[dy], Z_Y + SIDE[-dz]], IN_Z)
                sums = sums + turned(post_z_got[step, SIDE[dz], 0, edge : edge + 1, :], Y_Z)
                if corners:
                    sums = sums + jnp.where(row_low_x, turned(row_got[(1, dy, dz)], X_Z), 0.0)
                    sums = sums + jnp.where(row_high_x, turned(row_got[(-1, dy, dz)], X_Z), 0.0)
                corner = packed_ratio(sums)
                for x in (0, NX - 1) if corners else range(1, NX - 1):
                    line = scalars[here_, x + 1, row_ghost : row_ghost + 1, :]
                    line = pltpu.roll(line, 1 if dz == 1 else 127, axis=1)
                    line = jnp.where(row_lane == edge_lane(dz), unpack_z(corner, 2 * x + half, dz), line)
                    put(dz, 1, x + 1, slice(row_ghost, row_ghost + 1), line)

    blank = jnp.zeros((8, NZ), jnp.float32)

    def first_phase(x, packed):
        fluid = 1.0 - solid[x].astype(jnp.float32)
        phase = jnp.where(fluid > 0.0, -0.9 + 1.8 * labels[x].astype(jnp.float32), WETTING)
        return set_phase(x, [fluid, phase], packed)

    barrier = pltpu.get_barrier_semaphore()

    def greet(dy, dz):
        for dx in (0, 1, -1) if 0 in (dy, dz) else (0,):
            pl.semaphore_signal(barrier, inc=1, device_id=neighbour((dx, dy, dz)), device_id_type=MESH)

    by_class(greet)
    for dx in (1, -1):
        pl.semaphore_signal(barrier, inc=1, device_id=neighbour((dx, 0, 0)), device_id_type=MESH)
    beside_y = 2 - closed[(1, 1)].astype(jnp.int32) - closed[(1, -1)].astype(jnp.int32)
    beside_z = 2 - closed[(2, 1)].astype(jnp.int32) - closed[(2, -1)].astype(jnp.int32)
    beside = 2 + 3 * (beside_y + beside_z) + beside_y * beside_z

    def clear(dy, dz):
        for step in range(STEPS):
            if dz == 0:
                post_y_got[step, SIDE[dy]] = jnp.zeros((ROWS_Y_ALL, 1, NZ), jnp.float32)
            elif dy == 0:
                post_z_got[step, SIDE[dz]] = jnp.zeros((3, 8, NZ), jnp.float32)
            else:
                post_row_got[step, SIDE[dy], SIDE[dz]] = jnp.zeros((3, 1, NZ), jnp.float32)

    for dy, dz in CLASSES:
        pl.when(jnp.logical_not(has((0, -dy, -dz))))(functools.partial(clear, dy, dz))

    for step in range(STEPS):
        for side in range(2):
            post_part[step, side, Y_PART : Y_PART + 8, :] = blank
        for name in Y_FACE[1] + Y_FACE[-1]:
            if name not in ACROSS_YZ:
                ghost = LO - 1 if VELOCITY[name[1]][1] == 1 else HI
                for plane in range(1, NX + 1):
                    posts[step, SLOT[name], plane, ghost : ghost + 1, :] = blank[0:1]

    loads[0].wait()
    loads[1].wait()
    packed = lax.fori_loop(0, NX, first_phase, (blank, blank), unroll=True)
    pl.semaphore_wait(barrier, beside)
    send_phase(packed)
    loads[2].wait()
    lax.fori_loop(0, NX, lambda x, _: relax_body(0, x, True), None, unroll=True)
    unpack_phase()

    def collide_middle(step):
        return lax.fori_loop(1, NX - 1, lambda x, p: collide_body(step, x, p), (blank, blank), unroll=True)

    def move(step, packed, fused):
        packed = lax.fori_loop(0, 2, lambda turn, p: collide_body(step, 3 - 3 * turn, p), packed, unroll=True)
        if fused:
            packed = add_up(step, packed)
        put_edges(step, packed, fused)
        by_class(functools.partial(send_post_class, step, fused), classes=ON_Y + ON_YZ)
        if fused:
            by_class(functools.partial(send_corner_class, step), classes=ON_YZ)
        for dx, near, far in ((1, NX, 0), (-1, 1, NX + 1)):
            send(post_plane(step, dx, near), post_plane(step, dx, far), step + 1, X_CLASS[dx], (dx, 0, 0))
        by_class(functools.partial(send_post_class, step, fused), classes=ON_Z)
        if fused:
            for dx in (1, -1):
                side = SIDE[dx]
                send(post_part.at[step, side], post_part_got.at[step, side], step + 1, PART_CLASS[dx], (dx, 0, 0))
        last = not fused
        stream_inside(step, 0, 1, last)
        lax.fori_loop(1, NX - 1, lambda x, _: stream_inside(step, x, 0, last), None, unroll=True)
        stream_inside(step, NX - 1, -1, last)
        await_posts(send_sem, step, fused, CLASSES, False)
        await_x(send_sem, step)
        if fused:
            await_parts(send_sem, step)
            await_corners(send_sem, step, False)
        add_x, add_y, add_z, add_across = arrivals(step, last)
        await_posts(recv_sem, step, fused, ON_Z, True)
        add_z()
        await_posts(recv_sem, step, fused, ON_Y, True)
        add_y()
        if fused:
            finish_phase(step, (1, 2))
        await_posts(recv_sem, step, fused, ON_YZ, True)
        add_across()
        lax.fori_loop(0, NX, lambda x, _: stream_across(step, x, last), None, unroll=True)
        if fused:
            lax.fori_loop(1, 3, lambda x, _: relax_body(step + 1, x, False), None, unroll=True)
        await_x(recv_sem, step)
        add_x()
        if fused:
            finish_phase(step, (0, 3))
            lax.fori_loop(0, 2, lambda turn, _: relax_body(step + 1, 3 - 3 * turn, False), None, unroll=True)
            await_parts(recv_sem, step)
            finish_phase(step)
            packed = collide_middle(step + 1)
            await_corners(recv_sem, step, True)
            finish_phase(step, corners=True)
        return packed

    packed = lax.fori_loop(0, STEPS - 1, lambda step, p: move(step, p, True), collide_middle(0))
    move(STEPS - 1, packed, False)


def hand_out(every, momentum_out, red_out, blue_out, sem):
    copies = []
    first = 0
    for place, target in enumerate((momentum_out, red_out, blue_out)):
        count = target.shape[0]
        copies.append(pltpu.make_async_copy(every.at[pl.ds(first, count)], target, sem.at[place]))
        first += count
    for copy in copies:
        copy.start()
    for copy in copies:
        copy.wait()


def shards(sizes, momentum_sets, labels, solid_mask):
    block = (NX, NY, NZ)
    f32 = jnp.float32
    vmem = lambda *shape, dtype=f32: pltpu.VMEM(shape, dtype)
    every = pl.pallas_call(
        functools.partial(kernel, sizes=sizes),
        out_shape=vmem(33, *block),
        in_specs=[pl.BlockSpec(memory_space=pltpu.HBM)] * 3,
        out_specs=pl.BlockSpec(memory_space=pltpu.VMEM),
        scratch_shapes=[
            vmem(*block, dtype=jnp.int32),
            vmem(*block, dtype=jnp.int32),
            vmem(1 + STEPS, NX + 2, ROWS, NZ),
            vmem(2, NX + 2, ROWS, NZ),
            vmem(2, NX + 2, ROWS, NZ),
            vmem(STEPS, 33, NX + 2, ROWS, NZ),
            vmem(14, *block),
            vmem(3, *block),
            vmem(2, *block),
            vmem(2, 8, 1, NZ),
            vmem(2, 8, NZ),
            vmem(2, 2, 1, NZ),
            vmem(2, 12, 1, NZ),
            vmem(2, 3, 8, NZ),
            vmem(2, 2, 1, NZ),
            vmem(STEPS, 2, ROWS_Y, 1, NZ),
            vmem(STEPS, 2, 8, NZ),
            vmem(STEPS, 2, 2, 1, 1, NZ),
            vmem(STEPS, 2, 2, ROWS_XY, 1, NZ),
            vmem(STEPS, 2, ROWS_PART, NZ),
            vmem(STEPS, 2, ROWS_Y_ALL, 1, NZ),
            vmem(STEPS, 2, 3, 8, NZ),
            vmem(STEPS, 2, 2, 3, 1, NZ),
            vmem(STEPS, 2, ROWS_PART, NZ),
            vmem(2, *block),
            pltpu.SemaphoreType.DMA((3,)),
            pltpu.SemaphoreType.DMA((1 + STEPS, 16)),
            pltpu.SemaphoreType.DMA((1 + STEPS, 16)),
        ],
        compiler_params=pltpu.CompilerParams(
            collective_id=0, has_side_effects=True, vmem_limit_bytes=VMEM_LIMIT
        ),
        cost_estimate=pl.CostEstimate(flops=15_000_000, bytes_accessed=1_800_000, transcendentals=0),
    )(*(pltpu.with_memory_space_constraint(array, pltpu.HBM) for array in (momentum_sets, labels, solid_mask)))
    return pl.pallas_call(
        hand_out,
        out_shape=[jax.ShapeDtypeStruct((count,) + block, f32) for count in (19, 7, 7)],
        in_specs=[pl.BlockSpec(memory_space=pltpu.VMEM)],
        out_specs=[pl.BlockSpec(memory_space=pltpu.HBM)] * 3,
        scratch_shapes=[pltpu.SemaphoreType.DMA((3,))],
        cost_estimate=pl.CostEstimate(flops=0, bytes_accessed=2_200_000, transcendentals=0),
    )(pltpu.with_memory_space_constraint(every, pltpu.VMEM))


def solution(mesh):
    sizes = tuple(mesh.shape[axis] for axis in ("flow", "gy", "gz"))
    split = P("flow", "gy", "gz")
    split_sets = P(None, "flow", "gy", "gz")
    return jax.shard_map(
        functools.partial(shards, sizes),
        mesh=mesh,
        in_specs=(split_sets, split, split),
        out_specs=(split_sets, split_sets, split_sets),
        check_vma=False,
    )
```

```python
import functools

import jax
import jax.numpy as jnp
from jax import lax
from jax.experimental import pallas as pl
from jax.experimental.pallas import tpu as pltpu
from jax.sharding import PartitionSpec as P

STEPS = 3
NX, NY, NZ = 4, 16, 128
LO, HI = 8, 8 + NY
ROWS = 32
WETTING = 0.3
TENSION = 0.05
MESH = pl.DeviceIdType.MESH
VMEM_LIMIT = 40 * 1024 * 1024

VELOCITY = (
    (0, 0, 0),
    (1, 0, 0),
    (-1, 0, 0),
    (0, 1, 0),
    (0, -1, 0),
    (0, 0, 1),
    (0, 0, -1),
    (1, 1, 0),
    (-1, -1, 0),
    (1, -1, 0),
    (-1, 1, 0),
    (1, 0, 1),
    (-1, 0, -1),
    (1, 0, -1),
    (-1, 0, 1),
    (0, 1, 1),
    (0, -1, -1),
    (0, 1, -1),
    (0, -1, 1),
)
OPPOSITE = (0, 2, 1, 4, 3, 6, 5, 8, 7, 10, 9, 12, 11, 14, 13, 16, 15, 18, 17)
PAIRS = ((1, 2), (3, 4), (5, 6), (7, 8), (9, 10), (11, 12), (13, 14), (15, 16), (17, 18))

X_UP = [("f", i) for i in (1, 7, 9, 11, 13)] + [("r", 1), ("b", 1)]
X_DOWN = [("f", i) for i in (2, 8, 10, 12, 14)] + [("r", 2), ("b", 2)]
EVERY = [("f", i) for i in range(19)] + [("r", i) for i in range(7)] + [("b", i) for i in range(7)]
ORDER = X_UP + X_DOWN + [name for name in EVERY if name not in X_UP + X_DOWN]
SLOT = {name: place for place, name in enumerate(ORDER)}
Y_FACE = {
    1: (("f", 3), ("r", 3), ("f", 7), ("f", 10), ("f", 15), ("f", 17), ("b", 3)),
    -1: (("f", 4), ("r", 4), ("f", 9), ("f", 8), ("f", 18), ("f", 16), ("b", 4)),
}
Z_FACE = {
    1: (("f", 5), ("f", 11), ("f", 14), ("f", 15), ("f", 18), ("r", 5), ("b", 5)),
    -1: (("f", 6), ("f", 13), ("f", 12), ("f", 17), ("f", 16), ("r", 6), ("b", 6)),
}
Z_MOVING = Z_FACE[1] + Z_FACE[-1]
UNROLLED = {name: place for place, name in enumerate(Z_MOVING)}
DIRECTIONS = VELOCITY[1:]
CORNERS = tuple((a, b, c) for a in (1, -1) for b in (1, -1) for c in (1, -1))
NEIGHBOURS = DIRECTIONS + CORNERS
SIDE = {1: 0, -1: 1}
TURN = {0: 0, 1: 1, -1: 2}
FACE = {(1, 1): 3, (1, -1): 4, (0, 1): 1, (0, -1): 2, (2, 1): 5, (2, -1): 6}
IN_Z, SUM_Z, X_Z, Y_Z = 40, 56, 72, 88
SUM_Y, X_Y, Z_Y, ROWS_Y = 28, 36, 40, 48
Y_XY, SUM_XY, X_XY, ROWS_XY = 1, 3, 5, 8
ROWS_Y_ALL = ROWS_Y + 2 * ROWS_XY
ROWS_Y_LAST = 32
Y_PART, Z_PART, ROWS_PART = 32, 40, 48
ON_Y, ON_Z = ((1, 0), (-1, 0)), ((0, 1), (0, -1))
ON_YZ = ((1, 1), (1, -1), (-1, 1), (-1, -1))
CLASSES = ON_YZ + ON_Y + ON_Z
CLASS = {way: place for place, way in enumerate(CLASSES)}
X_CLASS = {1: 8, -1: 9}
PART_CLASS = {1: 10, -1: 11}
CORNER_CLASS = {way: 12 + place for place, way in enumerate(ON_YZ)}
ACROSS_YZ = tuple(("f", number) for number in (15, 16, 17, 18))


def kernel(
    momentum_in,
    labels_in,
    solid_in,
    state,
    labels,
    solid,
    scalars,
    scalars_down,
    scalars_up,
    posts,
    unrolled,
    speed,
    colour,
    phase_y,
    phase_z,
    phase_yz,
    phase_y_got,
    phase_z_got,
    phase_yz_got,
    post_y,
    post_z,
    post_row,
    post_xy,
    post_part,
    post_y_got,
    post_z_got,
    post_row_got,
    post_part_got,
    partial,
    in_sem,
    send_sem,
    recv_sem,
    *,
    sizes,
):
    here = tuple(lax.axis_index(axis) for axis in ("flow", "gy", "gz"))

    flow = {
        0: here[0],
        1: jnp.where(here[0] == sizes[0] - 1, 0, here[0] + 1),
        -1: jnp.where(here[0] == 0, sizes[0] - 1, here[0] - 1),
    }
    lateral = [{0: here[axis], 1: here[axis] + 1, -1: here[axis] - 1} for axis in (1, 2)]

    def neighbour(offset):
        return (flow[offset[0]], lateral[0][offset[1]], lateral[1][offset[2]])

    closed = {
        (1, -1): here[1] == 0,
        (1, 1): here[1] == sizes[1] - 1,
        (2, -1): here[2] == 0,
        (2, 1): here[2] == sizes[2] - 1,
    }
    def has(offset):
        known = [jnp.logical_not(closed[(axis, offset[axis])]) for axis in (1, 2) if offset[axis] != 0]
        return functools.reduce(jnp.logical_and, known) if known else None

    def when(condition, action):
        if condition is None:
            action()
        else:
            pl.when(condition)(action)

    def by_class(action, backward=False, classes=CLASSES):
        for dy, dz in classes:
            when(has((0, -dy, -dz) if backward else (0, dy, dz)), functools.partial(action, dy, dz))

    lane = lax.broadcasted_iota(jnp.int32, (8, NZ), 1)
    wide_lane = lax.broadcasted_iota(jnp.int32, (NY, NZ), 1)
    wide_row = lax.broadcasted_iota(jnp.int32, (NY, NZ), 0)
    row = lax.broadcasted_iota(jnp.int32, (8, NZ), 0)
    row_lane = lax.broadcasted_iota(jnp.int32, (1, NZ), 1)

    loads = [
        pltpu.make_async_copy(solid_in, solid, in_sem.at[0]),
        pltpu.make_async_copy(labels_in, labels, in_sem.at[1]),
        pltpu.make_async_copy(momentum_in, state.at[pl.ds(0, 19)], in_sem.at[2]),
    ]
    for load in loads:
        load.start()

    def send(source, target, turn, place, offset):
        pltpu.make_async_remote_copy(
            src_ref=source,
            dst_ref=target,
            send_sem=send_sem.at[turn, place],
            recv_sem=recv_sem.at[turn, place],
            device_id=neighbour(offset),
            device_id_type=MESH,
        ).start()

    def await_bytes(sems, turn, place, like):
        pltpu.make_async_copy(like, like, sems.at[turn, place]).wait()

    def send_phase_class(dy, dz):
        place = CLASS[(dy, dz)]
        if dz == 0:
            side = SIDE[dy]
            send(phase_y.at[side], phase_y_got.at[side, pl.ds(0, 8)], 0, place, (0, dy, 0))
            for dx, line, target in ((1, 6, 8), (-1, 0, 10)):
                source = phase_y.at[side, pl.ds(line, 2)]
                send(source, phase_y_got.at[side, pl.ds(target, 2)], 0, place, (dx, dy, 0))
        elif dy == 0:
            side = SIDE[dz]
            for dx in (0, 1, -1):
                send(phase_z.at[side], phase_z_got.at[side, TURN[dx]], 0, place, (dx, 0, dz))
        else:
            sides = SIDE[dy], SIDE[dz]
            send(phase_yz.at[sides], phase_yz_got.at[sides], 0, place, (0, dy, dz))

    def phase_like(dy, dz):
        if dz == 0:
            return phase_y_got.at[SIDE[dy]]
        if dy == 0:
            return phase_z_got.at[SIDE[dz]]
        return phase_yz_got.at[SIDE[dy], SIDE[dz]]

    def phase_plane(plane):
        return scalars.at[pl.ds(0, 2), plane, pl.ds(LO, NY)]

    def post_plane(step, dx, plane):
        return posts.at[step, pl.ds(0 if dx == 1 else 7, 7), plane, pl.ds(LO, NY)]

    def xy_place(dx, fused):
        return (ROWS_Y if fused else ROWS_Y_LAST) + ROWS_XY * SIDE[dx]

    def send_post_class(step, fused, dy, dz):
        turn, place = step + 1, CLASS[(dy, dz)]
        if dz == 0:
            side = SIDE[dy]
            rows = pl.ds(0, ROWS_Y if fused else ROWS_Y_LAST)
            send(post_y.at[step, side, rows], post_y_got.at[step, side, rows], turn, place, (0, dy, 0))
            for dx in (1, -1):
                source = post_xy.at[step, SIDE[dx], side]
                target = post_y_got.at[step, side, pl.ds(xy_place(dx, fused), ROWS_XY)]
                send(source, target, turn, place, (dx, dy, 0))
        elif dy == 0:
            side = SIDE[dz]
            for dx in (0, 1, -1):
                send(post_z.at[step, side], post_z_got.at[step, side, TURN[dx]], turn, place, (dx, 0, dz))
        else:
            sides = SIDE[dy], SIDE[dz]
            target = post_row_got.at[step, sides[0], sides[1], pl.ds(0, 1)]
            send(post_row.at[step, sides[0], sides[1]], target, turn, place, (0, dy, dz))

    def send_corner_class(step, dy, dz):
        sides = SIDE[dy], SIDE[dz]
        for dx in (1, -1):
            target = post_row_got.at[step, sides[0], sides[1], pl.ds(TURN[dx], 1)]
            send(post_row.at[step, sides[0], sides[1]], target, step + 1, CORNER_CLASS[(dy, dz)], (dx, dy, dz))

    def post_like(step, fused, dy, dz):
        if dz == 0:
            return post_y_got.at[step, SIDE[dy], pl.ds(0, (ROWS_Y if fused else ROWS_Y_LAST) + 2 * ROWS_XY)]
        if dy == 0:
            return post_z_got.at[step, SIDE[dz]]
        return post_row_got.at[step, SIDE[dy], SIDE[dz], pl.ds(0, 1)]

    def corner_like(step, dy, dz):
        return post_row_got.at[step, SIDE[dy], SIDE[dz], pl.ds(1, 2)]

    def await_posts(sems, step, fused, classes, backward):
        by_class(
            lambda dy, dz: await_bytes(sems, step + 1, CLASS[(dy, dz)], post_like(step, fused, dy, dz)),
            backward,
            classes,
        )

    def await_corners(sems, step, backward):
        by_class(
            lambda dy, dz: await_bytes(sems, step + 1, CORNER_CLASS[(dy, dz)], corner_like(step, dy, dz)),
            backward,
            ON_YZ,
        )

    def await_x(sems, step):
        for dx in (1, -1):
            await_bytes(sems, step + 1, X_CLASS[dx], post_plane(step, dx, 0 if dx == 1 else NX + 1))

    def await_parts(sems, step):
        for dx in (1, -1):
            await_bytes(sems, step + 1, PART_CLASS[dx], post_part_got.at[step, SIDE[dx]])

    def pack_z(tile, place, sign, packed):
        moved = pltpu.roll(tile, place + 1 if sign == 1 else place, axis=1)
        return jnp.where(lane == place, moved, packed)

    def unpack_z(packed, place, sign):
        return pltpu.roll(packed, (128 - place) % 128 if sign == 1 else 127 - place, axis=1)

    def edge_lane(sign):
        return 0 if sign == 1 else NZ - 1

    def set_phase(x, values, packed):
        up, down = packed
        for entry, value in enumerate(values):
            scalars[entry, x + 1, LO:HI, :] = value
            for dy, edge in ((1, HI - 1), (-1, LO)):
                phase_y[SIDE[dy], x * 2 + entry] = scalars[entry, x + 1, edge : edge + 1, :]
            for half in range(2):
                tile = value[8 * half : 8 * half + 8]
                place = entry * 8 + 2 * x + half
                up = pack_z(tile, place, 1, up)
                down = pack_z(tile, place, -1, down)
        return up, down

    def send_phase(packed):
        for dz in (1, -1):
            phase_z[SIDE[dz]] = packed[SIDE[dz]]
            for dy, edge in ((1, 7), (-1, 0)):
                phase_yz[SIDE[dy], SIDE[dz]] = phase_z[SIDE[dz], edge : edge + 1, :]
        by_class(send_phase_class)
        for dx, near, far in ((1, NX, 0), (-1, 1, NX + 1)):
            send(phase_plane(near), phase_plane(far), 0, X_CLASS[dx], (dx, 0, 0))

    def unpack_phase():
        first, count = 0, 2
        fills = (0.0, WETTING)
        shifted = {1: scalars_down, -1: scalars_up}

        def place_of(entry):
            return entry

        def cover(offset, value, fill):
            for axis in (1, 2):
                if offset[axis] != 0:
                    value = jnp.where(closed[(axis, -offset[axis])], fill, value)
            return value

        def arrive(sems, backward):
            by_class(lambda dy, dz: await_bytes(sems, 0, CLASS[(dy, dz)], phase_like(dy, dz)), backward)
            for dx in (1, -1):
                await_bytes(sems, 0, X_CLASS[dx], phase_plane(0))

        def shift_plane(entry, plane, dz, face, column):
            for half in range(2):
                rows = slice(LO + 8 * half, LO + 8 * half + 8)
                value = scalars[first + entry, plane, rows, :]
                place = entry * 8 + 2 * column + half
                ghost = cover((0, 0, dz), unpack_z(face, place, dz), fills[entry])
                shifted[dz][place_of(entry), plane, rows, :] = jnp.where(
                    lane == edge_lane(dz), ghost, pltpu.roll(value, 1 if dz == 1 else 127, axis=1)
                )

        arrive(send_sem, False)
        arrive(recv_sem, True)
        for dz in (1, -1):
            face = phase_z_got[SIDE[dz], 0]
            for entry in range(count):
                for x in range(NX):
                    shift_plane(entry, x + 1, dz, face, x)
        for dy, ghost in ((1, LO - 1), (-1, HI)):
            half = 1 if dy == 1 else 0
            for entry in range(count):
                for x in range(NX):
                    line = cover((0, dy, 0), phase_y_got[SIDE[dy], x * count + entry], fills[entry])
                    scalars[first + entry, x + 1, ghost : ghost + 1, :] = line
                    for dz in (1, -1):
                        corner = phase_yz_got[SIDE[dy], SIDE[dz]]
                        place = entry * 8 + 2 * x + half
                        corner = cover((0, dy, dz), unpack_z(corner, place, dz), fills[entry])
                        shifted[dz][place_of(entry), x + 1, ghost : ghost + 1, :] = jnp.where(
                            row_lane == edge_lane(dz), corner, pltpu.roll(line, 1 if dz == 1 else 127, axis=1)
                        )
        for dx, plane, column in ((1, 0, NX - 1), (-1, NX + 1, 0)):
            for dy, ghost in ((1, LO - 1), (-1, HI)):
                for entry in range(count):
                    line = phase_y_got[SIDE[dy], 8 + 2 * SIDE[dx] + entry]
                    scalars[first + entry, plane, ghost : ghost + 1, :] = cover((0, dy, 0), line, fills[entry])
            for dz in (1, -1):
                for entry in range(count):
                    shift_plane(entry, plane, dz, phase_z_got[SIDE[dz], TURN[dx]], column)

    def relax_body(step, x, initial):
        total = state[0, x]
        flux = [0.0, 0.0, 0.0]
        for up, down in PAIRS:
            first, second = state[up, x], state[down, x]
            total = total + (first + second)
            difference = first - second
            for axis in range(3):
                if VELOCITY[up][axis] == 1:
                    flux[axis] = flux[axis] + difference
                elif VELOCITY[up][axis] == -1:
                    flux[axis] = flux[axis] - difference
        inverse = 1.0 / total
        velocity = [part * inverse for part in flux]
        phase = scalars[step + 1, x + 1, LO:HI, :]
        tau = 1.3 - 0.3 * phase
        rate = 1.0 / tau
        keep = 1.0 - rate
        for axis in range(3):
            speed[axis, x] = velocity[axis]
        if initial:
            red = total * (0.05 + 0.9 * labels[x].astype(jnp.float32))
            blue = total - red
            colour[0, x] = red
            colour[1, x] = blue
        shifted = [velocity[0] + tau * inverse * 0.001, velocity[1], velocity[2]]
        square = shifted[0] * shifted[0] + shifted[1] * shifted[1] + shifted[2] * shifted[2]
        scale = rate * total
        base = scale * (1.0 - 1.5 * square)
        state[0, x] = keep * state[0, x] + base * (1.0 / 3.0)
        face, edge = base * (1.0 / 18.0), base * (1.0 / 36.0)
        for up, down in PAIRS:
            along = 0.0
            for axis in range(3):
                if VELOCITY[up][axis] == 1:
                    along = along + shifted[axis]
                elif VELOCITY[up][axis] == -1:
                    along = along - shifted[axis]
            push = scale * along
            if up < 7:
                even, odd = face + 0.25 * (push * along), push * (1.0 / 6.0)
            else:
                even, odd = edge + 0.125 * (push * along), push * (1.0 / 12.0)
            state[up, x] = keep * state[up, x] + (even + odd)
            state[down, x] = keep * state[down, x] + (even - odd)

    def gradient_at(step, x):
        def at(buffer, place, plane, dy):
            return buffer[place, plane, LO + dy : HI + dy, :]

        here_ = step + 1

        def spread(plane):
            return (
                2.0 * at(scalars, here_, plane, 0)
                + (at(scalars, here_, plane, 1) + at(scalars, here_, plane, -1))
                + (at(scalars_up, 1, plane, 0) + at(scalars_down, 1, plane, 0))
            )

        def slope_y(plane):
            return at(scalars, here_, plane, 1) - at(scalars, here_, plane, -1)

        def slope_z(plane):
            return at(scalars_up, 1, plane, 0) - at(scalars_down, 1, plane, 0)

        low, mid, high = x, x + 1, x + 2
        up_up, up_down = at(scalars_up, 1, mid, 1), at(scalars_up, 1, mid, -1)
        down_up, down_down = at(scalars_down, 1, mid, 1), at(scalars_down, 1, mid, -1)
        along_x = spread(high) - spread(low)
        along_y = 2.0 * slope_y(mid) + (slope_y(high) + slope_y(low)) + ((up_up - up_down) + (down_up - down_down))
        along_z = 2.0 * slope_z(mid) + (slope_z(high) + slope_z(low)) + ((up_up - down_up) + (up_down - down_down))
        return [part * (1.0 / 12.0) for part in (along_x, along_y, along_z)]

    def put_post(step, x, name, value, packed, fluid=None):
        kind, number = name
        offset = VELOCITY[number]
        value = jnp.where(fluid, value, 0.0)
        if offset[1] != 0:
            sign = offset[1]
            edge = HI - 1 if sign == 1 else LO
        up, down = packed
        if offset[2] != 0:
            unrolled[UNROLLED[name], x] = value
            sign_z = offset[2]
            first = Z_FACE[sign_z].index(name) * 8
            for half in range(2):
                tile = value[8 * half : 8 * half + 8]
                place = first + 2 * x + half
                if sign_z == 1:
                    up = pack_z(tile, place, 1, up)
                else:
                    down = pack_z(tile, place, -1, down)
            value = pltpu.roll(value, 1 if sign_z == 1 else 127, axis=1)
            if name not in ACROSS_YZ:
                value = jnp.where(wide_lane == edge_lane(sign_z), 0.0, value)
        posts[step, SLOT[name], x + 1, LO:HI, :] = value
        if offset[1] != 0:
            line = Y_FACE[sign].index(name) * 4 + x
            post_y[step, SIDE[sign], pl.ds(line, 1), :] = posts[step, SLOT[name], x + 1, edge : edge + 1, :]
        return up, down

    def collide_body(step, x, packed):
        gradient = gradient_at(step, x)
        squares = [part * part for part in gradient]
        total = squares[0] + squares[1] + squares[2]
        fluid = scalars[0, x + 1, LO:HI, :] > 0.0
        packed = put_post(step, x, ("f", 0), state[0, x], packed, fluid)
        third = total * (1.0 / 3.0)
        for up, down in PAIRS:
            if up < 7:
                surface = (TENSION / 18.0) * (squares[(up - 1) // 2] - third)
            else:
                slope = 0.0
                for axis in range(3):
                    if VELOCITY[up][axis] == 1:
                        slope = slope + gradient[axis]
                    elif VELOCITY[up][axis] == -1:
                        slope = slope - gradient[axis]
                surface = (TENSION / 36.0) * (slope * slope - 2.0 * third)
            packed = put_post(step, x, ("f", up), state[up, x] + surface, packed, fluid)
            packed = put_post(step, x, ("f", down), state[down, x] + surface, packed, fluid)
        red, blue = colour[0, x], colour[1, x]
        mixing = (0.5 * 0.125) * (red * blue / (red + blue)) * lax.rsqrt(jnp.maximum(total, 0.01))
        packed = put_post(step, x, ("r", 0), 0.25 * red, packed, fluid)
        packed = put_post(step, x, ("b", 0), 0.25 * blue, packed, fluid)
        for axis in range(3):
            drift = 0.5 * speed[axis, x]
            across = mixing * gradient[axis]
            for kind, amount, turn in (("r", red, 1.0), ("b", blue, -1.0)):
                mean = 0.125 * amount
                lean = amount * drift + turn * across
                packed = put_post(step, x, (kind, 2 * axis + 1), mean + lean, packed, fluid)
                packed = put_post(step, x, (kind, 2 * axis + 2), mean - lean, packed, fluid)
        return packed

    def state_at(name):
        return {"f": 0, "r": 19, "b": 26}[name[0]] + name[1]

    def opened_at(x, offset):
        dx, dy, dz = offset
        return shifted_scalars[dz][0, x + 1 - dx, LO - dy : HI - dy, :] > 0.0

    def bounced_at(step, x, name):
        back = (name[0], OPPOSITE[name[1]])
        if VELOCITY[name[1]][2] != 0:
            return unrolled[UNROLLED[back], x]
        return posts[step, SLOT[back], x + 1, LO:HI, :]

    def stream_inside(step, x, end, last):
        fluid = scalars[0, x + 1, LO:HI, :] > 0.0
        names = [name for name in EVERY if (last or name[0] == "f") and name not in ACROSS_YZ]
        for name in names:
            dx, dy, dz = VELOCITY[name[1]]
            if name[1] == 0:
                value = posts[step, SLOT[name], x + 1, LO:HI, :]
            else:
                if dx != 0 and dx == end:
                    arriving = 0.0
                else:
                    arriving = posts[step, SLOT[name], x + 1 - dx, LO - dy : HI - dy, :]
                value = jnp.where(opened_at(x, (dx, dy, dz)), arriving, bounced_at(step, x, name))
            state[state_at(name), x] = jnp.where(fluid, value, 0.0) if last else value

    def stream_across(step, x, last):
        fluid = scalars[0, x + 1, LO:HI, :] > 0.0
        for name in ACROSS_YZ:
            dx, dy, dz = VELOCITY[name[1]]
            arriving = posts[step, SLOT[name], x + 1, LO - dy : HI - dy, :]
            value = jnp.where(opened_at(x, (dx, dy, dz)), arriving, bounced_at(step, x, name))
            state[state_at(name), x] = jnp.where(fluid, value, 0.0) if last else value

    def arrivals(step, last):
        def wanted(name):
            return last or name[0] == "f"

        def kept(x, rows, value):
            if not last:
                return value
            return jnp.where(scalars[0, x + 1, LO + rows.start : LO + rows.stop, :] > 0.0, value, 0.0)

        def z_columns(name, dx, column, half):
            dz = VELOCITY[name[1]][2]
            place = Z_FACE[dz].index(name) * 8 + 2 * column + half
            face = post_z_got[step, SIDE[dz], TURN[dx]]
            return jnp.where(lane == edge_lane(dz), unpack_z(face, place, dz), 0.0)

        def add_z():
            for dz in (1, -1):
                for name in Z_FACE[dz]:
                    if name in ACROSS_YZ or not wanted(name):
                        continue
                    for x in range(NX):
                        source = x - VELOCITY[name[1]][0]
                        if not 0 <= source < NX:
                            continue
                        for half in range(2):
                            rows = slice(8 * half, 8 * half + 8)
                            value = kept(x, rows, z_columns(name, 0, source, half))
                            state[state_at(name), x, rows, :] = state[state_at(name), x, rows, :] + value
            for name in ACROSS_YZ:
                dz = VELOCITY[name[1]][2]
                face = post_z_got[step, SIDE[dz], 0]
                for x in range(NX):
                    for half in range(2):
                        rows = slice(LO + 8 * half, LO + 8 * half + 8)
                        place = Z_FACE[dz].index(name) * 8 + 2 * x + half
                        posts[step, SLOT[name], x + 1, rows, :] = jnp.where(
                            lane == edge_lane(dz), unpack_z(face, place, dz), posts[step, SLOT[name], x + 1, rows, :]
                        )

        def add_x():
            for dx, end, ghost, column, names in ((1, 0, 0, NX - 1, X_UP), (-1, NX - 1, NX + 1, 0, X_DOWN)):
                for name in names:
                    if not wanted(name):
                        continue
                    _, dy, dz = VELOCITY[name[1]]
                    if dy != 0:
                        row_ghost = LO - 1 if dy == 1 else HI
                        line = post_y_got[step, SIDE[dy], pl.ds(xy_place(dx, not last), 1), :]
                        posts[step, SLOT[name], ghost, row_ghost : row_ghost + 1, :] = line
                    for half in range(2):
                        rows = slice(8 * half, 8 * half + 8)
                        first = LO + 8 * half - dy
                        value = posts[step, SLOT[name], ghost, first : first + 8, :]
                        if dz != 0:
                            value = value + z_columns(name, dx, column, half)
                        state[state_at(name), end, rows, :] = state[state_at(name), end, rows, :] + kept(end, rows, value)
        def add_y():
            for dy, edge in ((1, 0), (-1, NY - 1)):
                rows = slice(edge, edge + 1)
                for entry, name in enumerate(Y_FACE[dy]):
                    if name in ACROSS_YZ or not wanted(name):
                        continue
                    for x in range(NX):
                        source = x - VELOCITY[name[1]][0]
                        if not 0 <= source < NX:
                            continue
                        value = kept(x, rows, post_y_got[step, SIDE[dy], pl.ds(entry * 4 + source, 1), :])
                        state[state_at(name), x, rows, :] = state[state_at(name), x, rows, :] + value

        def add_across():
            for name in ACROSS_YZ:
                _, dy, dz = VELOCITY[name[1]]
                entry, entry_z = Y_FACE[dy].index(name), Z_FACE[dz].index(name)
                half = 1 if dy == 1 else 0
                ghost = LO - 1 if dy == 1 else HI
                for x in range(NX):
                    corner = unpack_z(post_row_got[step, SIDE[dy], SIDE[dz], 0], entry_z * 8 + 2 * x + half, dz)
                    line = jnp.where(row_lane == edge_lane(dz), corner, post_y_got[step, SIDE[dy], pl.ds(entry * 4 + x, 1), :])
                    posts[step, SLOT[name], x + 1, ghost : ghost + 1, :] = line

        return add_x, add_y, add_z, add_across

    shifted_scalars = {0: scalars, 1: scalars_down, -1: scalars_up}

    def add_up(step, packed):
        up, down = packed
        for x in range(NX):
            for place, kind in enumerate(("r", "b")):
                total = posts[step, SLOT[(kind, 0)], x + 1, LO:HI, :]
                for number in range(1, 7):
                    dx, dy, dz = VELOCITY[number]
                    plane = x + 1 - dx
                    opened = shifted_scalars[dz][0, plane, LO - dy : HI - dy, :] > 0.0
                    back = (kind, OPPOSITE[number])
                    if dz != 0:
                        bounced = unrolled[UNROLLED[back], x]
                    else:
                        bounced = posts[step, SLOT[back], x + 1, LO:HI, :]
                    if 1 <= plane <= NX:
                        arriving = posts[step, SLOT[(kind, number)], plane, LO - dy : HI - dy, :]
                    else:
                        arriving = 0.0
                    total = total + jnp.where(opened, arriving, bounced)
                partial[place, x] = total
                for half in range(2):
                    tile = total[8 * half : 8 * half + 8]
                    lanes = SUM_Z + 8 * place + 2 * x + half
                    up, down = pack_z(tile, lanes, 1, up), pack_z(tile, lanes, -1, down)
                for dx, end in ((1, NX - 1), (-1, 0)):
                    if x == end:
                        post_part[step, SIDE[dx], NY * place : NY * place + NY, :] = total
                for dy, edge in ((1, NY - 1), (-1, 0)):
                    post_y[step, SIDE[dy], pl.ds(SUM_Y + 4 * place + x, 1), :] = partial[place, x, edge : edge + 1, :]
                for dy, half in ((1, 1), (-1, 0)):
                    rows = slice(LO + 8 * half, LO + 8 * half + 8)
                    tile = posts[step, SLOT[(kind, FACE[(1, dy)])], x + 1, rows, :]
                    lanes = Y_Z + 8 * place + 2 * x + (0 if dy == 1 else 1)
                    up, down = pack_z(tile, lanes, 1, up), pack_z(tile, lanes, -1, down)
        for place, kind in enumerate(("r", "b")):
            for dx, end in ((1, NX - 1), (-1, 0)):
                slot = SLOT[(kind, FACE[(0, dx)])]
                for half in range(2):
                    tile = posts[step, slot, end + 1, LO + 8 * half : LO + 8 * half + 8, :]
                    lanes = X_Z + 8 * place + (0 if dx == 1 else 6) + half
                    up, down = pack_z(tile, lanes, 1, up), pack_z(tile, lanes, -1, down)
                for dy, edge in ((1, HI - 1), (-1, LO)):
                    line = posts[step, slot, end + 1, edge : edge + 1, :]
                    post_y[step, SIDE[dy], pl.ds(X_Y + 2 * SIDE[dx] + place, 1), :] = line
                    post_xy[step, SIDE[dx], SIDE[dy], pl.ds(X_XY + place, 1), :] = line
                    post_xy[step, SIDE[dx], SIDE[dy], pl.ds(SUM_XY + place, 1), :] = partial[place, end, edge - LO : edge - LO + 1, :]
                    line = posts[step, SLOT[(kind, FACE[(1, dy)])], end + 1, edge : edge + 1, :]
                    post_xy[step, SIDE[dx], SIDE[dy], pl.ds(Y_XY + place, 1), :] = line
                    part = Y_PART + 2 * SIDE[dy] + place
                    post_part[step, SIDE[dx], part : part + 1, :] = line
        return up, down

    def put_edges(step, packed, fused):
        for dx, end in ((1, NX - 1), (-1, 0)):
            for dy, edge in ((1, HI - 1), (-1, LO)):
                slot = SLOT[("f", VELOCITY.index((dx, dy, 0)))]
                post_xy[step, SIDE[dx], SIDE[dy], pl.ds(0, 1), :] = posts[step, slot, end + 1, edge : edge + 1, :]
            if fused:
                both = jnp.where(lane < 64, packed[0], pltpu.roll(packed[1], 64, axis=1))
                post_part[step, SIDE[dx], Z_PART : Z_PART + 8, :] = both
        for dz in (1, -1):
            post_z[step, SIDE[dz]] = packed[SIDE[dz]]
            for dy, edge in ((1, 7), (-1, 0)):
                line = post_z[step, SIDE[dz], edge : edge + 1, :]
                post_row[step, SIDE[dy], SIDE[dz], 0] = line
                if fused:
                    post_y[step, SIDE[dy], pl.ds(Z_Y + SIDE[dz], 1), :] = line

    def turned(value, lanes):
        return pltpu.roll(value, 128 - lanes, axis=1)

    def ratio(red, blue):
        return (red - blue) / (red + blue)

    def packed_ratio(sums):
        blue = turned(sums, 8)
        return ratio(sums, blue)

    def finish_phase(step, planes=(), corners=False):
        inside = len(planes) > 0
        here_ = step + 2

        def put(target, entry, plane, rows, value):
            fluid = shifted_scalars[target][0, plane, rows, :] > 0.0
            shifted_scalars[target][entry, plane, rows, :] = jnp.where(fluid, value, WETTING)

        interior = slice(LO, HI)
        z_got = {(dx, dz): post_z_got[step, SIDE[dz], TURN[dx]] for dx in (-1, 0, 1) for dz in (1, -1)}
        row_got = {
            (dx, dy, dz): post_row_got[step, SIDE[dy], SIDE[dz], TURN[dx]]
            for dx in (() if inside else (-1, 0, 1) if corners else (0,))
            for dy in (1, -1)
            for dz in (1, -1)
        }

        def xy_got(dx, dy, line):
            return post_y_got[step, SIDE[dy], pl.ds(ROWS_Y + ROWS_XY * SIDE[dx] + line, 1), :]

        def with_columns(value, place, column, dx):
            halves = []
            for half in range(2):
                tile = value[8 * half : 8 * half + 8]
                for dz in (1, -1):
                    lanes = IN_Z + 8 * place + 2 * column + half
                    tile = tile + jnp.where(lane == edge_lane(dz), unpack_z(z_got[(dx, dz)], lanes, dz), 0.0)
                halves.append(tile)
            return jnp.concatenate(halves, axis=0)

        def with_rows(value, rows):
            for dy, edge in ((1, 0), (-1, NY - 1)):
                value = value + jnp.where(wide_row == edge, rows[dy], 0.0)
            return value

        def with_ends(line, offset, place, x):
            dx, dy = offset
            half = 1 if dy == 1 else 0
            for dz in (1, -1):
                lanes = IN_Z + 8 * place + 2 * x + half
                line = line + jnp.where(row_lane == edge_lane(dz), unpack_z(row_got[(dx, dy, dz)], lanes, dz), 0.0)
            return line

        for x in planes:
            sums = []
            for place, kind in enumerate(("r", "b")):
                total = partial[place, x]
                for dx, end, ghost in ((1, 0, 0), (-1, NX - 1, NX + 1)):
                    if x == end:
                        total = total + posts[step, SLOT[(kind, FACE[(0, dx)])], ghost, interior, :]
                rows = {}
                for dy in (1, -1):
                    entry = Y_FACE[dy].index((kind, FACE[(1, dy)]))
                    rows[dy] = post_y_got[step, SIDE[dy], pl.ds(entry * 4 + x, 1), :]
                total = with_columns(with_rows(total, rows), place, x, 0)
                colour[place, x] = total
                sums.append(total)
            put(0, here_, x + 1, interior, ratio(*sums))
        if inside:
            return
        for dx, ghost, end, column in ((1, 0, 0, NX - 1), (-1, NX + 1, NX - 1, 0)):
            sums = []
            lines = {1: [], -1: []}
            for place, kind in enumerate(("r", "b")):
                if not corners:
                    total = post_part_got[step, SIDE[dx], NY * place : NY * place + NY, :]
                    total = total + posts[step, SLOT[(kind, FACE[(0, -dx)])], end + 1, interior, :]
                    rows = {dy: xy_got(dx, dy, Y_XY + place) for dy in (1, -1)}
                    sums.append(with_columns(with_rows(total, rows), place, column, dx))
                    continue
                for dy in (1, -1):
                    part = Y_PART + 2 * SIDE[-dy] + place
                    line = (
                        xy_got(dx, dy, SUM_XY + place)
                        + post_part_got[step, SIDE[dx], part : part + 1, :]
                        + post_y_got[step, SIDE[dy], pl.ds(X_Y + 2 * SIDE[-dx] + place, 1), :]
                    )
                    lines[dy].append(with_ends(line, (dx, dy), place, column))
            if not corners:
                put(0, here_, ghost, interior, ratio(*sums))
                continue
            for dy, row_ghost in ((1, LO - 1), (-1, HI)):
                put(0, here_, ghost, slice(row_ghost, row_ghost + 1), ratio(*lines[dy]))
        for dy, row_ghost, edge in ((1, LO - 1, LO), (-1, HI, HI - 1)):
            for x in () if corners else range(NX):
                sums = []
                for place, kind in enumerate(("r", "b")):
                    line = post_y_got[step, SIDE[dy], pl.ds(SUM_Y + 4 * place + x, 1), :]
                    line = line + posts[step, SLOT[(kind, FACE[(1, -dy)])], x + 1, edge : edge + 1, :]
                    for dx, end in ((1, 0), (-1, NX - 1)):
                        if x == end:
                            line = line + xy_got(dx, dy, X_XY + place)
                    sums.append(with_ends(line, (0, dy), place, x))
                put(0, here_, x + 1, slice(row_ghost, row_ghost + 1), ratio(*sums))
        low_x, high_x = lane % 8 < 2, lane % 8 >= 6
        first_y, last_y = (row == 0) & (lane % 2 == 0), (row == 7) & (lane % 2 == 1)
        row_low_x, row_high_x = row_lane % 8 < 2, row_lane % 8 >= 6
        for dz in (1, -1):

            def with_y(sums, dx):
                sums = sums + jnp.where(first_y, turned(row_got[(dx, 1, dz)], Y_Z), 0.0)
                return sums + jnp.where(last_y, turned(row_got[(dx, -1, dz)], Y_Z), 0.0)

            faces = {}
            if not corners:
                sums = turned(z_got[(0, dz)], SUM_Z) + turned(post_z[step, SIDE[-dz]], IN_Z)
                sums = sums + jnp.where(low_x, turned(z_got[(1, dz)], X_Z), 0.0)
                sums = sums + jnp.where(high_x, turned(z_got[(-1, dz)], X_Z), 0.0)
                faces[0] = packed_ratio(with_y(sums, 0))
            for dx in (1, -1) if corners else ():
                sums = turned(z_got[(dx, dz)], SUM_Z) + turned(z_got[(0, dz)], X_Z)
                sums = sums + turned(post_part_got[step, SIDE[dx], Z_PART : Z_PART + 8, :], IN_Z + 64 * SIDE[-dz])
                faces[dx] = packed_ratio(with_y(sums, dx))
            for plane in (0, NX + 1) if corners else range(1, NX + 1):
                dx, column = {0: (1, NX - 1), NX + 1: (-1, 0)}.get(plane, (0, plane - 1))
                for half in range(2):
                    rows = slice(LO + 8 * half, LO + 8 * half + 8)
                    value = scalars[here_, plane, rows, :]
                    ghost = unpack_z(faces[dx], 2 * column + half, dz)
                    value = jnp.where(lane == edge_lane(dz), ghost, pltpu.roll(value, 1 if dz == 1 else 127, axis=1))
                    put(dz, 1, plane, rows, value)
            for dy, row_ghost in ((1, LO - 1), (-1, HI)):
                half = 1 if dy == 1 else 0
                edge = 0 if dy == 1 else 7
                sums = turned(row_got[(0, dy, dz)], SUM_Z)
                sums = sums + turned(post_y_got[step, SIDE[dy], pl.ds(Z_Y + SIDE[-dz], 1), :], IN_Z)
                sums = sums + turned(post_z_got[step, SIDE[dz], 0, edge : edge + 1, :], Y_Z)
                if corners:
                    sums = sums + jnp.where(row_low_x, turned(row_got[(1, dy, dz)], X_Z), 0.0)
                    sums = sums + jnp.where(row_high_x, turned(row_got[(-1, dy, dz)], X_Z), 0.0)
                corner = packed_ratio(sums)
                for x in (0, NX - 1) if corners else range(1, NX - 1):
                    line = scalars[here_, x + 1, row_ghost : row_ghost + 1, :]
                    line = pltpu.roll(line, 1 if dz == 1 else 127, axis=1)
                    line = jnp.where(row_lane == edge_lane(dz), unpack_z(corner, 2 * x + half, dz), line)
                    put(dz, 1, x + 1, slice(row_ghost, row_ghost + 1), line)

    blank = jnp.zeros((8, NZ), jnp.float32)

    def first_phase(x, packed):
        fluid = 1.0 - solid[x].astype(jnp.float32)
        phase = jnp.where(fluid > 0.0, -0.9 + 1.8 * labels[x].astype(jnp.float32), WETTING)
        return set_phase(x, [fluid, phase], packed)

    barrier = pltpu.get_barrier_semaphore()

    def greet(dy, dz):
        for dx in (0, 1, -1) if 0 in (dy, dz) else (0,):
            pl.semaphore_signal(barrier, inc=1, device_id=neighbour((dx, dy, dz)), device_id_type=MESH)

    by_class(greet)
    for dx in (1, -1):
        pl.semaphore_signal(barrier, inc=1, device_id=neighbour((dx, 0, 0)), device_id_type=MESH)
    beside_y = 2 - closed[(1, 1)].astype(jnp.int32) - closed[(1, -1)].astype(jnp.int32)
    beside_z = 2 - closed[(2, 1)].astype(jnp.int32) - closed[(2, -1)].astype(jnp.int32)
    beside = 2 + 3 * (beside_y + beside_z) + beside_y * beside_z

    def clear(dy, dz):
        for step in range(STEPS):
            if dz == 0:
                post_y_got[step, SIDE[dy]] = jnp.zeros((ROWS_Y_ALL, NZ), jnp.float32)
            elif dy == 0:
                post_z_got[step, SIDE[dz]] = jnp.zeros((3, 8, NZ), jnp.float32)
            else:
                post_row_got[step, SIDE[dy], SIDE[dz]] = jnp.zeros((3, 1, NZ), jnp.float32)

    for dy, dz in CLASSES:
        pl.when(jnp.logical_not(has((0, -dy, -dz))))(functools.partial(clear, dy, dz))

    for step in range(STEPS):
        for side in range(2):
            post_part[step, side, Y_PART : Y_PART + 8, :] = blank
        for name in Y_FACE[1] + Y_FACE[-1]:
            if name not in ACROSS_YZ:
                ghost = LO - 1 if VELOCITY[name[1]][1] == 1 else HI
                for plane in range(1, NX + 1):
                    posts[step, SLOT[name], plane, ghost : ghost + 1, :] = blank[0:1]

    loads[0].wait()
    loads[1].wait()
    packed = lax.fori_loop(0, NX, first_phase, (blank, blank), unroll=True)
    pl.semaphore_wait(barrier, beside)
    send_phase(packed)
    loads[2].wait()
    lax.fori_loop(0, NX, lambda x, _: relax_body(0, x, True), None, unroll=True)
    unpack_phase()

    def collide_middle(step):
        return lax.fori_loop(1, NX - 1, lambda x, p: collide_body(step, x, p), (blank, blank), unroll=True)

    def move(step, packed, fused):
        packed = lax.fori_loop(0, 2, lambda turn, p: collide_body(step, 3 - 3 * turn, p), packed, unroll=True)
        if fused:
            packed = add_up(step, packed)
        put_edges(step, packed, fused)
        by_class(functools.partial(send_post_class, step, fused), classes=ON_Y + ON_YZ)
        if fused:
            by_class(functools.partial(send_corner_class, step), classes=ON_YZ)
        for dx, near, far in ((1, NX, 0), (-1, 1, NX + 1)):
            send(post_plane(step, dx, near), post_plane(step, dx, far), step + 1, X_CLASS[dx], (dx, 0, 0))
        by_class(functools.partial(send_post_class, step, fused), classes=ON_Z)
        if fused:
            for dx in (1, -1):
                side = SIDE[dx]
                send(post_part.at[step, side], post_part_got.at[step, side], step + 1, PART_CLASS[dx], (dx, 0, 0))
        last = not fused
        stream_inside(step, 0, 1, last)
        lax.fori_loop(1, NX - 1, lambda x, _: stream_inside(step, x, 0, last), None, unroll=True)
        stream_inside(step, NX - 1, -1, last)
        await_posts(send_sem, step, fused, CLASSES, False)
        await_x(send_sem, step)
        if fused:
            await_parts(send_sem, step)
            await_corners(send_sem, step, False)
        add_x, add_y, add_z, add_across = arrivals(step, last)
        await_posts(recv_sem, step, fused, ON_Z, True)
        add_z()
        await_posts(recv_sem, step, fused, ON_Y, True)
        add_y()
        if fused:
            finish_phase(step, (1, 2))
        await_posts(recv_sem, step, fused, ON_YZ, True)
        add_across()
        lax.fori_loop(0, NX, lambda x, _: stream_across(step, x, last), None, unroll=True)
        if fused:
            lax.fori_loop(1, 3, lambda x, _: relax_body(step + 1, x, False), None, unroll=True)
        await_x(recv_sem, step)
        add_x()
        if fused:
            finish_phase(step, (0, 3))
            lax.fori_loop(0, 2, lambda turn, _: relax_body(step + 1, 3 - 3 * turn, False), None, unroll=True)
            await_parts(recv_sem, step)
            finish_phase(step)
            packed = collide_middle(step + 1)
            await_corners(recv_sem, step, True)
            finish_phase(step, corners=True)
        return packed

    packed = lax.fori_loop(0, STEPS - 1, lambda step, p: move(step, p, True), collide_middle(0))
    move(STEPS - 1, packed, False)


def hand_out(every, momentum_out, red_out, blue_out, sem):
    copies = []
    first = 0
    for place, target in enumerate((momentum_out, red_out, blue_out)):
        count = target.shape[0]
        copies.append(pltpu.make_async_copy(every.at[pl.ds(first, count)], target, sem.at[place]))
        first += count
    for copy in copies:
        copy.start()
    for copy in copies:
        copy.wait()


def shards(sizes, momentum_sets, labels, solid_mask):
    block = (NX, NY, NZ)
    f32 = jnp.float32
    vmem = lambda *shape, dtype=f32: pltpu.VMEM(shape, dtype)
    every = pl.pallas_call(
        functools.partial(kernel, sizes=sizes),
        out_shape=vmem(33, *block),
        in_specs=[pl.BlockSpec(memory_space=pltpu.HBM)] * 3,
        out_specs=pl.BlockSpec(memory_space=pltpu.VMEM),
        scratch_shapes=[
            vmem(*block, dtype=jnp.int32),
            vmem(*block, dtype=jnp.int32),
            vmem(1 + STEPS, NX + 2, ROWS, NZ),
            vmem(2, NX + 2, ROWS, NZ),
            vmem(2, NX + 2, ROWS, NZ),
            vmem(STEPS, 33, NX + 2, ROWS, NZ),
            vmem(14, *block),
            vmem(3, *block),
            vmem(2, *block),
            vmem(2, 8, 1, NZ),
            vmem(2, 8, NZ),
            vmem(2, 2, 1, NZ),
            vmem(2, 12, 1, NZ),
            vmem(2, 3, 8, NZ),
            vmem(2, 2, 1, NZ),
            vmem(STEPS, 2, ROWS_Y, NZ),
            vmem(STEPS, 2, 8, NZ),
            vmem(STEPS, 2, 2, 1, 1, NZ),
            vmem(STEPS, 2, 2, ROWS_XY, NZ),
            vmem(STEPS, 2, ROWS_PART, NZ),
            vmem(STEPS, 2, ROWS_Y_ALL, NZ),
            vmem(STEPS, 2, 3, 8, NZ),
            vmem(STEPS, 2, 2, 3, 1, NZ),
            vmem(STEPS, 2, ROWS_PART, NZ),
            vmem(2, *block),
            pltpu.SemaphoreType.DMA((3,)),
            pltpu.SemaphoreType.DMA((1 + STEPS, 16)),
            pltpu.SemaphoreType.DMA((1 + STEPS, 16)),
        ],
        compiler_params=pltpu.CompilerParams(
            collective_id=0, has_side_effects=True, vmem_limit_bytes=VMEM_LIMIT
        ),
        cost_estimate=pl.CostEstimate(flops=15_000_000, bytes_accessed=1_800_000, transcendentals=0),
    )(*(pltpu.with_memory_space_constraint(array, pltpu.HBM) for array in (momentum_sets, labels, solid_mask)))
    return pl.pallas_call(
        hand_out,
        out_shape=[jax.ShapeDtypeStruct((count,) + block, f32) for count in (19, 7, 7)],
        in_specs=[pl.BlockSpec(memory_space=pltpu.VMEM)],
        out_specs=[pl.BlockSpec(memory_space=pltpu.HBM)] * 3,
        scratch_shapes=[pltpu.SemaphoreType.DMA((3,))],
        cost_estimate=pl.CostEstimate(flops=0, bytes_accessed=2_200_000, transcendentals=0),
    )(pltpu.with_memory_space_constraint(every, pltpu.VMEM))


def solution(mesh):
    sizes = tuple(mesh.shape[axis] for axis in ("flow", "gy", "gz"))
    split = P("flow", "gy", "gz")
    split_sets = P(None, "flow", "gy", "gz")
    return jax.shard_map(
        functools.partial(shards, sizes),
        mesh=mesh,
        in_specs=(split_sets, split, split),
        out_specs=(split_sets, split_sets, split_sets),
        check_vma=False,
    )
```

```python
import functools

import jax
import jax.numpy as jnp
from jax import lax
from jax.experimental import pallas as pl
from jax.experimental.pallas import tpu as pltpu
from jax.sharding import PartitionSpec as P

STEPS = 3
NX, NY, NZ = 4, 16, 128
LO, HI = 8, 8 + NY
ROWS = 32
WETTING = 0.3
TENSION = 0.05
MESH = pl.DeviceIdType.MESH
VMEM_LIMIT = 40 * 1024 * 1024

VELOCITY = (
    (0, 0, 0),
    (1, 0, 0),
    (-1, 0, 0),
    (0, 1, 0),
    (0, -1, 0),
    (0, 0, 1),
    (0, 0, -1),
    (1, 1, 0),
    (-1, -1, 0),
    (1, -1, 0),
    (-1, 1, 0),
    (1, 0, 1),
    (-1, 0, -1),
    (1, 0, -1),
    (-1, 0, 1),
    (0, 1, 1),
    (0, -1, -1),
    (0, 1, -1),
    (0, -1, 1),
)
OPPOSITE = (0, 2, 1, 4, 3, 6, 5, 8, 7, 10, 9, 12, 11, 14, 13, 16, 15, 18, 17)
PAIRS = ((1, 2), (3, 4), (5, 6), (7, 8), (9, 10), (11, 12), (13, 14), (15, 16), (17, 18))

X_UP = [("f", i) for i in (1, 7, 9, 11, 13)] + [("r", 1), ("b", 1)]
X_DOWN = [("f", i) for i in (2, 8, 10, 12, 14)] + [("r", 2), ("b", 2)]
EVERY = [("f", i) for i in range(19)] + [("r", i) for i in range(7)] + [("b", i) for i in range(7)]
ORDER = X_UP + X_DOWN + [name for name in EVERY if name not in X_UP + X_DOWN]
SLOT = {name: place for place, name in enumerate(ORDER)}
Y_FACE = {
    1: (("f", 3), ("r", 3), ("f", 7), ("f", 10), ("f", 15), ("f", 17), ("b", 3)),
    -1: (("f", 4), ("r", 4), ("f", 9), ("f", 8), ("f", 18), ("f", 16), ("b", 4)),
}
Z_FACE = {
    1: (("f", 5), ("f", 11), ("f", 14), ("f", 15), ("f", 18), ("r", 5), ("b", 5)),
    -1: (("f", 6), ("f", 13), ("f", 12), ("f", 17), ("f", 16), ("r", 6), ("b", 6)),
}
Z_MOVING = Z_FACE[1] + Z_FACE[-1]
UNROLLED = {name: place for place, name in enumerate(Z_MOVING)}
DIRECTIONS = VELOCITY[1:]
CORNERS = tuple((a, b, c) for a in (1, -1) for b in (1, -1) for c in (1, -1))
NEIGHBOURS = DIRECTIONS + CORNERS
SIDE = {1: 0, -1: 1}
TURN = {0: 0, 1: 1, -1: 2}
FACE = {(1, 1): 3, (1, -1): 4, (0, 1): 1, (0, -1): 2, (2, 1): 5, (2, -1): 6}
IN_Z, SUM_Z, X_Z, Y_Z = 40, 56, 72, 88
SUM_Y, X_Y, Z_Y, ROWS_Y = 28, 36, 40, 42
Y_XY, SUM_XY, X_XY, ROWS_XY = 1, 3, 5, 7
ROWS_Y_ALL = ROWS_Y + 2 * ROWS_XY
Y_PART, Z_PART, ROWS_PART = 32, 40, 48
ON_Y, ON_Z = ((1, 0), (-1, 0)), ((0, 1), (0, -1))
ON_YZ = ((1, 1), (1, -1), (-1, 1), (-1, -1))
CLASSES = ON_YZ + ON_Y + ON_Z
CLASS = {way: place for place, way in enumerate(CLASSES)}
X_CLASS = {1: 8, -1: 9}
PART_CLASS = {1: 10, -1: 11}
CORNER_CLASS = {way: 12 + place for place, way in enumerate(ON_YZ)}
ACROSS_YZ = tuple(("f", number) for number in (15, 16, 17, 18))


def kernel(
    momentum_in,
    labels_in,
    solid_in,
    state,
    labels,
    solid,
    scalars,
    scalars_down,
    scalars_up,
    posts,
    unrolled,
    speed,
    colour,
    phase_y,
    phase_z,
    phase_yz,
    phase_y_got,
    phase_z_got,
    phase_yz_got,
    post_y,
    post_z,
    post_row,
    post_xy,
    post_part,
    post_y_got,
    post_z_got,
    post_row_got,
    post_part_got,
    partial,
    in_sem,
    send_sem,
    recv_sem,
    *,
    sizes,
):
    here = tuple(lax.axis_index(axis) for axis in ("flow", "gy", "gz"))

    flow = {
        0: here[0],
        1: jnp.where(here[0] == sizes[0] - 1, 0, here[0] + 1),
        -1: jnp.where(here[0] == 0, sizes[0] - 1, here[0] - 1),
    }
    lateral = [{0: here[axis], 1: here[axis] + 1, -1: here[axis] - 1} for axis in (1, 2)]

    def neighbour(offset):
        return (flow[offset[0]], lateral[0][offset[1]], lateral[1][offset[2]])

    closed = {
        (1, -1): here[1] == 0,
        (1, 1): here[1] == sizes[1] - 1,
        (2, -1): here[2] == 0,
        (2, 1): here[2] == sizes[2] - 1,
    }
    def has(offset):
        known = [jnp.logical_not(closed[(axis, offset[axis])]) for axis in (1, 2) if offset[axis] != 0]
        return functools.reduce(jnp.logical_and, known) if known else None

    def when(condition, action):
        if condition is None:
            action()
        else:
            pl.when(condition)(action)

    def by_class(action, backward=False, classes=CLASSES):
        for dy, dz in classes:
            when(has((0, -dy, -dz) if backward else (0, dy, dz)), functools.partial(action, dy, dz))

    lane = lax.broadcasted_iota(jnp.int32, (8, NZ), 1)
    wide_lane = lax.broadcasted_iota(jnp.int32, (NY, NZ), 1)
    wide_row = lax.broadcasted_iota(jnp.int32, (NY, NZ), 0)
    row = lax.broadcasted_iota(jnp.int32, (8, NZ), 0)
    row_lane = lax.broadcasted_iota(jnp.int32, (1, NZ), 1)

    loads = [
        pltpu.make_async_copy(solid_in, solid, in_sem.at[0]),
        pltpu.make_async_copy(labels_in, labels, in_sem.at[1]),
        pltpu.make_async_copy(momentum_in, state.at[pl.ds(0, 19)], in_sem.at[2]),
    ]
    for load in loads:
        load.start()

    def send(source, target, turn, place, offset):
        pltpu.make_async_remote_copy(
            src_ref=source,
            dst_ref=target,
            send_sem=send_sem.at[turn, place],
            recv_sem=recv_sem.at[turn, place],
            device_id=neighbour(offset),
            device_id_type=MESH,
        ).start()

    def await_bytes(sems, turn, place, like):
        pltpu.make_async_copy(like, like, sems.at[turn, place]).wait()

    def send_phase_class(dy, dz):
        place = CLASS[(dy, dz)]
        if dz == 0:
            side = SIDE[dy]
            send(phase_y.at[side], phase_y_got.at[side, pl.ds(0, 8)], 0, place, (0, dy, 0))
            for dx, line, target in ((1, 6, 8), (-1, 0, 10)):
                source = phase_y.at[side, pl.ds(line, 2)]
                send(source, phase_y_got.at[side, pl.ds(target, 2)], 0, place, (dx, dy, 0))
        elif dy == 0:
            side = SIDE[dz]
            for dx in (0, 1, -1):
                send(phase_z.at[side], phase_z_got.at[side, TURN[dx]], 0, place, (dx, 0, dz))
        else:
            sides = SIDE[dy], SIDE[dz]
            send(phase_yz.at[sides], phase_yz_got.at[sides], 0, place, (0, dy, dz))

    def phase_like(dy, dz):
        if dz == 0:
            return phase_y_got.at[SIDE[dy]]
        if dy == 0:
            return phase_z_got.at[SIDE[dz]]
        return phase_yz_got.at[SIDE[dy], SIDE[dz]]

    def phase_plane(plane):
        return scalars.at[pl.ds(0, 2), plane, pl.ds(LO, NY)]

    def post_plane(step, dx, plane):
        return posts.at[step, pl.ds(0 if dx == 1 else 7, 7), plane, pl.ds(LO, NY)]

    def xy_place(dx, fused):
        return ROWS_Y + ROWS_XY * SIDE[dx] if fused else SUM_Y + SIDE[dx]

    def send_post_class(step, fused, dy, dz):
        turn, place = step + 1, CLASS[(dy, dz)]
        if dz == 0:
            side = SIDE[dy]
            rows, rows_xy = pl.ds(0, ROWS_Y if fused else SUM_Y), ROWS_XY if fused else 1
            send(post_y.at[step, side, rows], post_y_got.at[step, side, rows], turn, place, (0, dy, 0))
            for dx in (1, -1):
                source = post_xy.at[step, SIDE[dx], side, pl.ds(0, rows_xy)]
                target = post_y_got.at[step, side, pl.ds(xy_place(dx, fused), rows_xy)]
                send(source, target, turn, place, (dx, dy, 0))
        elif dy == 0:
            side = SIDE[dz]
            for dx in (0, 1, -1):
                send(post_z.at[step, side], post_z_got.at[step, side, TURN[dx]], turn, place, (dx, 0, dz))
        else:
            sides = SIDE[dy], SIDE[dz]
            target = post_row_got.at[step, sides[0], sides[1], pl.ds(0, 1)]
            send(post_row.at[step, sides[0], sides[1]], target, turn, place, (0, dy, dz))

    def send_corner_class(step, dy, dz):
        sides = SIDE[dy], SIDE[dz]
        for dx in (1, -1):
            target = post_row_got.at[step, sides[0], sides[1], pl.ds(TURN[dx], 1)]
            send(post_row.at[step, sides[0], sides[1]], target, step + 1, CORNER_CLASS[(dy, dz)], (dx, dy, dz))

    def post_like(step, fused, dy, dz):
        if dz == 0:
            return post_y_got.at[step, SIDE[dy], pl.ds(0, ROWS_Y_ALL if fused else SUM_Y + 2)]
        if dy == 0:
            return post_z_got.at[step, SIDE[dz]]
        return post_row_got.at[step, SIDE[dy], SIDE[dz], pl.ds(0, 1)]

    def corner_like(step, dy, dz):
        return post_row_got.at[step, SIDE[dy], SIDE[dz], pl.ds(1, 2)]

    def await_posts(sems, step, fused, classes, backward):
        by_class(
            lambda dy, dz: await_bytes(sems, step + 1, CLASS[(dy, dz)], post_like(step, fused, dy, dz)),
            backward,
            classes,
        )

    def await_corners(sems, step, backward):
        by_class(
            lambda dy, dz: await_bytes(sems, step + 1, CORNER_CLASS[(dy, dz)], corner_like(step, dy, dz)),
            backward,
            ON_YZ,
        )

    def await_x(sems, step):
        for dx in (1, -1):
            await_bytes(sems, step + 1, X_CLASS[dx], post_plane(step, dx, 0 if dx == 1 else NX + 1))

    def await_parts(sems, step):
        for dx in (1, -1):
            await_bytes(sems, step + 1, PART_CLASS[dx], post_part_got.at[step, SIDE[dx]])

    def pack_z(tile, place, sign, packed):
        moved = pltpu.roll(tile, place + 1 if sign == 1 else place, axis=1)
        return jnp.where(lane == place, moved, packed)

    def unpack_z(packed, place, sign):
        return pltpu.roll(packed, (128 - place) % 128 if sign == 1 else 127 - place, axis=1)

    def edge_lane(sign):
        return 0 if sign == 1 else NZ - 1

    def set_phase(x, values, packed):
        up, down = packed
        for entry, value in enumerate(values):
            scalars[entry, x + 1, LO:HI, :] = value
            for dy, edge in ((1, HI - 1), (-1, LO)):
                phase_y[SIDE[dy], x * 2 + entry] = scalars[entry, x + 1, edge : edge + 1, :]
            for half in range(2):
                tile = value[8 * half : 8 * half + 8]
                place = entry * 8 + 2 * x + half
                up = pack_z(tile, place, 1, up)
                down = pack_z(tile, place, -1, down)
        return up, down

    def send_phase(packed):
        for dz in (1, -1):
            phase_z[SIDE[dz]] = packed[SIDE[dz]]
            for dy, edge in ((1, 7), (-1, 0)):
                phase_yz[SIDE[dy], SIDE[dz]] = phase_z[SIDE[dz], edge : edge + 1, :]
        by_class(send_phase_class)
        for dx, near, far in ((1, NX, 0), (-1, 1, NX + 1)):
            send(phase_plane(near), phase_plane(far), 0, X_CLASS[dx], (dx, 0, 0))

    def unpack_phase():
        first, count = 0, 2
        fills = (0.0, WETTING)
        shifted = {1: scalars_down, -1: scalars_up}

        def place_of(entry):
            return entry

        def cover(offset, value, fill):
            for axis in (1, 2):
                if offset[axis] != 0:
                    value = jnp.where(closed[(axis, -offset[axis])], fill, value)
            return value

        def arrive(sems, backward):
            by_class(lambda dy, dz: await_bytes(sems, 0, CLASS[(dy, dz)], phase_like(dy, dz)), backward)
            for dx in (1, -1):
                await_bytes(sems, 0, X_CLASS[dx], phase_plane(0))

        def shift_plane(entry, plane, dz, face, column):
            for half in range(2):
                rows = slice(LO + 8 * half, LO + 8 * half + 8)
                value = scalars[first + entry, plane, rows, :]
                place = entry * 8 + 2 * column + half
                ghost = cover((0, 0, dz), unpack_z(face, place, dz), fills[entry])
                shifted[dz][place_of(entry), plane, rows, :] = jnp.where(
                    lane == edge_lane(dz), ghost, pltpu.roll(value, 1 if dz == 1 else 127, axis=1)
                )

        arrive(send_sem, False)
        arrive(recv_sem, True)
        for dz in (1, -1):
            face = phase_z_got[SIDE[dz], 0]
            for entry in range(count):
                for x in range(NX):
                    shift_plane(entry, x + 1, dz, face, x)
        for dy, ghost in ((1, LO - 1), (-1, HI)):
            half = 1 if dy == 1 else 0
            for entry in range(count):
                for x in range(NX):
                    line = cover((0, dy, 0), phase_y_got[SIDE[dy], x * count + entry], fills[entry])
                    scalars[first + entry, x + 1, ghost : ghost + 1, :] = line
                    for dz in (1, -1):
                        corner = phase_yz_got[SIDE[dy], SIDE[dz]]
                        place = entry * 8 + 2 * x + half
                        corner = cover((0, dy, dz), unpack_z(corner, place, dz), fills[entry])
                        shifted[dz][place_of(entry), x + 1, ghost : ghost + 1, :] = jnp.where(
                            row_lane == edge_lane(dz), corner, pltpu.roll(line, 1 if dz == 1 else 127, axis=1)
                        )
        for dx, plane, column in ((1, 0, NX - 1), (-1, NX + 1, 0)):
            for dy, ghost in ((1, LO - 1), (-1, HI)):
                for entry in range(count):
                    line = phase_y_got[SIDE[dy], 8 + 2 * SIDE[dx] + entry]
                    scalars[first + entry, plane, ghost : ghost + 1, :] = cover((0, dy, 0), line, fills[entry])
            for dz in (1, -1):
                for entry in range(count):
                    shift_plane(entry, plane, dz, phase_z_got[SIDE[dz], TURN[dx]], column)

    def relax_body(step, x, initial):
        total = state[0, x]
        flux = [0.0, 0.0, 0.0]
        for up, down in PAIRS:
            first, second = state[up, x], state[down, x]
            total = total + (first + second)
            difference = first - second
            for axis in range(3):
                if VELOCITY[up][axis] == 1:
                    flux[axis] = flux[axis] + difference
                elif VELOCITY[up][axis] == -1:
                    flux[axis] = flux[axis] - difference
        inverse = 1.0 / total
        velocity = [part * inverse for part in flux]
        phase = scalars[step + 1, x + 1, LO:HI, :]
        tau = 1.3 - 0.3 * phase
        rate = 1.0 / tau
        keep = 1.0 - rate
        for axis in range(3):
            speed[axis, x] = velocity[axis]
        if initial:
            red = total * (0.05 + 0.9 * labels[x].astype(jnp.float32))
            blue = total - red
            colour[0, x] = red
            colour[1, x] = blue
        shifted = [velocity[0] + tau * inverse * 0.001, velocity[1], velocity[2]]
        square = shifted[0] * shifted[0] + shifted[1] * shifted[1] + shifted[2] * shifted[2]
        scale = rate * total
        base = scale * (1.0 - 1.5 * square)
        state[0, x] = keep * state[0, x] + base * (1.0 / 3.0)
        face, edge = base * (1.0 / 18.0), base * (1.0 / 36.0)
        for up, down in PAIRS:
            along = 0.0
            for axis in range(3):
                if VELOCITY[up][axis] == 1:
                    along = along + shifted[axis]
                elif VELOCITY[up][axis] == -1:
                    along = along - shifted[axis]
            push = scale * along
            if up < 7:
                even, odd = face + 0.25 * (push * along), push * (1.0 / 6.0)
            else:
                even, odd = edge + 0.125 * (push * along), push * (1.0 / 12.0)
            state[up, x] = keep * state[up, x] + (even + odd)
            state[down, x] = keep * state[down, x] + (even - odd)

    def gradient_at(step, x):
        def at(buffer, place, plane, dy):
            return buffer[place, plane, LO + dy : HI + dy, :]

        here_ = step + 1

        def spread(plane):
            return (
                2.0 * at(scalars, here_, plane, 0)
                + (at(scalars, here_, plane, 1) + at(scalars, here_, plane, -1))
                + (at(scalars_up, 1, plane, 0) + at(scalars_down, 1, plane, 0))
            )

        def slope_y(plane):
            return at(scalars, here_, plane, 1) - at(scalars, here_, plane, -1)

        def slope_z(plane):
            return at(scalars_up, 1, plane, 0) - at(scalars_down, 1, plane, 0)

        low, mid, high = x, x + 1, x + 2
        up_up, up_down = at(scalars_up, 1, mid, 1), at(scalars_up, 1, mid, -1)
        down_up, down_down = at(scalars_down, 1, mid, 1), at(scalars_down, 1, mid, -1)
        along_x = spread(high) - spread(low)
        along_y = 2.0 * slope_y(mid) + (slope_y(high) + slope_y(low)) + ((up_up - up_down) + (down_up - down_down))
        along_z = 2.0 * slope_z(mid) + (slope_z(high) + slope_z(low)) + ((up_up - down_up) + (up_down - down_down))
        return [part * (1.0 / 12.0) for part in (along_x, along_y, along_z)]

    def put_post(step, x, name, value, packed, fluid=None):
        kind, number = name
        offset = VELOCITY[number]
        value = jnp.where(fluid, value, 0.0)
        if offset[1] != 0:
            sign = offset[1]
            edge = HI - 1 if sign == 1 else LO
        up, down = packed
        if offset[2] != 0:
            unrolled[UNROLLED[name], x] = value
            sign_z = offset[2]
            first = Z_FACE[sign_z].index(name) * 8
            for half in range(2):
                tile = value[8 * half : 8 * half + 8]
                place = first + 2 * x + half
                if sign_z == 1:
                    up = pack_z(tile, place, 1, up)
                else:
                    down = pack_z(tile, place, -1, down)
            value = pltpu.roll(value, 1 if sign_z == 1 else 127, axis=1)
            if name not in ACROSS_YZ:
                value = jnp.where(wide_lane == edge_lane(sign_z), 0.0, value)
        posts[step, SLOT[name], x + 1, LO:HI, :] = value
        if offset[1] != 0:
            line = Y_FACE[sign].index(name) * 4 + x
            post_y[step, SIDE[sign], line] = posts[step, SLOT[name], x + 1, edge : edge + 1, :]
        return up, down

    def collide_body(step, x, packed):
        gradient = gradient_at(step, x)
        squares = [part * part for part in gradient]
        total = squares[0] + squares[1] + squares[2]
        fluid = scalars[0, x + 1, LO:HI, :] > 0.0
        packed = put_post(step, x, ("f", 0), state[0, x], packed, fluid)
        third = total * (1.0 / 3.0)
        for up, down in PAIRS:
            if up < 7:
                surface = (TENSION / 18.0) * (squares[(up - 1) // 2] - third)
            else:
                slope = 0.0
                for axis in range(3):
                    if VELOCITY[up][axis] == 1:
                        slope = slope + gradient[axis]
                    elif VELOCITY[up][axis] == -1:
                        slope = slope - gradient[axis]
                surface = (TENSION / 36.0) * (slope * slope - 2.0 * third)
            packed = put_post(step, x, ("f", up), state[up, x] + surface, packed, fluid)
            packed = put_post(step, x, ("f", down), state[down, x] + surface, packed, fluid)
        red, blue = colour[0, x], colour[1, x]
        mixing = (0.5 * 0.125) * (red * blue / (red + blue)) * lax.rsqrt(jnp.maximum(total, 0.01))
        packed = put_post(step, x, ("r", 0), 0.25 * red, packed, fluid)
        packed = put_post(step, x, ("b", 0), 0.25 * blue, packed, fluid)
        for axis in range(3):
            drift = 0.5 * speed[axis, x]
            across = mixing * gradient[axis]
            for kind, amount, turn in (("r", red, 1.0), ("b", blue, -1.0)):
                mean = 0.125 * amount
                lean = amount * drift + turn * across
                packed = put_post(step, x, (kind, 2 * axis + 1), mean + lean, packed, fluid)
                packed = put_post(step, x, (kind, 2 * axis + 2), mean - lean, packed, fluid)
        return packed

    def state_at(name):
        return {"f": 0, "r": 19, "b": 26}[name[0]] + name[1]

    def opened_at(x, offset):
        dx, dy, dz = offset
        return shifted_scalars[dz][0, x + 1 - dx, LO - dy : HI - dy, :] > 0.0

    def bounced_at(step, x, name):
        back = (name[0], OPPOSITE[name[1]])
        if VELOCITY[name[1]][2] != 0:
            return unrolled[UNROLLED[back], x]
        return posts[step, SLOT[back], x + 1, LO:HI, :]

    def stream_inside(step, x, end, last):
        fluid = scalars[0, x + 1, LO:HI, :] > 0.0
        names = [name for name in EVERY if (last or name[0] == "f") and name not in ACROSS_YZ]
        for name in names:
            dx, dy, dz = VELOCITY[name[1]]
            if name[1] == 0:
                value = posts[step, SLOT[name], x + 1, LO:HI, :]
            else:
                if dx != 0 and dx == end:
                    arriving = 0.0
                else:
                    arriving = posts[step, SLOT[name], x + 1 - dx, LO - dy : HI - dy, :]
                value = jnp.where(opened_at(x, (dx, dy, dz)), arriving, bounced_at(step, x, name))
            state[state_at(name), x] = jnp.where(fluid, value, 0.0) if last else value

    def stream_across(step, x, last):
        fluid = scalars[0, x + 1, LO:HI, :] > 0.0
        for name in ACROSS_YZ:
            dx, dy, dz = VELOCITY[name[1]]
            arriving = posts[step, SLOT[name], x + 1, LO - dy : HI - dy, :]
            value = jnp.where(opened_at(x, (dx, dy, dz)), arriving, bounced_at(step, x, name))
            state[state_at(name), x] = jnp.where(fluid, value, 0.0) if last else value

    def arrivals(step, last):
        def wanted(name):
            return last or name[0] == "f"

        def kept(x, rows, value):
            if not last:
                return value
            return jnp.where(scalars[0, x + 1, LO + rows.start : LO + rows.stop, :] > 0.0, value, 0.0)

        def z_columns(name, dx, column, half):
            dz = VELOCITY[name[1]][2]
            place = Z_FACE[dz].index(name) * 8 + 2 * column + half
            face = post_z_got[step, SIDE[dz], TURN[dx]]
            return jnp.where(lane == edge_lane(dz), unpack_z(face, place, dz), 0.0)

        def add_z():
            for dz in (1, -1):
                for name in Z_FACE[dz]:
                    if name in ACROSS_YZ or not wanted(name):
                        continue
                    for x in range(NX):
                        source = x - VELOCITY[name[1]][0]
                        if not 0 <= source < NX:
                            continue
                        for half in range(2):
                            rows = slice(8 * half, 8 * half + 8)
                            value = kept(x, rows, z_columns(name, 0, source, half))
                            state[state_at(name), x, rows, :] = state[state_at(name), x, rows, :] + value
            for name in ACROSS_YZ:
                dz = VELOCITY[name[1]][2]
                face = post_z_got[step, SIDE[dz], 0]
                for x in range(NX):
                    for half in range(2):
                        rows = slice(LO + 8 * half, LO + 8 * half + 8)
                        place = Z_FACE[dz].index(name) * 8 + 2 * x + half
                        posts[step, SLOT[name], x + 1, rows, :] = jnp.where(
                            lane == edge_lane(dz), unpack_z(face, place, dz), posts[step, SLOT[name], x + 1, rows, :]
                        )

        def add_x():
            for dx, end, ghost, column, names in ((1, 0, 0, NX - 1, X_UP), (-1, NX - 1, NX + 1, 0, X_DOWN)):
                for name in names:
                    if not wanted(name):
                        continue
                    _, dy, dz = VELOCITY[name[1]]
                    if dy != 0:
                        row_ghost = LO - 1 if dy == 1 else HI
                        line = post_y_got[step, SIDE[dy], xy_place(dx, not last)]
                        posts[step, SLOT[name], ghost, row_ghost : row_ghost + 1, :] = line
                    for half in range(2):
                        rows = slice(8 * half, 8 * half + 8)
                        first = LO + 8 * half - dy
                        value = posts[step, SLOT[name], ghost, first : first + 8, :]
                        if dz != 0:
                            value = value + z_columns(name, dx, column, half)
                        state[state_at(name), end, rows, :] = state[state_at(name), end, rows, :] + kept(end, rows, value)
        def add_y():
            for dy, edge in ((1, 0), (-1, NY - 1)):
                rows = slice(edge, edge + 1)
                for entry, name in enumerate(Y_FACE[dy]):
                    if name in ACROSS_YZ or not wanted(name):
                        continue
                    for x in range(NX):
                        source = x - VELOCITY[name[1]][0]
                        if not 0 <= source < NX:
                            continue
                        value = kept(x, rows, post_y_got[step, SIDE[dy], entry * 4 + source])
                        state[state_at(name), x, rows, :] = state[state_at(name), x, rows, :] + value

        def add_across():
            for name in ACROSS_YZ:
                _, dy, dz = VELOCITY[name[1]]
                entry, entry_z = Y_FACE[dy].index(name), Z_FACE[dz].index(name)
                half = 1 if dy == 1 else 0
                ghost = LO - 1 if dy == 1 else HI
                for x in range(NX):
                    corner = unpack_z(post_row_got[step, SIDE[dy], SIDE[dz], 0], entry_z * 8 + 2 * x + half, dz)
                    line = jnp.where(row_lane == edge_lane(dz), corner, post_y_got[step, SIDE[dy], entry * 4 + x])
                    posts[step, SLOT[name], x + 1, ghost : ghost + 1, :] = line

        return add_x, add_y, add_z, add_across

    shifted_scalars = {0: scalars, 1: scalars_down, -1: scalars_up}

    def add_up(step, packed):
        up, down = packed
        for x in range(NX):
            for place, kind in enumerate(("r", "b")):
                total = posts[step, SLOT[(kind, 0)], x + 1, LO:HI, :]
                for number in range(1, 7):
                    dx, dy, dz = VELOCITY[number]
                    plane = x + 1 - dx
                    opened = shifted_scalars[dz][0, plane, LO - dy : HI - dy, :] > 0.0
                    back = (kind, OPPOSITE[number])
                    if dz != 0:
                        bounced = unrolled[UNROLLED[back], x]
                    else:
                        bounced = posts[step, SLOT[back], x + 1, LO:HI, :]
                    if 1 <= plane <= NX:
                        arriving = posts[step, SLOT[(kind, number)], plane, LO - dy : HI - dy, :]
                    else:
                        arriving = 0.0
                    total = total + jnp.where(opened, arriving, bounced)
                partial[place, x] = total
                for half in range(2):
                    tile = total[8 * half : 8 * half + 8]
                    lanes = SUM_Z + 8 * place + 2 * x + half
                    up, down = pack_z(tile, lanes, 1, up), pack_z(tile, lanes, -1, down)
                for dx, end in ((1, NX - 1), (-1, 0)):
                    if x == end:
                        post_part[step, SIDE[dx], NY * place : NY * place + NY, :] = total
                for dy, edge in ((1, NY - 1), (-1, 0)):
                    post_y[step, SIDE[dy], SUM_Y + 4 * place + x] = partial[place, x, edge : edge + 1, :]
                for dy, half in ((1, 1), (-1, 0)):
                    rows = slice(LO + 8 * half, LO + 8 * half + 8)
                    tile = posts[step, SLOT[(kind, FACE[(1, dy)])], x + 1, rows, :]
                    lanes = Y_Z + 8 * place + 2 * x + (0 if dy == 1 else 1)
                    up, down = pack_z(tile, lanes, 1, up), pack_z(tile, lanes, -1, down)
        for place, kind in enumerate(("r", "b")):
            for dx, end in ((1, NX - 1), (-1, 0)):
                slot = SLOT[(kind, FACE[(0, dx)])]
                for half in range(2):
                    tile = posts[step, slot, end + 1, LO + 8 * half : LO + 8 * half + 8, :]
                    lanes = X_Z + 8 * place + (0 if dx == 1 else 6) + half
                    up, down = pack_z(tile, lanes, 1, up), pack_z(tile, lanes, -1, down)
                for dy, edge in ((1, HI - 1), (-1, LO)):
                    line = posts[step, slot, end + 1, edge : edge + 1, :]
                    post_y[step, SIDE[dy], X_Y + 2 * SIDE[dx] + place] = line
                    post_xy[step, SIDE[dx], SIDE[dy], X_XY + place] = line
                    post_xy[step, SIDE[dx], SIDE[dy], SUM_XY + place] = partial[place, end, edge - LO : edge - LO + 1, :]
                    line = posts[step, SLOT[(kind, FACE[(1, dy)])], end + 1, edge : edge + 1, :]
                    post_xy[step, SIDE[dx], SIDE[dy], Y_XY + place] = line
                    part = Y_PART + 2 * SIDE[dy] + place
                    post_part[step, SIDE[dx], part : part + 1, :] = line
        return up, down

    def put_edges(step, packed, fused):
        for dx, end in ((1, NX - 1), (-1, 0)):
            for dy, edge in ((1, HI - 1), (-1, LO)):
                slot = SLOT[("f", VELOCITY.index((dx, dy, 0)))]
                post_xy[step, SIDE[dx], SIDE[dy], 0] = posts[step, slot, end + 1, edge : edge + 1, :]
            if fused:
                both = jnp.where(lane < 64, packed[0], pltpu.roll(packed[1], 64, axis=1))
                post_part[step, SIDE[dx], Z_PART : Z_PART + 8, :] = both
        for dz in (1, -1):
            post_z[step, SIDE[dz]] = packed[SIDE[dz]]
            for dy, edge in ((1, 7), (-1, 0)):
                line = post_z[step, SIDE[dz], edge : edge + 1, :]
                post_row[step, SIDE[dy], SIDE[dz], 0] = line
                if fused:
                    post_y[step, SIDE[dy], Z_Y + SIDE[dz]] = line

    def turned(value, lanes):
        return pltpu.roll(value, 128 - lanes, axis=1)

    def ratio(red, blue):
        return (red - blue) / (red + blue)

    def packed_ratio(sums):
        blue = turned(sums, 8)
        return ratio(sums, blue)

    def finish_phase(step, planes=(), corners=False):
        inside = len(planes) > 0
        here_ = step + 2

        def put(target, entry, plane, rows, value):
            fluid = shifted_scalars[target][0, plane, rows, :] > 0.0
            shifted_scalars[target][entry, plane, rows, :] = jnp.where(fluid, value, WETTING)

        interior = slice(LO, HI)
        z_got = {(dx, dz): post_z_got[step, SIDE[dz], TURN[dx]] for dx in (-1, 0, 1) for dz in (1, -1)}
        row_got = {
            (dx, dy, dz): post_row_got[step, SIDE[dy], SIDE[dz], TURN[dx]]
            for dx in (() if inside else (-1, 0, 1) if corners else (0,))
            for dy in (1, -1)
            for dz in (1, -1)
        }

        def xy_got(dx, dy, line):
            return post_y_got[step, SIDE[dy], ROWS_Y + ROWS_XY * SIDE[dx] + line]

        def with_columns(value, place, column, dx):
            halves = []
            for half in range(2):
                tile = value[8 * half : 8 * half + 8]
                for dz in (1, -1):
                    lanes = IN_Z + 8 * place + 2 * column + half
                    tile = tile + jnp.where(lane == edge_lane(dz), unpack_z(z_got[(dx, dz)], lanes, dz), 0.0)
                halves.append(tile)
            return jnp.concatenate(halves, axis=0)

        def with_rows(value, rows):
            for dy, edge in ((1, 0), (-1, NY - 1)):
                value = value + jnp.where(wide_row == edge, rows[dy], 0.0)
            return value

        def with_ends(line, offset, place, x):
            dx, dy = offset
            half = 1 if dy == 1 else 0
            for dz in (1, -1):
                lanes = IN_Z + 8 * place + 2 * x + half
                line = line + jnp.where(row_lane == edge_lane(dz), unpack_z(row_got[(dx, dy, dz)], lanes, dz), 0.0)
            return line

        for x in planes:
            sums = []
            for place, kind in enumerate(("r", "b")):
                total = partial[place, x]
                for dx, end, ghost in ((1, 0, 0), (-1, NX - 1, NX + 1)):
                    if x == end:
                        total = total + posts[step, SLOT[(kind, FACE[(0, dx)])], ghost, interior, :]
                rows = {}
                for dy in (1, -1):
                    entry = Y_FACE[dy].index((kind, FACE[(1, dy)]))
                    rows[dy] = post_y_got[step, SIDE[dy], entry * 4 + x]
                total = with_columns(with_rows(total, rows), place, x, 0)
                colour[place, x] = total
                sums.append(total)
            put(0, here_, x + 1, interior, ratio(*sums))
        if inside:
            return
        for dx, ghost, end, column in ((1, 0, 0, NX - 1), (-1, NX + 1, NX - 1, 0)):
            sums = []
            lines = {1: [], -1: []}
            for place, kind in enumerate(("r", "b")):
                if not corners:
                    total = post_part_got[step, SIDE[dx], NY * place : NY * place + NY, :]
                    total = total + posts[step, SLOT[(kind, FACE[(0, -dx)])], end + 1, interior, :]
                    rows = {dy: xy_got(dx, dy, Y_XY + place) for dy in (1, -1)}
                    sums.append(with_columns(with_rows(total, rows), place, column, dx))
                    continue
                for dy in (1, -1):
                    part = Y_PART + 2 * SIDE[-dy] + place
                    line = (
                        xy_got(dx, dy, SUM_XY + place)
                        + post_part_got[step, SIDE[dx], part : part + 1, :]
                        + post_y_got[step, SIDE[dy], X_Y + 2 * SIDE[-dx] + place]
                    )
                    lines[dy].append(with_ends(line, (dx, dy), place, column))
            if not corners:
                put(0, here_, ghost, interior, ratio(*sums))
                continue
            for dy, row_ghost in ((1, LO - 1), (-1, HI)):
                put(0, here_, ghost, slice(row_ghost, row_ghost + 1), ratio(*lines[dy]))
        for dy, row_ghost, edge in ((1, LO - 1, LO), (-1, HI, HI - 1)):
            for x in () if corners else range(NX):
                sums = []
                for place, kind in enumerate(("r", "b")):
                    line = post_y_got[step, SIDE[dy], SUM_Y + 4 * place + x]
                    line = line + posts[step, SLOT[(kind, FACE[(1, -dy)])], x + 1, edge : edge + 1, :]
                    for dx, end in ((1, 0), (-1, NX - 1)):
                        if x == end:
                            line = line + xy_got(dx, dy, X_XY + place)
                    sums.append(with_ends(line, (0, dy), place, x))
                put(0, here_, x + 1, slice(row_ghost, row_ghost + 1), ratio(*sums))
        low_x, high_x = lane % 8 < 2, lane % 8 >= 6
        first_y, last_y = (row == 0) & (lane % 2 == 0), (row == 7) & (lane % 2 == 1)
        row_low_x, row_high_x = row_lane % 8 < 2, row_lane % 8 >= 6
        for dz in (1, -1):

            def with_y(sums, dx):
                sums = sums + jnp.where(first_y, turned(row_got[(dx, 1, dz)], Y_Z), 0.0)
                return sums + jnp.where(last_y, turned(row_got[(dx, -1, dz)], Y_Z), 0.0)

            faces = {}
            if not corners:
                sums = turned(z_got[(0, dz)], SUM_Z) + turned(post_z[step, SIDE[-dz]], IN_Z)
                sums = sums + jnp.where(low_x, turned(z_got[(1, dz)], X_Z), 0.0)
                sums = sums + jnp.where(high_x, turned(z_got[(-1, dz)], X_Z), 0.0)
                faces[0] = packed_ratio(with_y(sums, 0))
            for dx in (1, -1) if corners else ():
                sums = turned(z_got[(dx, dz)], SUM_Z) + turned(z_got[(0, dz)], X_Z)
                sums = sums + turned(post_part_got[step, SIDE[dx], Z_PART : Z_PART + 8, :], IN_Z + 64 * SIDE[-dz])
                faces[dx] = packed_ratio(with_y(sums, dx))
            for plane in (0, NX + 1) if corners else range(1, NX + 1):
                dx, column = {0: (1, NX - 1), NX + 1: (-1, 0)}.get(plane, (0, plane - 1))
                for half in range(2):
                    rows = slice(LO + 8 * half, LO + 8 * half + 8)
                    value = scalars[here_, plane, rows, :]
                    ghost = unpack_z(faces[dx], 2 * column + half, dz)
                    value = jnp.where(lane == edge_lane(dz), ghost, pltpu.roll(value, 1 if dz == 1 else 127, axis=1))
                    put(dz, 1, plane, rows, value)
            for dy, row_ghost in ((1, LO - 1), (-1, HI)):
                half = 1 if dy == 1 else 0
                edge = 0 if dy == 1 else 7
                sums = turned(row_got[(0, dy, dz)], SUM_Z)
                sums = sums + turned(post_y_got[step, SIDE[dy], Z_Y + SIDE[-dz]], IN_Z)
                sums = sums + turned(post_z_got[step, SIDE[dz], 0, edge : edge + 1, :], Y_Z)
                if corners:
                    sums = sums + jnp.where(row_low_x, turned(row_got[(1, dy, dz)], X_Z), 0.0)
                    sums = sums + jnp.where(row_high_x, turned(row_got[(-1, dy, dz)], X_Z), 0.0)
                corner = packed_ratio(sums)
                for x in (0, NX - 1) if corners else range(1, NX - 1):
                    line = scalars[here_, x + 1, row_ghost : row_ghost + 1, :]
                    line = pltpu.roll(line, 1 if dz == 1 else 127, axis=1)
                    line = jnp.where(row_lane == edge_lane(dz), unpack_z(corner, 2 * x + half, dz), line)
                    put(dz, 1, x + 1, slice(row_ghost, row_ghost + 1), line)

    blank = jnp.zeros((8, NZ), jnp.float32)

    def first_phase(x, packed):
        fluid = 1.0 - solid[x].astype(jnp.float32)
        phase = jnp.where(fluid > 0.0, -0.9 + 1.8 * labels[x].astype(jnp.float32), WETTING)
        return set_phase(x, [fluid, phase], packed)

    barrier = pltpu.get_barrier_semaphore()

    def greet(dy, dz):
        for dx in (0, 1, -1) if 0 in (dy, dz) else (0,):
            pl.semaphore_signal(barrier, inc=1, device_id=neighbour((dx, dy, dz)), device_id_type=MESH)

    by_class(greet)
    for dx in (1, -1):
        pl.semaphore_signal(barrier, inc=1, device_id=neighbour((dx, 0, 0)), device_id_type=MESH)
    beside_y = 2 - closed[(1, 1)].astype(jnp.int32) - closed[(1, -1)].astype(jnp.int32)
    beside_z = 2 - closed[(2, 1)].astype(jnp.int32) - closed[(2, -1)].astype(jnp.int32)
    beside = 2 + 3 * (beside_y + beside_z) + beside_y * beside_z

    def clear(dy, dz):
        for step in range(STEPS):
            if dz == 0:
                post_y_got[step, SIDE[dy]] = jnp.zeros((ROWS_Y_ALL, 1, NZ), jnp.float32)
            elif dy == 0:
                post_z_got[step, SIDE[dz]] = jnp.zeros((3, 8, NZ), jnp.float32)
            else:
                post_row_got[step, SIDE[dy], SIDE[dz]] = jnp.zeros((3, 1, NZ), jnp.float32)

    for dy, dz in CLASSES:
        pl.when(jnp.logical_not(has((0, -dy, -dz))))(functools.partial(clear, dy, dz))

    for step in range(STEPS):
        for side in range(2):
            post_part[step, side, Y_PART : Y_PART + 8, :] = blank
        for name in Y_FACE[1] + Y_FACE[-1]:
            if name not in ACROSS_YZ:
                ghost = LO - 1 if VELOCITY[name[1]][1] == 1 else HI
                for plane in range(1, NX + 1):
                    posts[step, SLOT[name], plane, ghost : ghost + 1, :] = blank[0:1]

    loads[0].wait()
    loads[1].wait()
    packed = lax.fori_loop(0, NX, first_phase, (blank, blank), unroll=False)
    pl.semaphore_wait(barrier, beside)
    send_phase(packed)
    loads[2].wait()
    lax.fori_loop(0, NX, lambda x, _: relax_body(0, x, True), None, unroll=False)
    unpack_phase()

    def collide_middle(step):
        return lax.fori_loop(1, NX - 1, lambda x, p: collide_body(step, x, p), (blank, blank), unroll=True)

    def move(step, packed, fused):
        packed = lax.fori_loop(0, 2, lambda turn, p: collide_body(step, 3 - 3 * turn, p), packed, unroll=True)
        if fused:
            packed = add_up(step, packed)
        put_edges(step, packed, fused)
        by_class(functools.partial(send_post_class, step, fused), classes=ON_Y + ON_YZ)
        if fused:
            by_class(functools.partial(send_corner_class, step), classes=ON_YZ)
        for dx, near, far in ((1, NX, 0), (-1, 1, NX + 1)):
            send(post_plane(step, dx, near), post_plane(step, dx, far), step + 1, X_CLASS[dx], (dx, 0, 0))
        by_class(functools.partial(send_post_class, step, fused), classes=ON_Z)
        if fused:
            for dx in (1, -1):
                side = SIDE[dx]
                send(post_part.at[step, side], post_part_got.at[step, side], step + 1, PART_CLASS[dx], (dx, 0, 0))
        last = not fused
        stream_inside(step, 0, 1, last)
        lax.fori_loop(1, NX - 1, lambda x, _: stream_inside(step, x, 0, last), None, unroll=False)
        stream_inside(step, NX - 1, -1, last)
        await_posts(send_sem, step, fused, CLASSES, False)
        await_x(send_sem, step)
        if fused:
            await_parts(send_sem, step)
            await_corners(send_sem, step, False)
        add_x, add_y, add_z, add_across = arrivals(step, last)
        await_posts(recv_sem, step, fused, ON_Z, True)
        add_z()
        await_posts(recv_sem, step, fused, ON_Y, True)
        add_y()
        if fused:
            finish_phase(step, (1, 2))
        await_posts(recv_sem, step, fused, ON_YZ, True)
        add_across()
        lax.fori_loop(0, NX, lambda x, _: stream_across(step, x, last), None, unroll=False)
        if fused:
            lax.fori_loop(1, 3, lambda x, _: relax_body(step + 1, x, False), None, unroll=False)
        await_x(recv_sem, step)
        add_x()
        if fused:
            finish_phase(step, (0, 3))
            lax.fori_loop(0, 2, lambda turn, _: relax_body(step + 1, 3 - 3 * turn, False), None, unroll=False)
            await_parts(recv_sem, step)
            finish_phase(step)
            packed = collide_middle(step + 1)
            await_corners(recv_sem, step, True)
            finish_phase(step, corners=True)
        return packed

    packed = lax.fori_loop(0, STEPS - 1, lambda step, p: move(step, p, True), collide_middle(0))
    move(STEPS - 1, packed, False)


def hand_out(every, momentum_out, red_out, blue_out, sem):
    copies = []
    first = 0
    for place, target in enumerate((momentum_out, red_out, blue_out)):
        count = target.shape[0]
        copies.append(pltpu.make_async_copy(every.at[pl.ds(first, count)], target, sem.at[place]))
        first += count
    for copy in copies:
        copy.start()
    for copy in copies:
        copy.wait()


def shards(sizes, momentum_sets, labels, solid_mask):
    block = (NX, NY, NZ)
    f32 = jnp.float32
    vmem = lambda *shape, dtype=f32: pltpu.VMEM(shape, dtype)
    every = pl.pallas_call(
        functools.partial(kernel, sizes=sizes),
        out_shape=vmem(33, *block),
        in_specs=[pl.BlockSpec(memory_space=pltpu.HBM)] * 3,
        out_specs=pl.BlockSpec(memory_space=pltpu.VMEM),
        scratch_shapes=[
            vmem(*block, dtype=jnp.int32),
            vmem(*block, dtype=jnp.int32),
            vmem(1 + STEPS, NX + 2, ROWS, NZ),
            vmem(2, NX + 2, ROWS, NZ),
            vmem(2, NX + 2, ROWS, NZ),
            vmem(STEPS, 33, NX + 2, ROWS, NZ),
            vmem(14, *block),
            vmem(3, *block),
            vmem(2, *block),
            vmem(2, 8, 1, NZ),
            vmem(2, 8, NZ),
            vmem(2, 2, 1, NZ),
            vmem(2, 12, 1, NZ),
            vmem(2, 3, 8, NZ),
            vmem(2, 2, 1, NZ),
            vmem(STEPS, 2, ROWS_Y, 1, NZ),
            vmem(STEPS, 2, 8, NZ),
            vmem(STEPS, 2, 2, 1, 1, NZ),
            vmem(STEPS, 2, 2, ROWS_XY, 1, NZ),
            vmem(STEPS, 2, ROWS_PART, NZ),
            vmem(STEPS, 2, ROWS_Y_ALL, 1, NZ),
            vmem(STEPS, 2, 3, 8, NZ),
            vmem(STEPS, 2, 2, 3, 1, NZ),
            vmem(STEPS, 2, ROWS_PART, NZ),
            vmem(2, *block),
            pltpu.SemaphoreType.DMA((3,)),
            pltpu.SemaphoreType.DMA((1 + STEPS, 16)),
            pltpu.SemaphoreType.DMA((1 + STEPS, 16)),
        ],
        compiler_params=pltpu.CompilerParams(
            collective_id=0, has_side_effects=True, vmem_limit_bytes=VMEM_LIMIT
        ),
        cost_estimate=pl.CostEstimate(flops=15_000_000, bytes_accessed=1_800_000, transcendentals=0),
    )(*(pltpu.with_memory_space_constraint(array, pltpu.HBM) for array in (momentum_sets, labels, solid_mask)))
    return pl.pallas_call(
        hand_out,
        out_shape=[jax.ShapeDtypeStruct((count,) + block, f32) for count in (19, 7, 7)],
        in_specs=[pl.BlockSpec(memory_space=pltpu.VMEM)],
        out_specs=[pl.BlockSpec(memory_space=pltpu.HBM)] * 3,
        scratch_shapes=[pltpu.SemaphoreType.DMA((3,))],
        cost_estimate=pl.CostEstimate(flops=0, bytes_accessed=2_200_000, transcendentals=0),
    )(pltpu.with_memory_space_constraint(every, pltpu.VMEM))


def solution(mesh):
    sizes = tuple(mesh.shape[axis] for axis in ("flow", "gy", "gz"))
    split = P("flow", "gy", "gz")
    split_sets = P(None, "flow", "gy", "gz")
    return jax.shard_map(
        functools.partial(shards, sizes),
        mesh=mesh,
        in_specs=(split_sets, split, split),
        out_specs=(split_sets, split_sets, split_sets),
        check_vma=False,
    )
```
